32 devices in a mesh: page: 8 (over y, x, core), row: 4 (over z).
Axes of the slice: x: 2, y: 2, z: 4, core: 2. Of those that a mesh axis runs over, the one named last changes fastest.
Arguments:
- vis_stream: bfloat16 [8, 48, 24, 768], P('page', 'row'), may hold values from -6 to 6
- query_stream: bfloat16 [8, 640, 768], P('page', 'row'), may hold values from -6 to 6
- w_qkv: bfloat16 [4, 768, 2304], replicated, may hold values from -0.21875 to 0.21875
- w_out: bfloat16 [4, 768, 768], replicated, may hold values from -2.5 to 2.5
- b_out: float32 [4, 768], replicated, may hold values from -3 to 3
- w_up: bfloat16 [2, 768, 3072], replicated, may hold values from -0.21875 to 0.21875
- b_up: float32 [2, 3072], replicated, may hold values from -3 to 3
- w_down: bfloat16 [2, 3072, 768], replicated, may hold values from -0.109375 to 0.109375
- b_down: float32 [2, 768], replicated, may hold values from -3 to 3
- norm_gain: float32 [7, 768], replicated, may hold values from 0.5 to 1.5
- norm_bias: float32 [7, 768], replicated, may hold values from -3 to 3
- page_cols: int32 [8], P('page'), may hold values from 12 to 24, as said below
- query_len: int32 [8], P('page'), may hold values from 481 to 640, as said below
- prompt_len: int32 [8], P('page'), may hold values from 1 to 319
- region_ids: int32 [8, 48, 24], P('page', 'row'), may hold values from 0 to 2
- vis_cotangent: bfloat16 [8, 48, 24, 768], P('page', 'row'), may hold values from -6 to 6
- query_cotangent: bfloat16 [8, 640, 768], P('page', 'row'), may hold values from -6 to 6
Outputs:
- vis_out: bfloat16 [8, 48, 24, 768], P('page', 'row')
- query_out: bfloat16 [8, 640, 768], P('page', 'row')
- vis_grad: float32 [8, 48, 24, 768], P('page', 'row')
- query_grad: float32 [8, 640, 768], P('page', 'row')
- grad_qkv: float32 [4, 768, 2304], P(None, 'page', 'row')
- grad_wout: float32 [4, 768, 768], P(None, 'page', 'row')
- grad_bout: float32 [4, 768], P(None, 'page')
- grad_wup: float32 [2, 768, 3072], P(None, 'page', 'row')
- grad_bup: float32 [2, 3072], P(None, 'page')
- grad_wdown: float32 [2, 3072, 768], P(None, 'page', 'row')
- grad_bdown: float32 [2, 768], P(None, 'page')
- grad_gain: float32 [7, 768], P(None, 'page')
- grad_bias: float32 [7, 768], P(None, 'page')
The draws below stay inside these ranges and needn't reach their ends.
Inputs may be any that keep to these rules, and one draw needn't show every extreme that they name: `page_cols`: some page has all 24 columns live. `query_len`: every page's query sequence reaches its last band of 160 slots; some page fills all 640 slots.
All inputs are finite; a program needn't handle non-finite values.
Results may differ from the reference program's by a relative error of at most 0.014.
Values may be sent and summed in bfloat16 or wider, within the bound.
A program may use at most 384 MiB of HBM per device.

```python
import jax
import jax.numpy as jnp
from jax import lax

D = 768
HDIM = 64
FF = 3072
WIN = 12
WCOL = 2
Q_DEV = 160
SHIFT = 6
PR = 48
PC = 24
QLEN = 640
PAGES = 8


def draw_page_cols(key, part):
    key = jax.random.fold_in(key, 11)
    key_draw, key_pick = jax.random.split(key)
    widths = jax.random.randint(key_draw, (PAGES,), WIN, WIN * WCOL + 1)
    chosen = jax.random.randint(key_pick, (), 0, PAGES)
    return jnp.where(jnp.arange(PAGES) == chosen, WIN * WCOL, widths).astype(jnp.int32)


def draw_query_len(key, part):
    key = jax.random.fold_in(key, 12)
    key_draw, key_pick = jax.random.split(key)
    lengths = jax.random.randint(key_draw, (PAGES,), QLEN - Q_DEV + 1, QLEN + 1)
    chosen = jax.random.randint(key_pick, (), 0, PAGES)
    return jnp.where(jnp.arange(PAGES) == chosen, QLEN, lengths).astype(jnp.int32)


def with_ends(result, own_key, low, largest):
    index_at = [jax.random.randint(jax.random.fold_in(own_key, axis), (), 0, length) for axis, length in enumerate(result.shape)]
    longest = result.shape.index(max(result.shape))
    neighbour = index_at[:longest] + [(index_at[longest] + 1) % result.shape[longest]] + index_at[longest + 1:]
    return result.at[tuple(index_at)].set(low).at[tuple(neighbour)].set(largest)


def levels(own_key, shape, cuts, low, top_value):
    factor_of, own = 1.0, jax.random.fold_in(own_key, 6)
    for dim, parts in cuts:
        heights = jnp.exp(jax.random.uniform(jax.random.fold_in(own, dim), (parts,), jnp.float32, low / len(cuts), top_value / len(cuts)))
        factor_of = factor_of * jnp.repeat(heights, shape[dim] // parts).reshape([-1 if axis == dim else 1 for axis in range(len(shape))])
    return factor_of


def normal_values(stream_key, extent, scale, reach, cuts=(), held_as=jnp.bfloat16):
    entries = scale * jax.random.normal(stream_key, extent, jnp.float32)
    if cuts:
        entries = entries * levels(stream_key, extent, cuts, -0.22, 0.18)
    return jnp.clip(entries, -reach, reach).astype(held_as)


def setup_inputs(seed: int = 0) -> dict:
    key_list = jax.random.split(jax.random.key(seed), 18)
    vis_stream = normal_values(key_list[0], (PAGES, PR, PC, D), 1.0, 6.0, ((0, 8), (1, 4)))
    query_stream = normal_values(key_list[1], (PAGES, QLEN, D), 1.0, 6.0, ((0, 8), (1, 4)))
    w_qkv = normal_values(key_list[2], (4, D, 3 * D), D ** -0.5, 0.21875)
    w_out = normal_values(key_list[3], (4, D, D), (max(D // 128, 1)) ** -0.5, 2.5)
    b_out = normal_values(key_list[4], (4, D), 0.5, 3.0, (), jnp.float32)
    w_up = normal_values(key_list[5], (2, D, FF), D ** -0.5, 0.21875)
    b_up = normal_values(key_list[6], (2, FF), 0.5, 3.0, (), jnp.float32)
    w_down = normal_values(key_list[7], (2, FF, D), FF ** -0.5, 0.109375)
    b_down = normal_values(key_list[8], (2, D), 0.5, 3.0, (), jnp.float32)
    norm_gain = jnp.clip(1.0 + 0.1 * jax.random.normal(key_list[9], (7, D), jnp.float32), 0.5, 1.5)
    norm_bias = normal_values(key_list[10], (7, D), 0.5, 3.0, (), jnp.float32)
    page_cols = draw_page_cols(jax.random.fold_in(key_list[17], 71), 0)
    query_len = draw_query_len(jax.random.fold_in(key_list[17], 71), 0)
    prompt_len = with_ends(jax.random.randint(key_list[13], (PAGES,), 1, 2 * Q_DEV), jax.random.fold_in(key_list[13], 1), 1, (2 * Q_DEV) - 1).astype(jnp.int32)
    region_ids = with_ends(jax.random.randint(key_list[14], (PAGES, PR, PC), 0, 3), jax.random.fold_in(key_list[14], 1), 0, 2).astype(jnp.int32)
    vis_cotangent = normal_values(key_list[15], (PAGES, PR, PC, D), 1.0, 6.0, ((0, 8), (1, 4)))
    query_cotangent = normal_values(key_list[16], (PAGES, QLEN, D), 1.0, 6.0, ((0, 8), (1, 4)))
    return dict(vis_stream=vis_stream, query_stream=query_stream, w_qkv=w_qkv, w_out=w_out, b_out=b_out, w_up=w_up, b_up=b_up, w_down=w_down, b_down=b_down, norm_gain=norm_gain, norm_bias=norm_bias, page_cols=page_cols, query_len=query_len, prompt_len=prompt_len, region_ids=region_ids, vis_cotangent=vis_cotangent, query_cotangent=query_cotangent)


@jax.custom_vjp
def low(v):
    return lax.optimization_barrier(v.astype(jnp.bfloat16)).astype(jnp.float32)

@jax.custom_vjp
def low_back(v):
    return v

def low_keep(v):
    return (low(v), None)

def low_pass(kept, grad):
    return (grad,)

def back_keep(v):
    return (v, None)

def back_low(kept, grad):
    return (low(grad),)
low.defvjp(low_keep, low_pass)
low_back.defvjp(back_keep, back_low)
highest = lax.Precision.HIGHEST
masked_score = -1e+30
norm_eps = 1e-05

def mat_dot(left, right):
    return jnp.dot(left, right, precision=highest, preferred_element_type=jnp.float32)

def rounded(values):
    return low_back(low(values))

def layer_norm(values, gain_row, bias_row):
    average = lax.optimization_barrier(jnp.mean(values, axis=-1, keepdims=True))
    centred = values - average
    spread = lax.optimization_barrier(jnp.mean(centred * centred, axis=-1, keepdims=True))
    return centred * lax.rsqrt(spread + norm_eps) * gain_row + bias_row

def to_windows(grid_cells):
    row_count, col_count = (grid_cells.shape[0], grid_cells.shape[1])
    trailing = grid_cells.shape[2:]
    carved = grid_cells.reshape((row_count // WIN, WIN, col_count // WIN, WIN) + trailing)
    return jnp.swapaxes(carved, 1, 2).reshape((-1, WIN * WIN) + trailing)

def from_windows(blocks, row_count, col_count):
    trailing = blocks.shape[2:]
    carved = blocks.reshape((row_count // WIN, col_count // WIN, WIN, WIN) + trailing)
    return jnp.swapaxes(carved, 1, 2).reshape((row_count, col_count) + trailing)

def attend_core(queries, key_rows, value_rows, allowed):
    q_heads = queries.reshape(queries.shape[0], -1, HDIM)
    k_heads = key_rows.reshape(key_rows.shape[0], -1, HDIM)
    v_heads = value_rows.reshape(value_rows.shape[0], -1, HDIM)
    scores = low_back(jnp.einsum('qhd,khd->hqk', q_heads, k_heads, precision=highest) * HDIM ** (-0.5))
    scores = jnp.where(allowed[None], scores, masked_score)
    probs_low = low(jax.nn.softmax(scores, axis=-1))
    context = jnp.einsum('hqk,khd->qhd', probs_low, v_heads, precision=highest)
    return context.reshape(queries.shape)

def attend_proj(from_rows, to_rows, weight, allowed):
    queries = rounded(mat_dot(from_rows, weight[:, :D]))
    paired = rounded(mat_dot(to_rows, weight[:, D:]))
    return attend_core(queries, paired[:, :D], paired[:, D:], allowed)

def window_attention(rolled, weight, region_page, live_cells):
    tiles = to_windows(rolled)
    window_count = tiles.shape[0]
    tile_rows = tiles.reshape(-1, D)
    queries = rounded(mat_dot(tile_rows, weight[:, :D])).reshape(window_count, WIN * WIN, D)
    paired = rounded(mat_dot(tile_rows, weight[:, D:])).reshape(window_count, WIN * WIN, 2 * D)
    region_tiles = to_windows(region_page)
    live_tiles = to_windows(live_cells)
    diagonal = jnp.eye(WIN * WIN, dtype=jnp.bool_)
    allowed = (region_tiles[:, :, None] == region_tiles[:, None, :]) & (live_tiles[:, None, :] | diagonal[None])
    context = jax.vmap(attend_core)(queries, paired[:, :, :D], paired[:, :, D:], allowed)
    return from_windows(context, rolled.shape[0], rolled.shape[1])

def branch_out(context, weight, bias_row):
    return low_back(mat_dot(rounded(context), weight) + bias_row)

def feed_forward(values, gain_row, bias_row, up_weight, up_bias, down_weight, down_bias):
    hidden = low(layer_norm(values, gain_row, bias_row))
    upward = low_back(mat_dot(hidden, up_weight) + up_bias)
    active = low(jax.nn.gelu(upward, approximate=True))
    return values + low_back(mat_dot(active, down_weight) + down_bias)

def page_forward(params, vis_page, query_page, col_limit, query_limit, prompt_limit, region_page):
    w_qkv, w_out, b_out, w_up, b_up, w_down, b_down, norm_gain, norm_bias = params
    page_rows, page_width = (vis_page.shape[0], vis_page.shape[1])
    positions = jnp.arange(query_page.shape[0])
    key_live = positions < query_limit
    hidden = low(layer_norm(query_page, norm_gain[1], norm_bias[1]))
    allowed = key_live[None, :] & ((positions[None, :] <= positions[:, None]) | (positions[None, :] < prompt_limit))
    query_page = query_page + branch_out(attend_proj(hidden, hidden, w_qkv[1], allowed), w_out[1], b_out[1])
    hidden = low(layer_norm(vis_page, norm_gain[0], norm_bias[0]))
    rolled = jnp.roll(hidden, (-SHIFT, -SHIFT), axis=(0, 1))
    rolled_live = (jnp.arange(page_width) + SHIFT) % page_width < col_limit
    live_cells = jnp.broadcast_to(rolled_live[None, :], (page_rows, page_width))
    context = jnp.roll(window_attention(rolled, w_qkv[0], region_page, live_cells), (SHIFT, SHIFT), axis=(0, 1))
    vis_rows = vis_page.reshape(-1, D) + branch_out(context.reshape(-1, D), w_out[0], b_out[0])
    hidden_ask = low(layer_norm(query_page, norm_gain[2], norm_bias[2]))
    hidden_look = low(layer_norm(vis_rows, norm_gain[3], norm_bias[3]))
    column_live = jnp.arange(vis_rows.shape[0]) % page_width < col_limit
    allowed = jnp.broadcast_to(column_live[None, :], (query_page.shape[0], vis_rows.shape[0]))
    query_page = query_page + branch_out(attend_proj(hidden_ask, hidden_look, w_qkv[2], allowed), w_out[2], b_out[2])
    hidden_memo = low(layer_norm(query_page, norm_gain[4], norm_bias[4]))
    allowed = jnp.broadcast_to(key_live[None, :], (vis_rows.shape[0], query_page.shape[0]))
    vis_rows = vis_rows + branch_out(attend_proj(hidden_look, hidden_memo, w_qkv[3], allowed), w_out[3], b_out[3])
    vis_rows = feed_forward(vis_rows, norm_gain[5], norm_bias[5], w_up[0], b_up[0], w_down[0], b_down[0])
    query_page = feed_forward(query_page, norm_gain[6], norm_bias[6], w_up[1], b_up[1], w_down[1], b_down[1])
    return (vis_rows.reshape(page_rows, page_width, D), query_page)

def reference(vis_stream, query_stream, w_qkv, w_out, b_out, w_up, b_up, w_down, b_down, norm_gain, norm_bias, page_cols, query_len, prompt_len, region_ids, vis_cotangent, query_cotangent):
    params = tuple((weight.astype(jnp.float32) for weight in (w_qkv, w_out, b_out, w_up, b_up, w_down, b_down, norm_gain, norm_bias)))

    def forward(weights, vis_all, query_all):

        def one_page(carried, page_items):
            return (carried, jax.checkpoint(page_forward)(weights, *page_items))
        return lax.scan(one_page, None, (vis_all, query_all, page_cols, query_len, prompt_len, region_ids))[1]
    outputs, pullback = jax.vjp(forward, params, vis_stream.astype(jnp.float32), query_stream.astype(jnp.float32))
    grads, vis_grad, query_grad = pullback((vis_cotangent.astype(jnp.float32), query_cotangent.astype(jnp.float32)))
    grad_qkv, grad_wout, grad_bout, grad_wup, grad_bup, grad_wdown, grad_bdown, grad_gain, grad_bias = grads
    return (outputs[0].astype(jnp.bfloat16), outputs[1].astype(jnp.bfloat16), vis_grad, query_grad, grad_qkv, grad_wout, grad_bout, grad_wup, grad_bup, grad_wdown, grad_bdown, grad_gain, grad_bias)
```

```python
from functools import partial

import jax
import jax.numpy as jnp
from jax import lax
from jax.sharding import PartitionSpec as P

HDIM = 64
WIN = 12
SHIFT = 6

masked_score = -1e30
norm_eps = 1e-05
bfloat = jnp.bfloat16


def ring(count, distance):
    return [(i, (i + distance) % count) for i in range(count)]


def flipped(count, bit):
    return [(i, i ^ bit) for i in range(count)]


def mat_dot(left, right):
    return jnp.dot(left, right, preferred_element_type=jnp.float32)


def mat_left(left, right):
    return lax.dot_general(
        left, right, (((0,), (0,)), ((), ())), preferred_element_type=jnp.float32
    )


def mat_right(left, right):
    return lax.dot_general(
        left, right, (((1,), (1,)), ((), ())), preferred_element_type=jnp.float32
    )


def norm_forward(values, gain_row, bias_row):
    average = jnp.mean(values, axis=-1, keepdims=True)
    centred = values - average
    spread = jnp.mean(centred * centred, axis=-1, keepdims=True)
    inverse = lax.rsqrt(spread + norm_eps)
    normal = centred * inverse
    return ((normal * gain_row + bias_row).astype(bfloat), normal, inverse)


def norm_backward(grad_result, normal, inverse, gain_row):
    grad_normal = grad_result * gain_row
    first_mean = jnp.mean(grad_normal, axis=-1, keepdims=True)
    second_mean = jnp.mean(grad_normal * normal, axis=-1, keepdims=True)
    grad_input = inverse * (grad_normal - first_mean - normal * second_mean)
    return (grad_input, jnp.sum(grad_result * normal, axis=0), jnp.sum(grad_result, axis=0))


def to_windows(grid_cells):
    row_count, col_count = (grid_cells.shape[0], grid_cells.shape[1])
    trailing = grid_cells.shape[2:]
    carved = grid_cells.reshape((row_count // WIN, WIN, col_count // WIN, WIN) + trailing)
    return jnp.swapaxes(carved, 1, 2).reshape((-1, WIN * WIN) + trailing)


def from_windows(blocks, row_count, col_count):
    trailing = blocks.shape[2:]
    carved = blocks.reshape((row_count // WIN, col_count // WIN, WIN, WIN) + trailing)
    return jnp.swapaxes(carved, 1, 2).reshape((row_count, col_count) + trailing)


def to_shifted(grid_cells):
    count = lax.axis_size("row")
    arriving = lax.ppermute(grid_cells[:SHIFT], "row", ring(count, -1))
    rolled = jnp.concatenate([grid_cells[SHIFT:], arriving], axis=0)
    return to_windows(jnp.roll(rolled, -SHIFT, axis=1)).reshape(-1, grid_cells.shape[2])


def from_shifted(tokens, row_count, col_count):
    count = lax.axis_size("row")
    cells = from_windows(tokens.reshape(-1, WIN * WIN, tokens.shape[1]), row_count, col_count)
    rolled = jnp.roll(cells, SHIFT, axis=1)
    arriving = lax.ppermute(rolled[row_count - SHIFT :], "row", ring(count, 1))
    return jnp.concatenate([arriving, rolled[: row_count - SHIFT]], axis=0)


def gather_row(values):
    count = lax.axis_size("row")
    parts = [values] + [lax.ppermute(values, "row", ring(count, s)) for s in range(1, count)]
    return jnp.concatenate(parts, axis=0)


def scatter_row(partial_sums):
    count = lax.axis_size("row")
    parts = jnp.split(partial_sums.astype(bfloat), count, axis=0)
    total = jnp.split(partial_sums, count, axis=0)[0]
    for s in range(1, count):
        total = total + lax.ppermute(parts[s], "row", ring(count, -s)).astype(jnp.float32)
    return total


def halve(blocks, bit, slot):
    count = lax.axis_size("page")
    mine = (lax.axis_index("page") // bit) % 2
    kept = lax.dynamic_index_in_dim(blocks, mine, slot, keepdims=False)
    sent = lax.dynamic_index_in_dim(blocks, 1 - mine, slot, keepdims=False)
    return kept + lax.ppermute(sent, "page", flipped(count, bit))


def reduce_matrix(grad):
    pages = lax.axis_size("page")
    rows = lax.axis_size("row")
    bits = []
    while 2 ** len(bits) < pages:
        bits.append(2 ** len(bits))
    height, width = grad.shape
    blocks = grad.astype(bfloat).reshape((2,) * len(bits) + (height // pages, width))
    if bits:
        blocks = halve(blocks, 1, len(bits) - 1)
    left, right = jnp.split(blocks, 2, axis=-1)
    rest = bits[1:]
    for bit in rest:
        left = halve(left, bit, left.ndim - 3)
    for bit in reversed(rest):
        right = halve(right, bit, 0)
    share = jnp.concatenate([left, right], axis=-1)
    me = lax.axis_index("row")
    pieces = share.reshape(share.shape[0], rows, width // rows)
    total = lax.dynamic_index_in_dim(pieces, me, 1, keepdims=False).astype(jnp.float32)
    for s in range(1, rows):
        sent = lax.dynamic_index_in_dim(pieces, (me + s) % rows, 1, keepdims=False)
        total = total + lax.ppermute(sent, "row", ring(rows, s)).astype(jnp.float32)
    return total


def reduce_vectors(stack):
    pages = lax.axis_size("page")
    rows = lax.axis_size("row")
    bit = 1
    while bit < pages:
        stack = stack.reshape(-1, 2, stack.shape[-1])
        stack = halve(stack, bit, 1)
        bit *= 2
    vector = stack.reshape(-1)
    total = vector
    for s in range(1, rows):
        total = total + lax.ppermute(vector, "row", ring(rows, s))
    return total


def split_heads(values):
    return values.reshape(values.shape[0], values.shape[1], -1, HDIM)


def masked_scores(queries, key_rows, allowed):
    scores = jnp.einsum(
        "gqhd,gkhd->ghqk",
        split_heads(queries),
        split_heads(key_rows),
        preferred_element_type=jnp.float32,
    ) * HDIM ** (-0.5)
    return jnp.where(allowed[:, None], scores, masked_score)


def attend_forward(queries, key_rows, value_rows, allowed):
    scores = masked_scores(queries, key_rows, allowed)
    row_max = jnp.max(scores, axis=-1, keepdims=True)
    raised = jnp.exp(scores - row_max)
    row_total = jnp.sum(raised, axis=-1, keepdims=True)
    probs_low = (raised / row_total).astype(bfloat)
    context = jnp.einsum(
        "ghqk,gkhd->gqhd", probs_low, split_heads(value_rows), preferred_element_type=jnp.float32
    )
    return (context.reshape(queries.shape).astype(bfloat), row_max + jnp.log(row_total))


def attend_backward(queries, key_rows, value_rows, allowed, log_total, grad_context):
    probs = jnp.exp(masked_scores(queries, key_rows, allowed) - log_total)
    probs_low = probs.astype(bfloat)
    grad_heads = split_heads(grad_context)
    grad_values = jnp.einsum(
        "ghqk,gqhd->gkhd", probs_low, grad_heads, preferred_element_type=jnp.float32
    )
    grad_probs = jnp.einsum(
        "gqhd,gkhd->ghqk", grad_heads, split_heads(value_rows), preferred_element_type=jnp.float32
    )
    row_delta = jnp.sum(probs * grad_probs, axis=-1, keepdims=True)
    grad_scores = (probs * (grad_probs - row_delta)).astype(bfloat)
    grad_queries = jnp.einsum(
        "ghqk,gkhd->gqhd", grad_scores, split_heads(key_rows), preferred_element_type=jnp.float32
    ) * HDIM ** (-0.5)
    grad_keys = jnp.einsum(
        "ghqk,gqhd->gkhd", grad_scores, split_heads(queries), preferred_element_type=jnp.float32
    ) * HDIM ** (-0.5)
    return (
        grad_queries.reshape(queries.shape).astype(bfloat),
        grad_keys.reshape(key_rows.shape).astype(bfloat),
        grad_values.reshape(value_rows.shape).astype(bfloat),
    )


def project(from_rows, to_rows, weight):
    width = weight.shape[0]
    queries = mat_dot(from_rows, weight[:, :width]).astype(bfloat)
    paired = mat_dot(to_rows, weight[:, width:]).astype(bfloat)
    return (queries, paired[:, :width], paired[:, width:])


def project_back(from_rows, to_rows, weight, dq, dk, dv):
    width = weight.shape[0]
    pair = jnp.concatenate([dk, dv], axis=1)
    weight_grad = jnp.concatenate([mat_left(from_rows, dq), mat_left(to_rows, pair)], axis=1)
    return (weight_grad, mat_right(dq, weight[:, :width]), mat_right(pair, weight[:, width:]))


def output_back(context_low, weight, grad_residual):
    grad_low = grad_residual.astype(bfloat)
    return (
        mat_left(context_low, grad_low),
        jnp.sum(grad_low, axis=0, dtype=jnp.float32),
        mat_right(grad_low, weight).astype(bfloat),
    )


def feed_forward(values, gain_row, bias_row, up_weight, up_bias, down_weight, down_bias):
    hidden, normal, inverse = norm_forward(values, gain_row, bias_row)
    upward = mat_dot(hidden, up_weight) + up_bias
    active = jax.nn.gelu(upward, approximate=True).astype(bfloat)
    return (
        values + (mat_dot(active, down_weight) + down_bias),
        (hidden, normal, inverse, upward, active),
    )


def feed_backward(grad_residual, kept_values, gain_row, up_weight, down_weight):
    hidden, normal, inverse, upward, active = kept_values
    grad_low = grad_residual.astype(bfloat)
    grad_down = mat_left(active, grad_low)
    grad_down_bias = jnp.sum(grad_low, axis=0, dtype=jnp.float32)
    grad_active = mat_right(grad_low, down_weight)
    gelu_pull = jax.vjp(partial(jax.nn.gelu, approximate=True), upward)[1]
    grad_up_low = gelu_pull(grad_active)[0].astype(bfloat)
    grad_up = mat_left(hidden, grad_up_low)
    grad_up_bias = jnp.sum(grad_up_low, axis=0, dtype=jnp.float32)
    grad_input, gain_grad, bias_grad = norm_backward(
        mat_right(grad_up_low, up_weight), normal, inverse, gain_row
    )
    return (
        grad_residual + grad_input,
        (grad_up, grad_up_bias, grad_down, grad_down_bias, gain_grad, bias_grad),
    )


def shards(
    vis_stream,
    query_stream,
    w_qkv,
    w_out,
    b_out,
    w_up,
    b_up,
    w_down,
    b_down,
    norm_gain,
    norm_bias,
    page_cols,
    query_len,
    prompt_len,
    region_ids,
    vis_cotangent,
    query_cotangent,
):
    band_rows, page_width, width = vis_stream.shape[1:]
    tokens = band_rows * page_width
    query_rows = query_stream.shape[1]
    bands = lax.axis_size("row")
    me = lax.axis_index("row")
    pages = lax.axis_size("page")
    x0 = to_shifted(vis_stream[0]).astype(jnp.float32)
    gx3 = to_shifted(vis_cotangent[0]).astype(jnp.float32)
    y0 = query_stream[0].astype(jnp.float32)
    gy3 = query_cotangent[0].astype(jnp.float32)
    col_limit, query_limit, prompt_limit = page_cols[0], query_len[0], prompt_len[0]

    own_positions = me * query_rows + jnp.arange(query_rows)
    all_positions = jnp.concatenate(
        [((me - s) % bands) * query_rows + jnp.arange(query_rows) for s in range(bands)]
    )
    key_live = all_positions < query_limit
    self_allowed = key_live[None, :] & (
        (all_positions[None, :] <= own_positions[:, None]) | (all_positions[None, :] < prompt_limit)
    )
    rolled_live = (jnp.arange(page_width) + SHIFT) % page_width < col_limit
    live_tiles = to_windows(jnp.broadcast_to(rolled_live[None, :], (band_rows, page_width)))
    visual_allowed = jnp.broadcast_to(
        jnp.tile(live_tiles.reshape(-1), bands)[None, :], (query_rows, bands * tokens)
    )
    query_allowed = jnp.broadcast_to(key_live[None, :], (tokens, query_rows * bands))
    region_tiles = to_windows(region_ids[0])
    diagonal = jnp.eye(WIN * WIN, dtype=jnp.bool_)
    window_allowed = (region_tiles[:, :, None] == region_tiles[:, None, :]) & (
        live_tiles[:, None, :] | diagonal[None]
    )
    tile_shape = (tokens // (WIN * WIN), WIN * WIN, width)

    hs, n1, i1 = norm_forward(y0, norm_gain[1], norm_bias[1])
    hs_all = gather_row(hs)
    hv, n0, i0 = norm_forward(x0, norm_gain[0], norm_bias[0])
    qw, kw, vw = (v.reshape(tile_shape) for v in project(hv, hv, w_qkv[0]))
    cw, lw = attend_forward(qw, kw, vw, window_allowed)
    cw = cw.reshape(tokens, width)
    x1 = x0 + (mat_dot(cw, w_out[0]) + b_out[0])
    hl, n3, i3 = norm_forward(x1, norm_gain[3], norm_bias[3])
    hl_all = gather_row(hl)

    qs, ks, vs = project(hs, hs_all, w_qkv[1])
    cs, ls = attend_forward(qs[None], ks[None], vs[None], self_allowed[None])
    cs = cs[0]
    y1 = y0 + (mat_dot(cs, w_out[1]) + b_out[1])
    ha, n2, i2 = norm_forward(y1, norm_gain[2], norm_bias[2])
    qa, kl, vl = project(ha, hl_all, w_qkv[2])
    ca, la = attend_forward(qa[None], kl[None], vl[None], visual_allowed[None])
    ca = ca[0]
    y2 = y1 + (mat_dot(ca, w_out[2]) + b_out[2])
    hm, n4, i4 = norm_forward(y2, norm_gain[4], norm_bias[4])
    hm_all = gather_row(hm)
    y3, kept_query = feed_forward(
        y2, norm_gain[6], norm_bias[6], w_up[1], b_up[1], w_down[1], b_down[1]
    )
    gy2, feed_query = feed_backward(gy3, kept_query, norm_gain[6], w_up[1], w_down[1])
    final_up1 = reduce_matrix(feed_query[0])
    final_down1 = reduce_matrix(feed_query[2])

    qr, km, vm = project(hl, hm_all, w_qkv[3])
    cr, lr = attend_forward(qr[None], km[None], vm[None], query_allowed[None])
    cr = cr[0]
    x2 = x1 + (mat_dot(cr, w_out[3]) + b_out[3])
    x3, kept_vis = feed_forward(
        x2, norm_gain[5], norm_bias[5], w_up[0], b_up[0], w_down[0], b_down[0]
    )
    gx2, feed_vis = feed_backward(gx3, kept_vis, norm_gain[5], w_up[0], w_down[0])
    final_up0 = reduce_matrix(feed_vis[0])
    final_down0 = reduce_matrix(feed_vis[2])

    wout3, bout3, dcr = output_back(cr, w_out[3], gx2)
    dqr, dkm, dvm = attend_backward(
        qr[None], km[None], vm[None], query_allowed[None], lr, dcr[None]
    )
    qkv3, dhl, dhm = project_back(hl, hm_all, w_qkv[3], dqr[0], dkm[0], dvm[0])
    gy_memo, gain4, bias4 = norm_backward(scatter_row(dhm), n4, i4, norm_gain[4])
    gy2 = gy2 + gy_memo
    final_out3 = reduce_matrix(wout3)
    final_qkv3 = reduce_matrix(qkv3)

    wout2, bout2, dca = output_back(ca, w_out[2], gy2)
    dqa, dkl, dvl = attend_backward(
        qa[None], kl[None], vl[None], visual_allowed[None], la, dca[None]
    )
    qkv2, dha, dhl_all = project_back(ha, hl_all, w_qkv[2], dqa[0], dkl[0], dvl[0])
    gy_ask, gain2, bias2 = norm_backward(dha, n2, i2, norm_gain[2])
    gy1 = gy2 + gy_ask
    gx_look, gain3, bias3 = norm_backward(dhl + scatter_row(dhl_all), n3, i3, norm_gain[3])
    gx1 = gx2 + gx_look
    final_out2 = reduce_matrix(wout2)
    final_qkv2 = reduce_matrix(qkv2)

    wout1, bout1, dcs = output_back(cs, w_out[1], gy1)
    dqs, dks, dvs = attend_backward(qs[None], ks[None], vs[None], self_allowed[None], ls, dcs[None])
    qkv1, dhs, dhs_all = project_back(hs, hs_all, w_qkv[1], dqs[0], dks[0], dvs[0])
    gy_self, gain1, bias1 = norm_backward(dhs + scatter_row(dhs_all), n1, i1, norm_gain[1])
    gy0 = gy1 + gy_self
    final_out1 = reduce_matrix(wout1)
    final_qkv1 = reduce_matrix(qkv1)

    wout0, bout0, dcw = output_back(cw, w_out[0], gx1)
    dqw, dkw, dvw = attend_backward(qw, kw, vw, window_allowed, lw, dcw.reshape(tile_shape))
    dqw, dkw, dvw = (v.reshape(tokens, width) for v in (dqw, dkw, dvw))
    qkv0, dr_from, dr_into = project_back(hv, hv, w_qkv[0], dqw, dkw, dvw)
    gx_win, gain0, bias0 = norm_backward(dr_from + dr_into, n0, i0, norm_gain[0])
    gx0 = gx1 + gx_win
    final_out0 = reduce_matrix(wout0)
    final_qkv0 = reduce_matrix(qkv0)

    vectors = [
        jnp.stack([bout0, bout1, bout2, bout3]),
        jnp.stack([feed_vis[1], feed_query[1]]),
        jnp.stack([feed_vis[3], feed_query[3]]),
        jnp.stack([gain0, gain1, gain2, gain3, gain4, feed_vis[4], feed_query[4]]),
        jnp.stack([bias0, bias1, bias2, bias3, bias4, feed_vis[5], feed_query[5]]),
    ]
    blocks = [
        jnp.swapaxes(v.reshape(v.shape[0], pages, -1), 0, 1).reshape(pages, -1) for v in vectors
    ]
    reduced = reduce_vectors(jnp.concatenate(blocks, axis=1))
    finals, start = [], 0
    for v in vectors:
        size = v.size // pages
        finals.append(reduced[start : start + size].reshape(v.shape[0], -1))
        start += size

    return (
        from_shifted(x3.astype(bfloat), band_rows, page_width)[None],
        y3[None].astype(bfloat),
        from_shifted(gx0, band_rows, page_width)[None],
        gy0[None],
        jnp.stack([final_qkv0, final_qkv1, final_qkv2, final_qkv3]),
        jnp.stack([final_out0, final_out1, final_out2, final_out3]),
        finals[0],
        jnp.stack([final_up0, final_up1]),
        finals[1],
        jnp.stack([final_down0, final_down1]),
        finals[2],
        finals[3],
        finals[4],
    )


def solution(mesh):
    return jax.shard_map(
        shards,
        mesh=mesh,
        in_specs=(
            P("page", "row", None, None),
            P("page", "row", None),
            P(),
            P(),
            P(),
            P(),
            P(),
            P(),
            P(),
            P(),
            P(),
            P("page"),
            P("page"),
            P("page"),
            P("page", "row", None),
            P("page", "row", None, None),
            P("page", "row", None),
        ),
        out_specs=(
            P("page", "row", None, None),
            P("page", "row", None),
            P("page", "row", None, None),
            P("page", "row", None),
            P(None, "page", "row"),
            P(None, "page", "row"),
            P(None, "page"),
            P(None, "page", "row"),
            P(None, "page"),
            P(None, "page", "row"),
            P(None, "page"),
            P(None, "page"),
            P(None, "page"),
        ),
        check_vma=False,
    )
```

```python
from functools import partial

import jax
import jax.numpy as jnp
import numpy as np
from jax import lax
from jax.experimental import pallas as pl
from jax.experimental.pallas import tpu as pltpu
from jax.sharding import PartitionSpec as P

HDIM = 64
WIN = 12
SHIFT = 6
PAIR = 2 * HDIM
SCALE = HDIM ** (-0.5)

masked_score = -1e30
norm_eps = 1e-05
bfloat = jnp.bfloat16
full = jnp.float32
ANY = pl.BlockSpec(memory_space=pl.ANY)
VMEM = pl.BlockSpec(memory_space=pltpu.VMEM)
SMEM = pl.BlockSpec(memory_space=pltpu.SMEM)
MESH = pl.DeviceIdType.MESH


def ring(count, distance):
    return [(i, (i + distance) % count) for i in range(count)]


def flipped(count, bit):
    return [(i, i ^ bit) for i in range(count)]


def dot_nn(left, right):
    return jnp.dot(left, right, preferred_element_type=full)


def dot_nt(left, right):
    return lax.dot_general(left, right, (((1,), (1,)), ((), ())), preferred_element_type=full)


def dot_tn(left, right):
    return lax.dot_general(left, right, (((0,), (0,)), ((), ())), preferred_element_type=full)


def normalise(values):
    centred = values - jnp.mean(values, axis=-1, keepdims=True)
    spread = jnp.mean(centred * centred, axis=-1, keepdims=True)
    inverse = lax.rsqrt(spread + norm_eps)
    return centred * inverse, inverse


def norm_forward(values, gain_row, bias_row):
    return (normalise(values)[0] * gain_row + bias_row).astype(bfloat)


def norm_backward(grad, values, gain_row):
    normal, inverse = normalise(values)
    grad_normal = grad * gain_row
    first = jnp.mean(grad_normal, axis=-1, keepdims=True)
    second = jnp.mean(grad_normal * normal, axis=-1, keepdims=True)
    return (
        inverse * (grad_normal - first - normal * second),
        jnp.sum(grad * normal, axis=0, keepdims=True),
        jnp.sum(grad, axis=0, keepdims=True),
    )


def tile_cols(index, size):
    return pl.ds(pl.multiple_of(index * size, size), size)


def matmul_into(out_ref, left_ref, weight_ref, size):
    def step(i, _):
        cols = tile_cols(i, size)
        out_ref[:, cols] = dot_nn(left_ref[...], weight_ref[:, cols]).astype(out_ref.dtype)
        return 0

    lax.fori_loop(0, weight_ref.shape[1] // size, step, 0)


def two_heads(values):
    lane = lax.broadcasted_iota(jnp.int32, values.shape, 1)
    zero = jnp.zeros_like(values)
    return jnp.concatenate(
        [jnp.where(lane < HDIM, values, zero), jnp.where(lane < HDIM, zero, values)], axis=0
    )


def one_pair(stacked):
    count = stacked.shape[0] // 2
    lane = lax.broadcasted_iota(jnp.int32, (count, PAIR), 1)
    return jnp.where(lane < HDIM, stacked[:count], stacked[count:])


def attend_pair(queries, key_rows, value_rows, bias):
    scores = dot_nt(two_heads(queries), key_rows) + bias
    top = jnp.max(scores, axis=-1, keepdims=True)
    raised = jnp.exp(scores - top)
    total = jnp.sum(raised, axis=-1, keepdims=True)
    context = dot_nn(raised.astype(bfloat), value_rows) / total
    return one_pair(context).astype(bfloat), top + jnp.log(total)


def attend_pair_back(queries, key_rows, value_rows, bias, log_total, context, grad_context):
    both = two_heads(queries)
    grad_both = two_heads(grad_context)
    probs = jnp.exp(dot_nt(both, key_rows) + bias - log_total)
    grad_probs = dot_nt(grad_both, value_rows)
    delta = jnp.sum(
        grad_both.astype(full) * jnp.concatenate([context, context], axis=0).astype(full),
        axis=-1,
        keepdims=True,
    )
    grad_scores = (probs * (grad_probs - delta)).astype(bfloat)
    grad_queries = one_pair(dot_nn(grad_scores, key_rows)) * SCALE
    grad_keys = dot_tn(grad_scores, both)
    grad_values = dot_tn(probs.astype(bfloat), grad_both)
    return grad_queries.astype(bfloat), grad_keys.astype(bfloat), grad_values.astype(bfloat)


def put_logs(log_ref, rows, pair, log_total):
    count = log_total.shape[0] // 2
    lane = lax.broadcasted_iota(jnp.int32, (count, PAIR), 1)
    kept = log_ref[rows, :]
    kept = jnp.where(lane == 2 * pair, log_total[:count], kept)
    log_ref[rows, :] = jnp.where(lane == 2 * pair + 1, log_total[count:], kept)


def take_logs(log_ref, rows, pair):
    kept = log_ref[rows, :]
    lane = lax.broadcasted_iota(jnp.int32, kept.shape, 1)
    parts = [
        jnp.sum(jnp.where(lane == 2 * pair + i, kept, 0.0), axis=-1, keepdims=True)
        for i in range(2)
    ]
    return jnp.concatenate(parts, axis=0)


def attend_rows(q_ref, kv_ref, context_ref, log_ref, bias, rows, keys):
    width = q_ref.shape[1]
    key_start = kv_ref.shape[1] - 2 * width

    def step(pair, _):
        cols = tile_cols(pair, PAIR)
        key_cols = pl.ds(pl.multiple_of(key_start + pair * PAIR, PAIR), PAIR)
        value_cols = pl.ds(pl.multiple_of(key_start + width + pair * PAIR, PAIR), PAIR)
        context, log_total = attend_pair(
            q_ref[rows, cols], kv_ref[keys, key_cols], kv_ref[keys, value_cols], bias
        )
        context_ref[rows, cols] = context
        put_logs(log_ref, rows, pair, log_total)
        return 0

    lax.fori_loop(0, width // PAIR, step, 0)


def attend_rows_back(
    q_ref, kv_ref, context_ref, log_ref, grad_ref, dq_ref, dkv_ref, bias, rows, keys
):
    width = q_ref.shape[1]
    key_start = kv_ref.shape[1] - 2 * width
    grad_start = dkv_ref.shape[1] - 2 * width

    def step(pair, _):
        cols = tile_cols(pair, PAIR)
        key_cols = pl.ds(pl.multiple_of(key_start + pair * PAIR, PAIR), PAIR)
        value_cols = pl.ds(pl.multiple_of(key_start + width + pair * PAIR, PAIR), PAIR)
        dq, dk, dv = attend_pair_back(
            q_ref[rows, cols],
            kv_ref[keys, key_cols],
            kv_ref[keys, value_cols],
            bias,
            take_logs(log_ref, rows, pair),
            context_ref[rows, cols],
            grad_ref[rows, cols],
        )
        dq_ref[rows, cols] = dq
        dkv_ref[keys, pl.ds(pl.multiple_of(grad_start + pair * PAIR, PAIR), PAIR)] = dk
        dkv_ref[keys, pl.ds(pl.multiple_of(grad_start + width + pair * PAIR, PAIR), PAIR)] = dv
        return 0

    lax.fori_loop(0, width // PAIR, step, 0)


def allowed_bias(allowed):
    return jnp.where(allowed, 0.0, masked_score).astype(full)


def key_positions(me, bands, rows):
    lane = lax.broadcasted_iota(jnp.int32, (1, bands * rows), 1)
    part = sum((lane >= s * rows).astype(jnp.int32) for s in range(1, bands))
    band = lax.rem(me - part + bands, bands)
    return band * rows + lane - part * rows


def window_live(first, count, scalars, page_width):
    token = first + lax.broadcasted_iota(jnp.int32, (1, count), 1)
    window = lax.div(token, WIN * WIN)
    column = lax.rem(token, WIN) + WIN * lax.rem(window, page_width // WIN)
    return lax.rem(column + SHIFT, page_width) < scalars[1]


def copies_in(pairs, sems):
    copies = [pltpu.make_async_copy(src, dst, sems.at[i]) for i, (src, dst) in enumerate(pairs)]
    for copy in copies:
        copy.start()
    return copies


def low_shape(*shape):
    return jax.ShapeDtypeStruct(shape, bfloat)


def full_shape(*shape):
    return jax.ShapeDtypeStruct(shape, full)


def source_order(page_width, band_rows):
    tokens = band_rows * page_width
    token = np.arange(tokens)
    across = page_width // WIN
    window, inside = token // (WIN * WIN), token % (WIN * WIN)
    row = window // across * WIN + inside // WIN
    column = window % across * WIN + inside % WIN
    source = row * page_width + (column + SHIFT) % page_width
    order = np.zeros((tokens, tokens), np.float32)
    order[token, source] = 1.0
    return order


def fill_shifted(own_ref, arriving_ref, rows_ref):
    band_rows, width = own_ref.shape[1], own_ref.shape[2]
    for i in range(band_rows - SHIFT):
        rows_ref[i * width : (i + 1) * width, :] = own_ref[0, i + SHIFT].astype(full)
    for i in range(SHIFT):
        j = band_rows - SHIFT + i
        rows_ref[j * width : (j + 1) * width, :] = arriving_ref[i].astype(full)


def window_bias(scalars, region_col_ref, region_row_ref, w, page_width):
    size = WIN * WIN
    live = window_live(w * size, size, scalars, page_width)
    own = lax.broadcasted_iota(jnp.int32, (size, size), 0)
    other = lax.broadcasted_iota(jnp.int32, (size, size), 1)
    same = region_col_ref[w] == region_row_ref[w]
    allowed = same & ((own == other) | live)
    bias = allowed_bias(allowed)
    return jnp.concatenate([bias, bias], axis=0)


def self_bias(me, scalars, rows, bands):
    position = key_positions(me, bands, rows)
    own = me * rows + lax.broadcasted_iota(jnp.int32, (rows, 1), 0)
    bias = allowed_bias(
        (position < scalars[2]) & ((position <= own) | (position < scalars[3]))
    )
    return jnp.concatenate([bias, bias], axis=0)


def look_bias(dims, scalars):
    tokens, bands, page_width = dims["tokens"], dims["bands"], dims["page_width"]
    live = window_live(0, tokens, scalars, page_width)
    return jnp.concatenate([allowed_bias(live)] * bands, axis=1)


def read_bias(me, dims, scalars):
    return allowed_bias(key_positions(me, dims["bands"], dims["rows"]) < scalars[2])


class Kernel:
    def __init__(self, refs, hbm, sems):
        self.__dict__.update(refs)
        self.hbm, self.sems = hbm, sems
        self.coming, self.going = {}, []

    def fetch(self, *names):
        for name in names:
            copy = pltpu.make_async_copy(
                self.hbm[name], getattr(self, name), self.sems[name]
            )
            copy.start()
            self.coming[name] = copy

    def ready(self, *names):
        for name in names:
            self.coming.pop(name).wait()

    def save(self, *names):
        for name in names:
            copy = pltpu.make_async_copy(
                getattr(self, name), self.hbm[name], self.sems[name]
            )
            copy.start()
            self.going.append(copy)

    def finish(self):
        for copy in self.going:
            copy.wait()


def launch(body, given, staged, made, kept, scratch, collective, flops):
    sources = list(given) + list(staged)
    results = list(made) + list(kept)
    moved = list(staged) + list(kept)
    arrays = [given[n][0] for n in given] + [staged[n] for n in staged]
    stages = {n: pltpu.VMEM(staged[n].shape, staged[n].dtype) for n in staged}
    stages.update({n: pltpu.VMEM(kept[n].shape, kept[n].dtype) for n in kept})

    def inner(*refs):
        first, second = len(sources), len(sources) + len(results)
        outer = dict(zip(sources, refs[:first])) | dict(zip(results, refs[first:second]))
        inside = dict(zip(list(stages) + list(scratch), refs[second:-1]))
        sems = {n: refs[-1].at[i] for i, n in enumerate(moved)}
        body(Kernel(outer | inside, {n: outer[n] for n in moved}, sems))

    outs = pl.pallas_call(
        inner,
        out_shape=[made[n][0] for n in made] + [kept[n] for n in kept],
        in_specs=[given[n][1] for n in given] + [ANY] * len(staged),
        out_specs=[made[n][1] for n in made] + [ANY] * len(kept),
        scratch_shapes=list(stages.values())
        + list(scratch.values())
        + [pltpu.SemaphoreType.DMA((max(len(moved), 1),))],
        compiler_params=pltpu.CompilerParams(
            vmem_limit_bytes=62 * 2**20, collective_id=collective, has_side_effects=True
        ),
        cost_estimate=pl.CostEstimate(flops=flops, bytes_accessed=2**24, transcendentals=0),
    )(*arrays)
    return dict(zip(results, outs))


def greet(devices):
    barrier = pltpu.get_barrier_semaphore()
    for device in devices:
        pl.semaphore_signal(barrier, inc=1, device_id=device, device_id_type=MESH)
    pl.semaphore_wait(barrier, len(devices))


def band_peers(bands):
    me = lax.axis_index("row")
    return [{"row": lax.rem(me + s, bands)} for s in range(1, bands)]


def gather_start(ref, bands, send, recv):
    copies = []
    for s, peer in enumerate(band_peers(bands), 1):
        copy = pltpu.make_async_remote_copy(
            src_ref=ref.at[0],
            dst_ref=ref.at[s],
            send_sem=send.at[s - 1],
            recv_sem=recv.at[s - 1],
            device_id=peer,
            device_id_type=MESH,
        )
        copy.start()
        copies.append(copy)
    return copies


def front_kernel(dims, r):
    page_width, bands, rows, tokens = (dims[n] for n in ("page_width", "bands", "rows", "tokens"))
    width = r.y0.shape[1]
    me = lax.axis_index("row")
    greet(band_peers(bands))
    loads = {}
    for a in range(3):
        for i, (name, ref) in enumerate((("wqkv%d", r.w_qkv), ("wout%d", r.w_out))):
            copy = pltpu.make_async_copy(
                ref.at[a], getattr(r, name % a), r.weight_sems.at[2 * a + i]
            )
            copy.start()
            loads[name % a] = copy
    above = {"row": lax.rem(me + bands - 1, bands)}
    halos = []
    for i, ref in enumerate((r.vis, r.cot)):
        halo = pltpu.make_async_remote_copy(
            src_ref=ref.at[0, 0:SHIFT],
            dst_ref=r.halo.at[i],
            send_sem=r.halo_send.at[i],
            recv_sem=r.halo_recv.at[i],
            device_id=above,
            device_id_type=MESH,
        )
        halo.start()
        halos.append(halo)
    r.hs[0] = norm_forward(r.y0[...].astype(full), r.gain[1:2, :], r.bias[1:2, :])
    self_copies = gather_start(r.hs, bands, r.self_send, r.self_recv)

    r.log0[...] = jnp.zeros_like(r.log0)
    r.log1[...] = jnp.zeros_like(r.log1)
    r.log2[...] = jnp.zeros_like(r.log2)
    halos[0].wait()
    fill_shifted(r.vis, r.halo.at[0], r.cells)
    x0 = dot_nn(r.order[...], r.cells[...].astype(bfloat))
    r.x0[...] = x0.astype(bfloat)
    r.hv[...] = norm_forward(x0, r.gain[0:1, :], r.bias[0:1, :])
    r.save("x0", "hv")
    loads["wqkv0"].wait()
    r.q0[...] = (dot_nn(r.hv[...], r.wqkv0[:, :width]) * SCALE).astype(bfloat)
    matmul_into(r.kv0, r.hv, r.wqkv0.at[:, width:], width)
    r.save("q0", "kv0")
    size = WIN * WIN
    for w in range(tokens // size):
        part = slice(w * size, (w + 1) * size)
        bias = window_bias(r.scalars, r.region_col, r.region_row, w, page_width)
        attend_rows(r.q0, r.kv0, r.c0, r.log0, bias, part, part)
    r.save("c0", "log0")
    loads["wout0"].wait()
    x1 = r.x0[...].astype(full) + (dot_nn(r.c0[...], r.wout0[...]) + r.b_out[0:1, :])
    r.x1[...] = x1
    r.hl[0] = norm_forward(x1, r.gain[3:4, :], r.bias[3:4, :])
    look_copies = gather_start(r.hl, bands, r.look_send, r.look_recv)
    r.save("x1")

    halos[1].wait()
    fill_shifted(r.cot, r.halo.at[1], r.cells)
    r.gx3[...] = dot_nn(r.order[...], r.cells[...].astype(bfloat)).astype(bfloat)
    r.save("gx3")
    loads["wqkv1"].wait()
    r.q1[...] = (dot_nn(r.hs[0], r.wqkv1[:, :width]) * SCALE).astype(bfloat)
    for copy in self_copies:
        copy.wait_recv()

    def project_self(s, _):
        part = pl.ds(pl.multiple_of(s * rows, rows), rows)
        r.kv1[part, :] = dot_nn(r.hs[s], r.wqkv1[:, width:]).astype(bfloat)
        return 0

    lax.fori_loop(0, bands, project_self, 0)
    r.save("hs", "q1", "kv1")
    bias = self_bias(me, r.scalars, rows, bands)
    attend_rows(r.q1, r.kv1, r.c1, r.log1, bias, slice(None), slice(None))
    r.save("c1", "log1")
    loads["wout1"].wait()
    y1 = r.y0[...].astype(full) + (dot_nn(r.c1[...], r.wout1[...]) + r.b_out[1:2, :])
    r.y1[...] = y1
    r.ha[...] = norm_forward(y1, r.gain[2:3, :], r.bias[2:3, :])
    loads["wqkv2"].wait()
    r.q2[...] = (dot_nn(r.ha[...], r.wqkv2[:, :width]) * SCALE).astype(bfloat)
    r.save("y1", "ha", "q2")

    for s in range(bands):
        if s:
            look_copies[s - 1].wait_recv()
        part = slice(s * tokens, (s + 1) * tokens)
        matmul_into(r.kv2.at[part], r.hl.at[s], r.wqkv2.at[:, width:], width)
    r.save("hl", "kv2")
    attend_rows(r.q2, r.kv2, r.c2, r.log2, look_bias(dims, r.scalars), slice(None), slice(None))
    loads["wout2"].wait()
    y2 = r.y1[...] + (dot_nn(r.c2[...], r.wout2[...]) + r.b_out[2:3, :])
    r.y2[...] = y2
    r.hm[...] = norm_forward(y2, r.gain[4:5, :], r.bias[4:5, :])
    r.save("c2", "log2", "y2", "hm")
    for copy in self_copies + look_copies:
        copy.wait_send()
    r.finish()


def feed_phase(dims, r, stream, norm, values, cot, out, grad, units):
    pages, slab, bands = dims["pages"], dims["slab"], dims["bands"]
    count, width = values.shape
    core = lax.rem(lax.axis_index("page"), 2)
    r.hidden[...] = norm_forward(values[...], r.gain[norm : norm + 1, :], r.bias[norm : norm + 1, :])
    r.total[...] = values[...] + r.b_down[stream : stream + 1, :]
    r.back[...] = jnp.zeros_like(r.back)
    r.down_bias[...] = jnp.sum(cot[...].astype(full), axis=0, keepdims=True)

    def quarter(j, _):
        feed_copy(r, stream, 0, j).wait()
        hidden = r.hidden[...]
        z = dot_nn(hidden, r.up[j]) + r.b_up[stream : stream + 1, tile_cols(j, width)]
        square = z * z
        bend = jnp.tanh(0.7978845608028654 * (z + 0.044715 * (square * z)))
        half = 0.5 * (1.0 + bend)
        slope = half + (0.5 * z) * (1.0 - bend * bend) * (
            0.7978845608028654 * (1.0 + 0.134145 * square)
        )
        active = (z * half).astype(bfloat)
        feed_copy(r, stream, 1, j).wait()
        r.total[...] += dot_nn(active, r.down[j])
        low_grad = cot[...]
        dz = dot_nt(low_grad, r.down[j]) * slope
        r.up_bias[:, tile_cols(j, width)] = jnp.sum(dz, axis=0, keepdims=True)
        dz = dz.astype(bfloat)
        r.back[...] += dot_nt(dz, r.up[j])
        split_blocks(dims, r.tile.at[j, 0], dot_tn(hidden, dz).astype(bfloat), core)
        exchange(r, j, 0).start()
        down_grad = dot_tn(active, low_grad).astype(bfloat)
        deep = bands * slab
        for side in range(2):
            part = down_grad[side * deep : (side + 1) * deep]
            for k in range(bands):
                r.tile[j, 1, lax.rem(side + core, 2), k] = part[k * slab : (k + 1) * slab]
        exchange(r, j, 1).start()
        return 0

    lax.fori_loop(0, bands, quarter, 0)
    out[...] = r.total[...].astype(bfloat)
    pull, gain_grad, bias_grad = norm_backward(
        r.back[...], values[...], r.gain[norm : norm + 1, :]
    )
    grad[...] = cot[...].astype(full) + pull
    r.gain_grad[...] = gain_grad
    r.bias_grad[...] = bias_grad


def feed_copy(r, stream, which, j):
    width = r.up.shape[1]
    if which == 0:
        return pltpu.make_async_copy(
            r.w_up.at[stream, :, tile_cols(j, width)], r.up.at[j], r.weight_sems.at[0, j]
        )
    return pltpu.make_async_copy(
        r.w_down.at[stream, tile_cols(j, width), :], r.down.at[j], r.weight_sems.at[1, j]
    )


def split_blocks(dims, tile, grad, core):
    slab = dims["slab"]
    for block in range(dims["pages"]):
        tile[lax.rem(block + core, 2), block // 2] = grad[block * slab : (block + 1) * slab]


def exchange(r, j, which):
    page = lax.axis_index("page")
    return pltpu.make_async_remote_copy(
        src_ref=r.tile.at[j, which, 1],
        dst_ref=r.landed.at[j, which],
        send_sem=r.core_send.at[j, which],
        recv_sem=r.core_recv.at[j, which],
        device_id={"page": page + 1 - 2 * lax.rem(page, 2)},
        device_id_type=MESH,
    )


def query_feed_kernel(dims, r):
    bands, slab = dims["bands"], dims["slab"]
    page = lax.axis_index("page")
    greet(band_peers(bands) + [{"page": page + 1 - 2 * lax.rem(page, 2)}])
    for j in range(bands):
        feed_copy(r, 1, 0, j).start()
        feed_copy(r, 1, 1, j).start()
    memo = []
    for s, peer in enumerate(band_peers(bands)):
        copy = pltpu.make_async_remote_copy(
            src_ref=r.hm,
            dst_ref=r.memo.at[s],
            send_sem=r.memo_send.at[s],
            recv_sem=r.memo_recv.at[s],
            device_id=peer,
            device_id_type=MESH,
        )
        copy.start()
        memo.append(copy)
    feed_phase(dims, r, 1, 6, r.y2, r.gy3, r.out, r.grad, 0)
    sum_units(r, bands)
    for copy in memo:
        copy.wait()
    r.finish()


def unit_out(r, j, which):
    slab = r.landed.shape[3]
    if which == 0:
        rows = pl.ds(j * slab, slab)
        places = [(pl.ds(2 * y, 2), r.bags.at[0, y, :, rows]) for y in range(2)]
    else:
        places = [
            (k, r.bags.at[1, j // 2, j % 2, pl.ds(k * slab, slab)])
            for k in range(r.landed.shape[2])
        ]
    return [
        pltpu.make_async_copy(r.landed.at[j, which, part], place, r.core_out.at[j, which, i])
        for i, (part, place) in enumerate(places)
    ]


def sum_units(r, count):
    for j in range(count):
        for which in range(2):
            exchange(r, j, which).wait()
            r.landed[j, which] = r.landed[j, which] + r.tile[j, which, 0]
            for copy in unit_out(r, j, which):
                copy.start()
    for j in range(count):
        for which in range(2):
            for copy in unit_out(r, j, which):
                copy.wait()


RING = 3


def page_place():
    page = lax.axis_index("page")
    core, x, y = lax.rem(page, 2), lax.rem(page // 2, 2), page // 4
    partners = (page + 1 - 2 * core, page + 2 - 4 * x, page + 4 - 8 * y)
    return (core, x, y), [{"page": p} for p in partners]


def remote(src, dst, send, recv, device):
    return pltpu.make_async_remote_copy(
        src_ref=src,
        dst_ref=dst,
        send_sem=send,
        recv_sem=recv,
        device_id=device,
        device_id_type=MESH,
    )


class Loads:
    def __init__(self, sems):
        self.sems, self.used = sems, 0

    def __call__(self, src, dst):
        copy = pltpu.make_async_copy(src, dst, self.sems.at[self.used])
        self.used += 1
        copy.start()
        return copy


class Reducer:
    def __init__(self, dims, r, loads):
        self.dims, self.r, self.loads = dims, r, loads
        (self.core, self.x, self.y), (self.other, self.along_x, self.along_y) = page_place()
        bands = dims["bands"]
        me = lax.axis_index("row")
        self.me = me
        self.next = me + 1 - 2 * lax.rem(me, 2)
        self.far = lax.rem(me + 2, bands)
        self.across = bands - 1 - me
        self.units, self.sent, self.outs, self.stages = 0, {}, {}, {}
        self.total_units = 24
        self.loading = {}


    def unit(self, fill):
        r, u = self.r, self.units
        slot = u % RING
        for copy in self.outs.pop(slot, []):
            copy.wait()
        fill(r.tile.at[slot])
        if u >= RING:
            pl.semaphore_wait(r.core_free, 1)
        self.sent[slot] = self.exchange(slot)
        self.sent[slot].start()
        self.units += 1
        return u

    def exchange(self, slot):
        r = self.r
        return remote(
            r.tile.at[slot, 1],
            r.landed.at[slot],
            r.core_send.at[slot],
            r.core_recv.at[slot],
            self.other,
        )

    def settle(self, u, targets):
        r, slot = self.r, u % RING
        self.sent.pop(slot).wait()
        r.tile[slot, 0] = r.tile[slot, 0] + r.landed[slot]
        if u + RING < self.total_units:
            pl.semaphore_signal(r.core_free, inc=1, device_id=self.other, device_id_type=MESH)
        outs = []
        for i, (part, target) in enumerate(targets):
            copy = pltpu.make_async_copy(r.tile.at[slot, 0, part], target, r.core_out.at[slot, i])
            copy.start()
            outs.append(copy)
        self.outs[slot] = outs

    def slab_targets(self, b, j):
        slab = self.dims["slab"]
        rows = pl.ds(j * slab, slab)
        return [(pl.ds(2 * y, 2), self.bag(b).at[y, :, rows]) for y in range(2)]

    def block_targets(self, b, j):
        slab = self.dims["slab"]
        return [
            (k, self.bag(b).at[j // 2, j % 2, pl.ds(k * slab, slab)])
            for k in range(self.dims["bands"])
        ]

    def flush(self):
        for slot in list(self.outs):
            for copy in self.outs.pop(slot):
                copy.wait()

    def bag(self, b):
        return self.r.query_bags.at[b] if b < 2 else self.r.bags.at[b - 2]


    def start(self, b, stage, parts):
        r, copies = self.r, []
        for i, (src, dst, device) in enumerate(parts):
            at = (b, 2 * stage + i)
            copy = remote(src, dst, r.stage_send.at[at], r.stage_recv.at[at], device)
            copy.start()
            copies.append(copy)
        self.stages[b, stage] = copies

    def halves(self):
        height = self.r.share.shape[0] // 2
        return pl.ds(0, height), pl.ds(height, height)

    def first(self, *bags):
        r = self.r
        top, bottom = self.halves()
        for b in bags:
            bag = self.bag(b)
            self.start(
                b,
                0,
                [
                    (bag.at[:, 1 - self.x, top], r.recv1.at[b, 0], self.along_x),
                    (bag.at[1 - self.y, :, bottom], r.recv1.at[b, 1], self.along_y),
                ],
            )

    def arrived(self, b, stage):
        for copy in self.stages[b, stage]:
            copy.wait()

    def second(self, *bags):
        r = self.r
        top, bottom = self.halves()
        loads = {}
        for b in bags:
            self.arrived(b, 0)
            bag, slot = self.bag(b), b % 2
            loads[b] = [
                self.loads(bag.at[:, self.x, top], r.sums.at[slot, 0]),
                self.loads(bag.at[self.y, :, bottom], r.sums.at[slot, 1]),
                self.loads(r.recv1.at[b], r.came.at[slot]),
            ]
        for b in bags:
            slot = b % 2
            for copy in loads[b]:
                copy.wait()
            r.sums[slot] = r.sums[slot] + r.came[slot]
            self.start(
                b,
                1,
                [
                    (r.sums.at[slot, 0, 1 - self.y], r.recv2.at[b, 0], self.along_y),
                    (r.sums.at[slot, 1, 1 - self.x], r.recv2.at[b, 1], self.along_x),
                ],
            )

    def third(self, *bags):
        r = self.r
        loads = {}
        for b in bags:
            self.arrived(b, 1)
            loads[b] = self.loads(r.recv2.at[b], r.came.at[b % 2, :, 0])
        for b in bags:
            slot = b % 2
            loads[b].wait()
            height = r.share.shape[0] // 2
            r.share[:height] = r.sums[slot, 0, self.y] + r.came[slot, 0, 0]
            r.share[height:] = r.sums[slot, 1, self.x] + r.came[slot, 1, 0]
            self.cut(b)
            self.start(
                b,
                2,
                [
                    (r.pieces.at[slot, self.next], r.recv3.at[b, 0], {"row": self.next}),
                    (r.pieces.at[slot, self.across], r.recv3.at[b, 1], {"row": self.next}),
                ],
            )

    def cut(self, b):
        r, slab, bands = self.r, self.dims["slab"], self.dims["bands"]
        slot = b % 2
        width = r.share.shape[1]
        size = width // bands
        parts = [r.share[k * slab : (k + 1) * slab, :] for k in range(bands)]
        if b in (0, 2):
            made = parts
        elif b in (1, 3):
            made = [
                jnp.concatenate([p[:, z * size : (z + 1) * size] for p in parts], axis=1)
                for z in range(bands)
            ]
        else:
            rest = jnp.concatenate(parts[1:], axis=1)
            made = [
                jnp.concatenate(
                    [
                        parts[0][:, z * size : (z + 1) * size],
                        rest[:, 3 * z * size : 3 * (z + 1) * size],
                    ],
                    axis=1,
                )
                for z in range(bands)
            ]
        for z in range(bands):
            r.pieces[slot, z] = made[z]

    def fourth(self, *bags):
        r = self.r
        loads = {}
        for b in bags:
            self.arrived(b, 2)
            loads[b] = self.loads(r.recv3.at[b], r.came3.at[b % 2])
        for b in bags:
            slot = b % 2
            loads[b].wait()
            r.last[slot, 0] = r.pieces[slot, self.me] + r.came3[slot, 0]
            r.last[slot, 1] = r.pieces[slot, self.far] + r.came3[slot, 1]
            self.start(b, 3, [(r.last.at[slot, 1], r.recv4.at[b], {"row": self.far})])

    def end(self, *bags):
        r = self.r
        loads, outs = {}, []
        for b in bags:
            self.arrived(b, 3)
            loads[b] = self.loads(r.recv4.at[b], r.came4.at[b % 2])
        for b in bags:
            slot = b % 2
            loads[b].wait()
            if ("final", slot) in self.loading:
                self.loading.pop(("final", slot)).wait()
            r.final[slot] = r.last[slot, 0].astype(full) + r.came4[slot].astype(full)
            self.loading["final", slot] = self.loads(r.final.at[slot], r.shares.at[b])

    def finish(self):
        for copy in self.loading.values():
            copy.wait()


def layer_loads(r, loads, layer, arena):
    width = arena.shape[1]
    copies = [
        loads(r.w_qkv.at[layer, :, i * width : (i + 1) * width], arena.at[i]) for i in range(3)
    ]
    return copies + [loads(r.w_out.at[layer], arena.at[3])]


def wait_all(copies):
    for copy in copies:
        copy.wait()


def project_pair_into(kv_ref, into_ref, arena, start, count):
    width = arena.shape[1]
    part = slice(start, start + count)
    kv_ref[part, :width] = dot_nn(into_ref[part, :], arena[1]).astype(bfloat)
    kv_ref[part, width:] = dot_nn(into_ref[part, :], arena[2]).astype(bfloat)


def pair_back(dkv_ref, arena, start, count):
    width = arena.shape[1]
    part = slice(start, start + count)
    return dot_nt(dkv_ref[part, :width], arena[1]) + dot_nt(dkv_ref[part, width:], arena[2])


def scatter_back(r, bands, dkv_ref, arena, count, parts, landing, send, recv):
    me = lax.axis_index("row")
    copies = []
    for s in (2, 1, 3):
        parts[s - 1] = pair_back(dkv_ref, arena, s * count, count).astype(bfloat)
        copy = remote(
            parts.at[s - 1],
            landing.at[s - 1],
            send.at[s - 1],
            recv.at[s - 1],
            {"row": lax.rem(me + bands - s, bands)},
        )
        copy.start()
        copies.append(copy)
    return pair_back(dkv_ref, arena, 0, count), copies


def weight_units(dims, r, red, b, context, low, from_rows, into_rows, dq, dkv):
    width = r.tile.shape[-1]
    sides = [
        lambda: dot_tn(context[...], low[...]),
        lambda: dot_tn(from_rows[...], dq[...]),
        lambda: dot_tn(into_rows[...], dkv[:, :width]),
        lambda: dot_tn(into_rows[...], dkv[:, width:]),
    ]
    units = []
    for j, side in enumerate(sides):
        grad = side().astype(bfloat)
        units.append(red.unit(lambda tile: split_blocks(dims, tile, grad, red.core)))
        if j:
            red.settle(units[j - 1], red.slab_targets(b, j - 1))
    red.settle(units[-1], red.slab_targets(b, 3))


def vec_rows(dims):
    quarters = dims["bands"]
    return 0, 4, 4 + 2 * quarters, 6 + 2 * quarters, 13 + 2 * quarters


def back_kernel(dims, r):
    page_width, bands, rows, tokens = (dims[n] for n in ("page_width", "bands", "rows", "tokens"))
    slab = dims["slab"]
    width = r.f1.shape[1]
    me = lax.axis_index("row")
    loads = Loads(r.load_sems)
    red = Reducer(dims, r, loads)
    greet(band_peers(bands) + [red.other, red.along_x, red.along_y])
    red.first(0, 1)
    row_out, row_up, row_down, row_gain, row_bias = vec_rows(dims)

    weights3 = layer_loads(r, loads, 3, r.att)
    hl_load = loads(r.hl_hbm, r.from_rows)
    memo_load = [
        loads(r.hm_hbm, r.into.at[0:rows]),
        loads(r.memo_hbm, r.into.at[rows : bands * rows]),
    ]
    x1_load = loads(r.x1_hbm, r.f1)
    gx3_load = loads(r.gx3_hbm, r.cot)
    feed_loads = [[feed_copy(r, 0, i, j) for i in range(2)] for j in range(bands)]
    for pair in feed_loads:
        for copy in pair:
            copy.start()
    small = [
        loads(src, dst)
        for src, dst in (
            (r.q2_hbm, r.q2),
            (r.c2_hbm, r.c2),
            (r.log2_hbm, r.log2),
            (r.q1_hbm, r.q1),
            (r.c1_hbm, r.c1),
            (r.log1_hbm, r.log1),
            (r.ha_hbm, r.ha),
            (r.y2_hbm, r.y2),
            (r.y1_hbm, r.y1),
            (r.gy2_hbm, r.gy),
        )
    ]
    r.vec[...] = jnp.zeros_like(r.vec)
    for j in range(bands):
        r.vec[row_up + bands + j : row_up + bands + j + 1, :] = r.up_bias1[
            :, j * width : (j + 1) * width
        ]
    r.vec[row_down + 1 : row_down + 2, :] = r.down_bias1[...]
    r.vec[row_gain + 6 : row_gain + 7, :] = r.gain6[...]
    r.vec[row_bias + 6 : row_bias + 7, :] = r.bias6[...]

    every = slice(None)
    few = slice(0, bands * rows)
    hl_load.wait()
    wait_all(weights3)
    r.q[...] = (dot_nn(r.from_rows[...], r.att[0]) * SCALE).astype(bfloat)
    wait_all(memo_load)
    for s in range(bands):
        project_pair_into(r.kv, r.into, r.att, s * rows, rows)
    bias = read_bias(me, dims, r.scalars)
    r.log[...] = jnp.zeros_like(r.log)
    attend_rows(r.q, r.kv, r.context, r.log, bias, every, few)
    x1_load.wait()
    r.f2[...] = r.f1[...] + (dot_nn(r.context[...], r.att[3]) + r.b_out[3:4, :])

    gx3_load.wait()
    r.low[...] = norm_forward(r.f2[...], r.gain[5:6, :], r.bias[5:6, :])
    r.f3[...] = r.f2[...] + r.b_down[0:1, :]
    r.f4[...] = jnp.zeros_like(r.f4)
    r.vec[row_down : row_down + 1, :] = jnp.sum(r.cot[...].astype(full), axis=0, keepdims=True)
    waiting = []
    for j in range(bands):
        feed_loads[j][0].wait()
        hidden = r.low[...]
        z = dot_nn(hidden, r.up[j]) + r.b_up[0:1, j * width : (j + 1) * width]
        square = z * z
        bend = jnp.tanh(0.7978845608028654 * (z + 0.044715 * (square * z)))
        half = 0.5 * (1.0 + bend)
        slope = half + (0.5 * z) * (1.0 - bend * bend) * (
            0.7978845608028654 * (1.0 + 0.134145 * square)
        )
        active = (z * half).astype(bfloat)
        feed_loads[j][1].wait()
        r.f3[...] += dot_nn(active, r.down[j])
        low_grad = r.cot[...]
        dz = dot_nt(low_grad, r.down[j]) * slope
        r.vec[row_up + j : row_up + j + 1, :] = jnp.sum(dz, axis=0, keepdims=True)
        dz = dz.astype(bfloat)
        r.f4[...] += dot_nt(dz, r.up[j])
        up_grad = dot_tn(hidden, dz).astype(bfloat)
        unit = red.unit(lambda tile: split_blocks(dims, tile, up_grad, red.core))
        waiting.append((unit, red.slab_targets(2, j)))
        down_grad = dot_tn(active, low_grad).astype(bfloat)
        deep = bands * slab

        def fill(tile):
            for side in range(2):
                part = down_grad[side * deep : (side + 1) * deep]
                for k in range(bands):
                    tile[lax.rem(side + red.core, 2), k] = part[k * slab : (k + 1) * slab]

        if len(waiting) > 1:
            red.settle(*waiting.pop(0))
        unit = red.unit(fill)
        waiting.append((unit, red.block_targets(3, j)))
        red.settle(*waiting.pop(0))
        if j == 1:
            red.second(0, 1)
    for item in waiting:
        red.settle(*item)
    red.flush()
    red.first(2, 3)
    weights2 = layer_loads(r, loads, 2, r.up)
    weights1 = layer_loads(r, loads, 1, r.down)
    to_right = {"row": lax.rem(me + 1, bands)}
    moved = dot_tn(r.order[...], r.f3[...].astype(bfloat)).astype(bfloat)
    stay = tokens - SHIFT * page_width
    r.vis_out[tokens - stay :, :] = moved[:stay]
    r.halo_low[...] = moved[stay:]
    halo = remote(
        r.halo_low, r.vis_out.at[: tokens - stay], r.halo_send.at[0], r.halo_recv.at[0], to_right
    )
    halo.start()
    pull, gain5, bias5 = norm_backward(r.f4[...], r.f2[...], r.gain[5:6, :])
    r.vec[row_gain + 5 : row_gain + 6, :] = gain5
    r.vec[row_bias + 5 : row_bias + 6, :] = bias5
    gx2 = r.cot[...].astype(full) + pull
    r.f5[...] = gx2

    low = gx2.astype(bfloat)
    r.low[...] = low
    r.vec[row_out + 3 : row_out + 4, :] = jnp.sum(low.astype(full), axis=0, keepdims=True)
    r.grad[...] = dot_nt(low, r.att[3]).astype(bfloat)
    attend_rows_back(r.q, r.kv, r.context, r.log, r.grad, r.dq, r.dkv, bias, every, few)
    kv_load = loads(r.kv2_hbm, r.kv)
    red.third(0, 1)
    own, memo_sends = scatter_back(
        r, bands, r.dkv, r.att, rows, r.parts_m, r.got_m, r.memo_send, r.memo_recv
    )
    r.own_m[...] = own
    r.f4[...] = dot_nt(r.dq[...], r.att[0])
    weights0 = layer_loads(r, loads, 0, r.att)
    few_dkv, few_into = r.dkv.at[0 : bands * rows], r.into.at[0 : bands * rows]
    weight_units(dims, r, red, 4, r.context, r.low, r.from_rows, few_into, r.dq, few_dkv)
    red.flush()
    red.first(4)
    red.fourth(0, 1)
    red.second(2, 3)
    late = [
        loads(r.hl_all_hbm, r.into),
        loads(r.q0_hbm, r.q),
        loads(r.c0_hbm, r.context),
        loads(r.log0_hbm, r.log),
        loads(r.hv_hbm, r.from_rows),
        loads(r.x1_hbm, r.f1),
        loads(r.x0_hbm, r.cot),
    ]

    wait_all(small)
    wait_all(memo_sends)
    pull, gain4, bias4 = norm_backward(
        r.own_m[...] + sum(r.got_m[s].astype(full) for s in range(bands - 1)),
        r.y2[...],
        r.gain[4:5, :],
    )
    r.vec[row_gain + 4 : row_gain + 5, :] = gain4
    r.vec[row_bias + 4 : row_bias + 5, :] = bias4
    gy = r.gy[...] + pull
    r.gy[...] = gy
    low = gy.astype(bfloat)
    r.low_s[...] = low
    r.vec[row_out + 2 : row_out + 3, :] = jnp.sum(low.astype(full), axis=0, keepdims=True)
    wait_all(weights2)
    r.grad_s[...] = dot_nt(low, r.up[3]).astype(bfloat)
    kv_load.wait()
    attend_rows_back(
        r.q2, r.kv, r.c2, r.log2, r.grad_s, r.dq_s, r.dkv, look_bias(dims, r.scalars), every, every
    )
    kv_load = loads(r.kv1_hbm, r.kv.at[0 : bands * rows])
    own, look_sends = scatter_back(
        r, bands, r.dkv, r.up, tokens, r.parts_l, r.got_l, r.look_send, r.look_recv
    )
    r.f4[...] += own
    pull, gain2, bias2 = norm_backward(dot_nt(r.dq_s[...], r.up[0]), r.y1[...], r.gain[2:3, :])
    r.vec[row_gain + 2 : row_gain + 3, :] = gain2
    r.vec[row_bias + 2 : row_bias + 3, :] = bias2
    r.gy[...] += pull
    red.end(0, 1)
    red.third(2, 3)
    wait_all(late)
    weight_units(dims, r, red, 5, r.c2, r.low_s, r.ha, r.into, r.dq_s, r.dkv)
    hidden_load = loads(r.hs_hbm, r.into.at[0 : bands * rows])
    red.flush()
    red.first(5)
    red.second(4)

    low = r.gy[...].astype(bfloat)
    r.low_s[...] = low
    r.vec[row_out + 1 : row_out + 2, :] = jnp.sum(low.astype(full), axis=0, keepdims=True)
    wait_all(weights1)
    r.grad_s[...] = dot_nt(low, r.down[3]).astype(bfloat)
    kv_load.wait()
    bias = self_bias(me, r.scalars, rows, bands)
    attend_rows_back(r.q1, r.kv, r.c1, r.log1, r.grad_s, r.dq_s, r.dkv, bias, every, few)
    kv_load = loads(r.kv0_hbm, r.kv.at[0:tokens])
    own, self_sends = scatter_back(
        r, bands, r.dkv, r.down, rows, r.parts_m, r.got_s, r.self_send, r.self_recv
    )
    r.own_m[...] = own + dot_nt(r.dq_s[...], r.down[0])
    red.fourth(2, 3)
    hidden_load.wait()
    weight_units(
        dims, r, red, 6, r.c1, r.low_s, r.into.at[0:rows], few_into, r.dq_s, few_dkv
    )
    red.flush()
    red.first(6)
    red.third(4)
    red.second(5)

    wait_all(look_sends)
    pull, gain3, bias3 = norm_backward(
        r.f4[...] + sum(r.got_l[s].astype(full) for s in range(bands - 1)),
        r.f1[...],
        r.gain[3:4, :],
    )
    r.vec[row_gain + 3 : row_gain + 4, :] = gain3
    r.vec[row_bias + 3 : row_bias + 4, :] = bias3
    gx1 = r.f5[...] + pull
    r.f5[...] = gx1
    low = gx1.astype(bfloat)
    r.low[...] = low
    r.vec[row_out : row_out + 1, :] = jnp.sum(low.astype(full), axis=0, keepdims=True)
    wait_all(weights0)
    r.grad[...] = dot_nt(low, r.att[3]).astype(bfloat)
    kv_load.wait()
    size = WIN * WIN
    for w in range(tokens // size):
        part = slice(w * size, (w + 1) * size)
        bias = window_bias(r.scalars, r.region_col, r.region_row, w, page_width)
        attend_rows_back(
            r.q, r.kv, r.context, r.log, r.grad, r.dq, r.dkv, bias, part, part
        )
    dr = pair_back(r.dkv, r.att, 0, tokens) + dot_nt(r.dq[...], r.att[0])
    pull, gain0, bias0 = norm_backward(dr, r.cot[...].astype(full), r.gain[0:1, :])
    r.vec[row_gain : row_gain + 1, :] = gain0
    r.vec[row_bias : row_bias + 1, :] = bias0
    gx0 = r.f5[...] + pull
    high = gx0.astype(bfloat)
    rest = (gx0 - high.astype(full)).astype(bfloat)
    moved = dot_tn(r.order[...], high) + dot_tn(r.order[...], rest)
    r.vis_grad[tokens - stay :, :] = moved[:stay]
    r.f2[: tokens - stay, :] = moved[stay:]
    halo_back = remote(
        r.f2.at[: tokens - stay], r.vis_grad.at[: tokens - stay], r.halo_send.at[1], r.halo_recv.at[1], to_right
    )
    halo_back.start()
    weight_units(
        dims, r, red, 7, r.context, r.low, r.from_rows, r.from_rows, r.dq, r.dkv.at[0:tokens]
    )
    red.flush()
    red.first(7)
    red.end(2, 3)
    red.fourth(4)
    red.third(5)
    red.second(6)

    wait_all(self_sends)
    pull, gain1, bias1 = norm_backward(
        r.own_m[...] + sum(r.got_s[s].astype(full) for s in range(bands - 1)),
        r.y0[...].astype(full),
        r.gain[1:2, :],
    )
    r.query_grad[...] = r.gy[...] + pull
    r.vec[row_gain + 1 : row_gain + 2, :] = gain1
    r.vec[row_bias + 1 : row_bias + 2, :] = bias1

    def swap(i, device):
        copy = remote(r.vec, r.vec_in.at[i], r.vec_send.at[i], r.vec_recv.at[i], device)
        copy.start()
        copy.wait()
        r.vec[...] = r.vec[...] + r.vec_in[i]

    swap(0, red.other)
    red.end(4)
    red.fourth(5)
    swap(1, red.along_x)
    red.second(7)
    swap(2, red.along_y)
    red.third(6)
    swap(3, {"row": red.next})
    red.end(5)
    red.third(7)
    red.fourth(6)
    swap(4, {"row": red.far})
    red.fourth(7)
    red.end(6)
    r.vec_out[...] = r.vec[...]
    red.end(7)
    halo.wait()
    halo_back.wait()
    red.finish()


def shards(
    vis_stream,
    query_stream,
    w_qkv,
    w_out,
    b_out,
    w_up,
    b_up,
    w_down,
    b_down,
    norm_gain,
    norm_bias,
    page_cols,
    query_len,
    prompt_len,
    region_ids,
    vis_cotangent,
    query_cotangent,
):
    band_rows, page_width, width = vis_stream.shape[1:]
    tokens = band_rows * page_width
    rows = query_stream.shape[1]
    bands, pages = lax.axis_size("row"), lax.axis_size("page")
    me = lax.axis_index("row")
    hidden_units = w_up.shape[2]
    slab = width // pages
    dims = dict(
        page_width=page_width,
        bands=bands,
        tokens=tokens,
        rows=rows,
        pages=pages,
        slab=slab,
    )
    scalars = jnp.stack([me, page_cols[0], query_len[0], prompt_len[0]]).astype(jnp.int32)
    scalar = (scalars, SMEM)
    qkv_any, out_any = (w_qkv, ANY), (w_out, ANY)
    log_lanes = full_shape(tokens, PAIR)
    y0, gy3 = query_stream[0], query_cotangent[0]
    across = page_width // WIN
    region = region_ids[0].reshape(band_rows // WIN, WIN, across, WIN)
    region = jnp.swapaxes(region, 1, 2).reshape(-1, WIN * WIN)
    region_col, region_row = region[:, :, None], region[:, None, :]
    order = jnp.asarray(source_order(page_width, band_rows), bfloat)

    given = dict(
        scalars=scalar,
        vis=(vis_stream, VMEM),
        cot=(vis_cotangent, VMEM),
        y0=(y0, VMEM),
        order=(order, VMEM),
        region_col=(region_col, VMEM),
        region_row=(region_row, VMEM),
        gain=(norm_gain, VMEM),
        bias=(norm_bias, VMEM),
        b_out=(b_out, VMEM),
        w_qkv=qkv_any,
        w_out=out_any,
    )
    weight = {}
    for a in range(3):
        weight["wqkv%d" % a] = pltpu.VMEM((width, 3 * width), bfloat)
        weight["wout%d" % a] = pltpu.VMEM((width, width), bfloat)
    pair_sems = pltpu.SemaphoreType.DMA((2,))
    peer_sems = pltpu.SemaphoreType.DMA((bands - 1,))
    front = launch(
        partial(front_kernel, dims),
        given,
        {},
        {},
        dict(
            x0=low_shape(tokens, width),
            hv=low_shape(tokens, width),
            q0=low_shape(tokens, width),
            kv0=low_shape(tokens, 2 * width),
            c0=low_shape(tokens, width),
            log0=log_lanes,
            x1=full_shape(tokens, width),
            gx3=low_shape(tokens, width),
            hs=low_shape(bands, rows, width),
            q1=low_shape(rows, width),
            kv1=low_shape(bands * rows, 2 * width),
            c1=low_shape(rows, width),
            log1=full_shape(rows, PAIR),
            y1=full_shape(rows, width),
            ha=low_shape(rows, width),
            q2=low_shape(rows, width),
            hl=low_shape(bands, tokens, width),
            kv2=low_shape(bands * tokens, 2 * width),
            c2=low_shape(rows, width),
            log2=full_shape(rows, PAIR),
            y2=full_shape(rows, width),
            hm=low_shape(rows, width),
        ),
        dict(
            cells=pltpu.VMEM((tokens, width), full),
            halo=pltpu.VMEM((2, SHIFT, page_width, width), bfloat),
            halo_send=pair_sems,
            halo_recv=pair_sems,
            self_send=peer_sems,
            self_recv=peer_sems,
            look_send=peer_sems,
            look_recv=peer_sems,
            weight_sems=pltpu.SemaphoreType.DMA((6,)),
            **weight,
        ),
        0,
        40 * tokens * width * width,
    )
    bag_shape = (2, 2, 2, bands * slab, width)
    quarter_sems = pltpu.SemaphoreType.DMA((bands, 2))
    feed = launch(
        partial(query_feed_kernel, dims),
        dict(
            y2=(front["y2"], VMEM),
            gy3=(gy3, VMEM),
            hm=(front["hm"], VMEM),
            gain=(norm_gain, VMEM),
            bias=(norm_bias, VMEM),
            b_up=(b_up, VMEM),
            b_down=(b_down, VMEM),
            w_up=(w_up, ANY),
            w_down=(w_down, ANY),
        ),
        {},
        dict(
            out=(low_shape(rows, width), VMEM),
            grad=(full_shape(rows, width), VMEM),
            memo=(low_shape(bands - 1, rows, width), VMEM),
            up_bias=(full_shape(1, hidden_units), VMEM),
            down_bias=(full_shape(1, width), VMEM),
            gain_grad=(full_shape(1, width), VMEM),
            bias_grad=(full_shape(1, width), VMEM),
            bags=(low_shape(*bag_shape), ANY),
        ),
        {},
        dict(
            hidden=pltpu.VMEM((rows, width), bfloat),
            total=pltpu.VMEM((rows, width), full),
            back=pltpu.VMEM((rows, width), full),
            up=pltpu.VMEM((bands, width, width), bfloat),
            down=pltpu.VMEM((bands, width, width), bfloat),
            tile=pltpu.VMEM((bands, 2, 2, pages // 2, slab, width), bfloat),
            landed=pltpu.VMEM((bands, 2, pages // 2, slab, width), bfloat),
            weight_sems=pltpu.SemaphoreType.DMA((2, bands)),
            core_send=quarter_sems,
            core_recv=quarter_sems,
            core_out=pltpu.SemaphoreType.DMA((bands, 2, bands)),
            memo_send=peer_sems,
            memo_recv=peer_sems,
        ),
        1,
        12 * rows * width * hidden_units,
    )
    hbm = {
        "x1_hbm": front["x1"],
        "x0_hbm": front["x0"],
        "gx3_hbm": front["gx3"],
        "hv_hbm": front["hv"],
        "hl_hbm": front["hl"][0],
        "hl_all_hbm": front["hl"].reshape(bands * tokens, width),
        "hs_hbm": front["hs"].reshape(bands * rows, width),
        "ha_hbm": front["ha"],
        "hm_hbm": front["hm"],
        "memo_hbm": feed["memo"].reshape((bands - 1) * rows, width),
        "y1_hbm": front["y1"],
        "y2_hbm": front["y2"],
        "gy2_hbm": feed["grad"],
        "query_bags": feed["bags"],
        "w_qkv": w_qkv,
        "w_out": w_out,
        "w_up": w_up,
        "w_down": w_down,
    }
    for a in range(3):
        for name in ("q", "kv", "c", "log"):
            hbm["%s%d_hbm" % (name, a)] = front["%s%d" % (name, a)]
    near = dict(
        y0=y0,
        order=order,
        region_col=region_col,
        region_row=region_row,
        gain=norm_gain,
        bias=norm_bias,
        b_out=b_out,
        b_up=b_up,
        b_down=b_down,
        up_bias1=feed["up_bias"],
        down_bias1=feed["down_bias"],
        gain6=feed["gain_grad"],
        bias6=feed["bias_grad"],
    )
    height = bands * slab
    halo_rows = SHIFT * page_width
    vec_shape = full_shape(vec_rows(dims)[-1] + 11, width)
    wide = lambda count: pltpu.VMEM((count, width), full)
    narrow = lambda count: pltpu.VMEM((count, width), bfloat)
    dma = pltpu.SemaphoreType.DMA
    scratch = dict(
        att=pltpu.VMEM((4, width, width), bfloat),
        up=pltpu.VMEM((bands, width, width), bfloat),
        down=pltpu.VMEM((bands, width, width), bfloat),
        tile=pltpu.VMEM((RING, 2, pages // 2, slab, width), bfloat),
        landed=pltpu.VMEM((RING, pages // 2, slab, width), bfloat),
        sums=pltpu.VMEM((2, 2, 2, height // 2, width), bfloat),
        came=pltpu.VMEM((2, 2, 2, height // 2, width), bfloat),
        share=narrow(height),
        pieces=pltpu.VMEM((2, bands, slab, width), bfloat),
        last=pltpu.VMEM((2, 2, slab, width), bfloat),
        came3=pltpu.VMEM((2, 2, slab, width), bfloat),
        came4=pltpu.VMEM((2, slab, width), bfloat),
        final=pltpu.VMEM((2, slab, width), full),
        q=narrow(tokens),
        kv=pltpu.VMEM((bands * tokens, 2 * width), bfloat),
        context=narrow(tokens),
        log=pltpu.VMEM((tokens, PAIR), full),
        grad=narrow(tokens),
        dq=narrow(tokens),
        dkv=pltpu.VMEM((bands * tokens, 2 * width), bfloat),
        low=narrow(tokens),
        cot=narrow(tokens),
        from_rows=narrow(tokens),
        into=narrow(bands * tokens),
        f1=wide(tokens),
        f2=wide(tokens),
        f3=wide(tokens),
        f4=wide(tokens),
        f5=wide(tokens),
        q2=narrow(rows),
        c2=narrow(rows),
        q1=narrow(rows),
        c1=narrow(rows),
        log2=pltpu.VMEM((rows, PAIR), full),
        log1=pltpu.VMEM((rows, PAIR), full),
        ha=narrow(rows),
        low_s=narrow(rows),
        grad_s=narrow(rows),
        dq_s=narrow(rows),
        y1=wide(rows),
        y2=wide(rows),
        gy=wide(rows),
        own_m=wide(rows),
        parts_m=pltpu.VMEM((bands - 1, rows, width), bfloat),
        parts_l=pltpu.VMEM((bands - 1, tokens, width), bfloat),
        got_m=pltpu.VMEM((bands - 1, rows, width), bfloat),
        got_l=pltpu.VMEM((bands - 1, tokens, width), bfloat),
        got_s=pltpu.VMEM((bands - 1, rows, width), bfloat),
        halo_low=narrow(halo_rows),
        vec=pltpu.VMEM(vec_shape.shape, full),
        vec_in=pltpu.VMEM((5,) + vec_shape.shape, full),
        load_sems=dma((128,)),
        weight_sems=dma((2, bands)),
        core_send=dma((RING,)),
        core_recv=dma((RING,)),
        core_out=dma((RING, bands)),
        core_free=pltpu.SemaphoreType.REGULAR,
        stage_send=dma((8, 8)),
        stage_recv=dma((8, 8)),
        halo_send=pair_sems,
        halo_recv=pair_sems,
        memo_send=peer_sems,
        memo_recv=peer_sems,
        look_send=peer_sems,
        look_recv=peer_sems,
        self_send=peer_sems,
        self_recv=peer_sems,
        vec_send=dma((5,)),
        vec_recv=dma((5,)),
    )
    result = launch(
        partial(back_kernel, dims),
        dict(scalars=scalar)
        | {n: (v, VMEM) for n, v in near.items()}
        | {n: (v, ANY) for n, v in hbm.items()},
        {},
        dict(
            vis_out=(low_shape(tokens, width), VMEM),
            vis_grad=(full_shape(tokens, width), VMEM),
            query_grad=(full_shape(rows, width), VMEM),
            vec_out=(vec_shape, VMEM),
            shares=(full_shape(8, slab, width), ANY),
            bags=(low_shape(6, 2, 2, height, width), ANY),
            recv1=(low_shape(8, 2, 2, height // 2, width), ANY),
            recv2=(low_shape(8, 2, height // 2, width), ANY),
            recv3=(low_shape(8, 2, slab, width), ANY),
            recv4=(low_shape(8, slab, width), ANY),
        ),
        {},
        scratch,
        2,
        100 * tokens * width * width,
    )

    shares, vec = result["shares"], result["vec_out"]
    column = width // bands
    attention = shares[7:3:-1]
    down = shares[3::-2].reshape(2, slab, bands, column).swapaxes(1, 2)
    page = lax.axis_index("page")
    row_out, row_up, row_down, row_gain, row_bias = vec_rows(dims)
    own = lax.dynamic_slice_in_dim(vec, page * slab, slab, 1)
    hidden = hidden_units // pages
    up_bias = lax.dynamic_slice_in_dim(
        vec[row_up:row_down].reshape(2, hidden_units), page * hidden, hidden, 1
    )
    grid_shape = (1, band_rows, page_width, width)
    return (
        result["vis_out"].reshape(grid_shape),
        feed["out"][None],
        result["vis_grad"].reshape(grid_shape),
        result["query_grad"][None],
        attention[:, :, column:],
        attention[:, :, :column],
        own[row_out:row_up],
        shares[2::-2],
        up_bias,
        down.reshape(2, bands * slab, column),
        own[row_down:row_gain],
        own[row_gain:row_bias],
        own[row_bias : row_bias + 7],
    )


def plain_ring(count, distance):
    return [(i, (i + distance) % count) for i in range(count)]


def plain_flipped(count, bit):
    return [(i, i ^ bit) for i in range(count)]


def plain_mat_dot(left, right):
    return jnp.dot(left, right, preferred_element_type=jnp.float32)


def plain_mat_left(left, right):
    return lax.dot_general(
        left, right, (((0,), (0,)), ((), ())), preferred_element_type=jnp.float32
    )


def plain_mat_right(left, right):
    return lax.dot_general(
        left, right, (((1,), (1,)), ((), ())), preferred_element_type=jnp.float32
    )


def plain_norm_forward(values, gain_row, bias_row):
    average = jnp.mean(values, axis=-1, keepdims=True)
    centred = values - average
    spread = jnp.mean(centred * centred, axis=-1, keepdims=True)
    inverse = lax.rsqrt(spread + norm_eps)
    normal = centred * inverse
    return ((normal * gain_row + bias_row).astype(bfloat), normal, inverse)


def plain_norm_backward(grad_result, normal, inverse, gain_row):
    grad_normal = grad_result * gain_row
    first_mean = jnp.mean(grad_normal, axis=-1, keepdims=True)
    second_mean = jnp.mean(grad_normal * normal, axis=-1, keepdims=True)
    grad_input = inverse * (grad_normal - first_mean - normal * second_mean)
    return (grad_input, jnp.sum(grad_result * normal, axis=0), jnp.sum(grad_result, axis=0))


def plain_to_windows(grid_cells):
    row_count, col_count = (grid_cells.shape[0], grid_cells.shape[1])
    trailing = grid_cells.shape[2:]
    carved = grid_cells.reshape((row_count // WIN, WIN, col_count // WIN, WIN) + trailing)
    return jnp.swapaxes(carved, 1, 2).reshape((-1, WIN * WIN) + trailing)


def plain_from_windows(blocks, row_count, col_count):
    trailing = blocks.shape[2:]
    carved = blocks.reshape((row_count // WIN, col_count // WIN, WIN, WIN) + trailing)
    return jnp.swapaxes(carved, 1, 2).reshape((row_count, col_count) + trailing)


def plain_to_shifted(grid_cells):
    count = lax.axis_size("row")
    arriving = lax.ppermute(grid_cells[:SHIFT], "row", plain_ring(count, -1))
    rolled = jnp.concatenate([grid_cells[SHIFT:], arriving], axis=0)
    return plain_to_windows(jnp.roll(rolled, -SHIFT, axis=1)).reshape(-1, grid_cells.shape[2])


def plain_from_shifted(tokens, row_count, col_count):
    count = lax.axis_size("row")
    cells = plain_from_windows(tokens.reshape(-1, WIN * WIN, tokens.shape[1]), row_count, col_count)
    rolled = jnp.roll(cells, SHIFT, axis=1)
    arriving = lax.ppermute(rolled[row_count - SHIFT :], "row", plain_ring(count, 1))
    return jnp.concatenate([arriving, rolled[: row_count - SHIFT]], axis=0)


def plain_gather_row(values):
    count = lax.axis_size("row")
    parts = [values] + [lax.ppermute(values, "row", plain_ring(count, s)) for s in range(1, count)]
    return jnp.concatenate(parts, axis=0)


def plain_scatter_row(partial_sums):
    count = lax.axis_size("row")
    parts = jnp.split(partial_sums.astype(bfloat), count, axis=0)
    total = jnp.split(partial_sums, count, axis=0)[0]
    for s in range(1, count):
        total = total + lax.ppermute(parts[s], "row", plain_ring(count, -s)).astype(jnp.float32)
    return total


def plain_halve(blocks, bit, slot):
    count = lax.axis_size("page")
    mine = (lax.axis_index("page") // bit) % 2
    kept = lax.dynamic_index_in_dim(blocks, mine, slot, keepdims=False)
    sent = lax.dynamic_index_in_dim(blocks, 1 - mine, slot, keepdims=False)
    return kept + lax.ppermute(sent, "page", plain_flipped(count, bit))


def plain_reduce_matrix(grad):
    pages = lax.axis_size("page")
    rows = lax.axis_size("row")
    bits = []
    while 2 ** len(bits) < pages:
        bits.append(2 ** len(bits))
    height, width = grad.shape
    blocks = grad.astype(bfloat).reshape((2,) * len(bits) + (height // pages, width))
    if bits:
        blocks = plain_halve(blocks, 1, len(bits) - 1)
    left, right = jnp.split(blocks, 2, axis=-1)
    rest = bits[1:]
    for bit in rest:
        left = plain_halve(left, bit, left.ndim - 3)
    for bit in reversed(rest):
        right = plain_halve(right, bit, 0)
    share = jnp.concatenate([left, right], axis=-1)
    me = lax.axis_index("row")
    pieces = share.reshape(share.shape[0], rows, width // rows)
    total = lax.dynamic_index_in_dim(pieces, me, 1, keepdims=False).astype(jnp.float32)
    for s in range(1, rows):
        sent = lax.dynamic_index_in_dim(pieces, (me + s) % rows, 1, keepdims=False)
        total = total + lax.ppermute(sent, "row", plain_ring(rows, s)).astype(jnp.float32)
    return total


def plain_reduce_vectors(stack):
    pages = lax.axis_size("page")
    rows = lax.axis_size("row")
    bit = 1
    while bit < pages:
        stack = stack.reshape(-1, 2, stack.shape[-1])
        stack = plain_halve(stack, bit, 1)
        bit *= 2
    vector = stack.reshape(-1)
    total = vector
    for s in range(1, rows):
        total = total + lax.ppermute(vector, "row", plain_ring(rows, s))
    return total


def plain_split_heads(values):
    return values.reshape(values.shape[0], values.shape[1], -1, HDIM)


def plain_masked_scores(queries, key_rows, allowed):
    scores = jnp.einsum(
        "gqhd,gkhd->ghqk",
        plain_split_heads(queries),
        plain_split_heads(key_rows),
        preferred_element_type=jnp.float32,
    ) * HDIM ** (-0.5)
    return jnp.where(allowed[:, None], scores, masked_score)


def plain_attend_forward(queries, key_rows, value_rows, allowed):
    scores = plain_masked_scores(queries, key_rows, allowed)
    row_max = jnp.max(scores, axis=-1, keepdims=True)
    raised = jnp.exp(scores - row_max)
    row_total = jnp.sum(raised, axis=-1, keepdims=True)
    probs_low = (raised / row_total).astype(bfloat)
    context = jnp.einsum(
        "ghqk,gkhd->gqhd", probs_low, plain_split_heads(value_rows), preferred_element_type=jnp.float32
    )
    return (context.reshape(queries.shape).astype(bfloat), row_max + jnp.log(row_total))


def plain_attend_backward(queries, key_rows, value_rows, allowed, log_total, grad_context):
    probs = jnp.exp(plain_masked_scores(queries, key_rows, allowed) - log_total)
    probs_low = probs.astype(bfloat)
    grad_heads = plain_split_heads(grad_context)
    grad_values = jnp.einsum(
        "ghqk,gqhd->gkhd", probs_low, grad_heads, preferred_element_type=jnp.float32
    )
    grad_probs = jnp.einsum(
        "gqhd,gkhd->ghqk", grad_heads, plain_split_heads(value_rows), preferred_element_type=jnp.float32
    )
    row_delta = jnp.sum(probs * grad_probs, axis=-1, keepdims=True)
    grad_scores = (probs * (grad_probs - row_delta)).astype(bfloat)
    grad_queries = jnp.einsum(
        "ghqk,gkhd->gqhd", grad_scores, plain_split_heads(key_rows), preferred_element_type=jnp.float32
    ) * HDIM ** (-0.5)
    grad_keys = jnp.einsum(
        "ghqk,gqhd->gkhd", grad_scores, plain_split_heads(queries), preferred_element_type=jnp.float32
    ) * HDIM ** (-0.5)
    return (
        grad_queries.reshape(queries.shape).astype(bfloat),
        grad_keys.reshape(key_rows.shape).astype(bfloat),
        grad_values.reshape(value_rows.shape).astype(bfloat),
    )


def plain_project(from_rows, to_rows, weight):
    width = weight.shape[0]
    queries = plain_mat_dot(from_rows, weight[:, :width]).astype(bfloat)
    paired = plain_mat_dot(to_rows, weight[:, width:]).astype(bfloat)
    return (queries, paired[:, :width], paired[:, width:])


def plain_project_back(from_rows, to_rows, weight, dq, dk, dv):
    width = weight.shape[0]
    pair = jnp.concatenate([dk, dv], axis=1)
    weight_grad = jnp.concatenate([plain_mat_left(from_rows, dq), plain_mat_left(to_rows, pair)], axis=1)
    return (weight_grad, plain_mat_right(dq, weight[:, :width]), plain_mat_right(pair, weight[:, width:]))


def plain_output_back(context_low, weight, grad_residual):
    grad_low = grad_residual.astype(bfloat)
    return (
        plain_mat_left(context_low, grad_low),
        jnp.sum(grad_low, axis=0, dtype=jnp.float32),
        plain_mat_right(grad_low, weight).astype(bfloat),
    )


def plain_feed_forward(values, gain_row, bias_row, up_weight, up_bias, down_weight, down_bias):
    hidden, normal, inverse = plain_norm_forward(values, gain_row, bias_row)
    upward = plain_mat_dot(hidden, up_weight) + up_bias
    active = jax.nn.gelu(upward, approximate=True).astype(bfloat)
    return (
        values + (plain_mat_dot(active, down_weight) + down_bias),
        (hidden, normal, inverse, upward, active),
    )


def plain_feed_backward(grad_residual, kept_values, gain_row, up_weight, down_weight):
    hidden, normal, inverse, upward, active = kept_values
    grad_low = grad_residual.astype(bfloat)
    grad_down = plain_mat_left(active, grad_low)
    grad_down_bias = jnp.sum(grad_low, axis=0, dtype=jnp.float32)
    grad_active = plain_mat_right(grad_low, down_weight)
    gelu_pull = jax.vjp(partial(jax.nn.gelu, approximate=True), upward)[1]
    grad_up_low = gelu_pull(grad_active)[0].astype(bfloat)
    grad_up = plain_mat_left(hidden, grad_up_low)
    grad_up_bias = jnp.sum(grad_up_low, axis=0, dtype=jnp.float32)
    grad_input, gain_grad, bias_grad = plain_norm_backward(
        plain_mat_right(grad_up_low, up_weight), normal, inverse, gain_row
    )
    return (
        grad_residual + grad_input,
        (grad_up, grad_up_bias, grad_down, grad_down_bias, gain_grad, bias_grad),
    )


def plain_shards(
    vis_stream,
    query_stream,
    w_qkv,
    w_out,
    b_out,
    w_up,
    b_up,
    w_down,
    b_down,
    norm_gain,
    norm_bias,
    page_cols,
    query_len,
    prompt_len,
    region_ids,
    vis_cotangent,
    query_cotangent,
):
    band_rows, page_width, width = vis_stream.shape[1:]
    tokens = band_rows * page_width
    query_rows = query_stream.shape[1]
    bands = lax.axis_size("row")
    me = lax.axis_index("row")
    pages = lax.axis_size("page")
    x0 = plain_to_shifted(vis_stream[0]).astype(jnp.float32)
    gx3 = plain_to_shifted(vis_cotangent[0]).astype(jnp.float32)
    y0 = query_stream[0].astype(jnp.float32)
    gy3 = query_cotangent[0].astype(jnp.float32)
    col_limit, query_limit, prompt_limit = page_cols[0], query_len[0], prompt_len[0]

    own_positions = me * query_rows + jnp.arange(query_rows)
    all_positions = jnp.concatenate(
        [((me - s) % bands) * query_rows + jnp.arange(query_rows) for s in range(bands)]
    )
    key_live = all_positions < query_limit
    self_allowed = key_live[None, :] & (
        (all_positions[None, :] <= own_positions[:, None]) | (all_positions[None, :] < prompt_limit)
    )
    rolled_live = (jnp.arange(page_width) + SHIFT) % page_width < col_limit
    live_tiles = plain_to_windows(jnp.broadcast_to(rolled_live[None, :], (band_rows, page_width)))
    visual_allowed = jnp.broadcast_to(
        jnp.tile(live_tiles.reshape(-1), bands)[None, :], (query_rows, bands * tokens)
    )
    query_allowed = jnp.broadcast_to(key_live[None, :], (tokens, query_rows * bands))
    region_tiles = plain_to_windows(region_ids[0])
    diagonal = jnp.eye(WIN * WIN, dtype=jnp.bool_)
    window_allowed = (region_tiles[:, :, None] == region_tiles[:, None, :]) & (
        live_tiles[:, None, :] | diagonal[None]
    )
    tile_shape = (tokens // (WIN * WIN), WIN * WIN, width)

    hs, n1, i1 = plain_norm_forward(y0, norm_gain[1], norm_bias[1])
    hs_all = plain_gather_row(hs)
    hv, n0, i0 = plain_norm_forward(x0, norm_gain[0], norm_bias[0])
    qw, kw, vw = (v.reshape(tile_shape) for v in plain_project(hv, hv, w_qkv[0]))
    cw, lw = plain_attend_forward(qw, kw, vw, window_allowed)
    cw = cw.reshape(tokens, width)
    x1 = x0 + (plain_mat_dot(cw, w_out[0]) + b_out[0])
    hl, n3, i3 = plain_norm_forward(x1, norm_gain[3], norm_bias[3])
    hl_all = plain_gather_row(hl)

    qs, ks, vs = plain_project(hs, hs_all, w_qkv[1])
    cs, ls = plain_attend_forward(qs[None], ks[None], vs[None], self_allowed[None])
    cs = cs[0]
    y1 = y0 + (plain_mat_dot(cs, w_out[1]) + b_out[1])
    ha, n2, i2 = plain_norm_forward(y1, norm_gain[2], norm_bias[2])
    qa, kl, vl = plain_project(ha, hl_all, w_qkv[2])
    ca, la = plain_attend_forward(qa[None], kl[None], vl[None], visual_allowed[None])
    ca = ca[0]
    y2 = y1 + (plain_mat_dot(ca, w_out[2]) + b_out[2])
    hm, n4, i4 = plain_norm_forward(y2, norm_gain[4], norm_bias[4])
    hm_all = plain_gather_row(hm)
    y3, kept_query = plain_feed_forward(
        y2, norm_gain[6], norm_bias[6], w_up[1], b_up[1], w_down[1], b_down[1]
    )
    gy2, feed_query = plain_feed_backward(gy3, kept_query, norm_gain[6], w_up[1], w_down[1])
    final_up1 = plain_reduce_matrix(feed_query[0])
    final_down1 = plain_reduce_matrix(feed_query[2])

    qr, km, vm = plain_project(hl, hm_all, w_qkv[3])
    cr, lr = plain_attend_forward(qr[None], km[None], vm[None], query_allowed[None])
    cr = cr[0]
    x2 = x1 + (plain_mat_dot(cr, w_out[3]) + b_out[3])
    x3, kept_vis = plain_feed_forward(
        x2, norm_gain[5], norm_bias[5], w_up[0], b_up[0], w_down[0], b_down[0]
    )
    gx2, feed_vis = plain_feed_backward(gx3, kept_vis, norm_gain[5], w_up[0], w_down[0])
    final_up0 = plain_reduce_matrix(feed_vis[0])
    final_down0 = plain_reduce_matrix(feed_vis[2])

    wout3, bout3, dcr = plain_output_back(cr, w_out[3], gx2)
    dqr, dkm, dvm = plain_attend_backward(
        qr[None], km[None], vm[None], query_allowed[None], lr, dcr[None]
    )
    qkv3, dhl, dhm = plain_project_back(hl, hm_all, w_qkv[3], dqr[0], dkm[0], dvm[0])
    gy_memo, gain4, bias4 = plain_norm_backward(plain_scatter_row(dhm), n4, i4, norm_gain[4])
    gy2 = gy2 + gy_memo
    final_out3 = plain_reduce_matrix(wout3)
    final_qkv3 = plain_reduce_matrix(qkv3)

    wout2, bout2, dca = plain_output_back(ca, w_out[2], gy2)
    dqa, dkl, dvl = plain_attend_backward(
        qa[None], kl[None], vl[None], visual_allowed[None], la, dca[None]
    )
    qkv2, dha, dhl_all = plain_project_back(ha, hl_all, w_qkv[2], dqa[0], dkl[0], dvl[0])
    gy_ask, gain2, bias2 = plain_norm_backward(dha, n2, i2, norm_gain[2])
    gy1 = gy2 + gy_ask
    gx_look, gain3, bias3 = plain_norm_backward(dhl + plain_scatter_row(dhl_all), n3, i3, norm_gain[3])
    gx1 = gx2 + gx_look
    final_out2 = plain_reduce_matrix(wout2)
    final_qkv2 = plain_reduce_matrix(qkv2)

    wout1, bout1, dcs = plain_output_back(cs, w_out[1], gy1)
    dqs, dks, dvs = plain_attend_backward(qs[None], ks[None], vs[None], self_allowed[None], ls, dcs[None])
    qkv1, dhs, dhs_all = plain_project_back(hs, hs_all, w_qkv[1], dqs[0], dks[0], dvs[0])
    gy_self, gain1, bias1 = plain_norm_backward(dhs + plain_scatter_row(dhs_all), n1, i1, norm_gain[1])
    gy0 = gy1 + gy_self
    final_out1 = plain_reduce_matrix(wout1)
    final_qkv1 = plain_reduce_matrix(qkv1)

    wout0, bout0, dcw = plain_output_back(cw, w_out[0], gx1)
    dqw, dkw, dvw = plain_attend_backward(qw, kw, vw, window_allowed, lw, dcw.reshape(tile_shape))
    dqw, dkw, dvw = (v.reshape(tokens, width) for v in (dqw, dkw, dvw))
    qkv0, dr_from, dr_into = plain_project_back(hv, hv, w_qkv[0], dqw, dkw, dvw)
    gx_win, gain0, bias0 = plain_norm_backward(dr_from + dr_into, n0, i0, norm_gain[0])
    gx0 = gx1 + gx_win
    final_out0 = plain_reduce_matrix(wout0)
    final_qkv0 = plain_reduce_matrix(qkv0)

    vectors = [
        jnp.stack([bout0, bout1, bout2, bout3]),
        jnp.stack([feed_vis[1], feed_query[1]]),
        jnp.stack([feed_vis[3], feed_query[3]]),
        jnp.stack([gain0, gain1, gain2, gain3, gain4, feed_vis[4], feed_query[4]]),
        jnp.stack([bias0, bias1, bias2, bias3, bias4, feed_vis[5], feed_query[5]]),
    ]
    blocks = [
        jnp.swapaxes(v.reshape(v.shape[0], pages, -1), 0, 1).reshape(pages, -1) for v in vectors
    ]
    reduced = plain_reduce_vectors(jnp.concatenate(blocks, axis=1))
    finals, start = [], 0
    for v in vectors:
        size = v.size // pages
        finals.append(reduced[start : start + size].reshape(v.shape[0], -1))
        start += size

    return (
        plain_from_shifted(x3.astype(bfloat), band_rows, page_width)[None],
        y3[None].astype(bfloat),
        plain_from_shifted(gx0, band_rows, page_width)[None],
        gy0[None],
        jnp.stack([final_qkv0, final_qkv1, final_qkv2, final_qkv3]),
        jnp.stack([final_out0, final_out1, final_out2, final_out3]),
        finals[0],
        jnp.stack([final_up0, final_up1]),
        finals[1],
        jnp.stack([final_down0, final_down1]),
        finals[2],
        finals[3],
        finals[4],
    )


def solution(mesh):
    planned = mesh.shape["page"] == 8 and mesh.shape["row"] == 4
    return jax.shard_map(
        shards if planned else plain_shards,
        mesh=mesh,
        in_specs=(
            P("page", "row", None, None),
            P("page", "row", None),
            P(),
            P(),
            P(),
            P(),
            P(),
            P(),
            P(),
            P(),
            P(),
            P("page"),
            P("page"),
            P("page"),
            P("page", "row", None),
            P("page", "row", None, None),
            P("page", "row", None),
        ),
        out_specs=(
            P("page", "row", None, None),
            P("page", "row", None),
            P("page", "row", None, None),
            P("page", "row", None),
            P(None, "page", "row"),
            P(None, "page", "row"),
            P(None, "page"),
            P(None, "page", "row"),
            P(None, "page"),
            P(None, "page", "row"),
            P(None, "page"),
            P(None, "page"),
            P(None, "page"),
        ),
        check_vma=False,
    )
```

```python
from functools import partial

import jax
import jax.numpy as jnp
import numpy as np
from jax import lax
from jax.experimental import pallas as pl
from jax.experimental.pallas import tpu as pltpu
from jax.sharding import PartitionSpec as P

HDIM = 64
WIN = 12
SHIFT = 6
PAIR = 2 * HDIM
SCALE = HDIM ** (-0.5)

masked_score = -1e30
norm_eps = 1e-05
bfloat = jnp.bfloat16
full = jnp.float32
ANY = pl.BlockSpec(memory_space=pl.ANY)
VMEM = pl.BlockSpec(memory_space=pltpu.VMEM)
SMEM = pl.BlockSpec(memory_space=pltpu.SMEM)
MESH = pl.DeviceIdType.MESH


def ring(count, distance):
    return [(i, (i + distance) % count) for i in range(count)]


def flipped(count, bit):
    return [(i, i ^ bit) for i in range(count)]


def dot_nn(left, right):
    return jnp.dot(left, right, preferred_element_type=full)


def dot_nt(left, right):
    return lax.dot_general(left, right, (((1,), (1,)), ((), ())), preferred_element_type=full)


def dot_tn(left, right):
    return lax.dot_general(left, right, (((0,), (0,)), ((), ())), preferred_element_type=full)


def normalise(values):
    centred = values - jnp.mean(values, axis=-1, keepdims=True)
    spread = jnp.mean(centred * centred, axis=-1, keepdims=True)
    inverse = lax.rsqrt(spread + norm_eps)
    return centred * inverse, inverse


def norm_forward(values, gain_row, bias_row):
    return (normalise(values)[0] * gain_row + bias_row).astype(bfloat)


def norm_backward(grad, values, gain_row):
    normal, inverse = normalise(values)
    grad_normal = grad * gain_row
    first = jnp.mean(grad_normal, axis=-1, keepdims=True)
    second = jnp.mean(grad_normal * normal, axis=-1, keepdims=True)
    return (
        inverse * (grad_normal - first - normal * second),
        jnp.sum(grad * normal, axis=0, keepdims=True),
        jnp.sum(grad, axis=0, keepdims=True),
    )


def tile_cols(index, size):
    return pl.ds(pl.multiple_of(index * size, size), size)


def matmul_into(out_ref, left_ref, weight_ref, size):
    def step(i, _):
        cols = tile_cols(i, size)
        out_ref[:, cols] = dot_nn(left_ref[...], weight_ref[:, cols]).astype(out_ref.dtype)
        return 0

    lax.fori_loop(0, weight_ref.shape[1] // size, step, 0)


def two_heads(values):
    lane = lax.broadcasted_iota(jnp.int32, values.shape, 1)
    zero = jnp.zeros_like(values)
    return jnp.concatenate(
        [jnp.where(lane < HDIM, values, zero), jnp.where(lane < HDIM, zero, values)], axis=0
    )


def one_pair(stacked):
    count = stacked.shape[0] // 2
    lane = lax.broadcasted_iota(jnp.int32, (count, PAIR), 1)
    return jnp.where(lane < HDIM, stacked[:count], stacked[count:])


def attend_pair(queries, key_rows, value_rows, bias):
    scores = dot_nt(two_heads(queries), key_rows) + bias
    top = jnp.max(scores, axis=-1, keepdims=True)
    raised = jnp.exp(scores - top)
    total = jnp.sum(raised, axis=-1, keepdims=True)
    context = dot_nn(raised.astype(bfloat), value_rows) / total
    return one_pair(context).astype(bfloat), top + jnp.log(total)


def attend_pair_back(queries, key_rows, value_rows, bias, log_total, context, grad_context):
    both = two_heads(queries)
    grad_both = two_heads(grad_context)
    probs = jnp.exp(dot_nt(both, key_rows) + bias - log_total)
    grad_probs = dot_nt(grad_both, value_rows)
    delta = jnp.sum(
        grad_both.astype(full) * jnp.concatenate([context, context], axis=0).astype(full),
        axis=-1,
        keepdims=True,
    )
    grad_scores = (probs * (grad_probs - delta)).astype(bfloat)
    grad_queries = one_pair(dot_nn(grad_scores, key_rows)) * SCALE
    grad_keys = dot_tn(grad_scores, both)
    grad_values = dot_tn(probs.astype(bfloat), grad_both)
    return grad_queries.astype(bfloat), grad_keys.astype(bfloat), grad_values.astype(bfloat)


def put_logs(log_ref, rows, pair, log_total):
    count = log_total.shape[0] // 2
    lane = lax.broadcasted_iota(jnp.int32, (count, PAIR), 1)
    kept = log_ref[rows, :]
    kept = jnp.where(lane == 2 * pair, log_total[:count], kept)
    log_ref[rows, :] = jnp.where(lane == 2 * pair + 1, log_total[count:], kept)


def take_logs(log_ref, rows, pair):
    kept = log_ref[rows, :]
    lane = lax.broadcasted_iota(jnp.int32, kept.shape, 1)
    parts = [
        jnp.sum(jnp.where(lane == 2 * pair + i, kept, 0.0), axis=-1, keepdims=True)
        for i in range(2)
    ]
    return jnp.concatenate(parts, axis=0)


def in_parts(step, count, between):
    parts = len(between) + 1
    for i in range(parts):
        lax.fori_loop(count * i // parts, count * (i + 1) // parts, step, 0)
        if i < len(between):
            between[i]()


def attend_rows(q_ref, kv_ref, context_ref, log_ref, bias, rows, keys, between=()):
    width = q_ref.shape[1]
    key_start = kv_ref.shape[1] - 2 * width

    def step(pair, _):
        cols = tile_cols(pair, PAIR)
        key_cols = pl.ds(pl.multiple_of(key_start + pair * PAIR, PAIR), PAIR)
        value_cols = pl.ds(pl.multiple_of(key_start + width + pair * PAIR, PAIR), PAIR)
        context, log_total = attend_pair(
            q_ref[rows, cols], kv_ref[keys, key_cols], kv_ref[keys, value_cols], bias
        )
        context_ref[rows, cols] = context
        put_logs(log_ref, rows, pair, log_total)
        return 0

    in_parts(step, width // PAIR, between)


def attend_rows_back(
    q_ref, kv_ref, context_ref, log_ref, grad_ref, dq_ref, dkv_ref, bias, rows, keys, between=()
):
    width = q_ref.shape[1]
    key_start = kv_ref.shape[1] - 2 * width
    grad_start = dkv_ref.shape[1] - 2 * width

    def step(pair, _):
        cols = tile_cols(pair, PAIR)
        key_cols = pl.ds(pl.multiple_of(key_start + pair * PAIR, PAIR), PAIR)
        value_cols = pl.ds(pl.multiple_of(key_start + width + pair * PAIR, PAIR), PAIR)
        dq, dk, dv = attend_pair_back(
            q_ref[rows, cols],
            kv_ref[keys, key_cols],
            kv_ref[keys, value_cols],
            bias,
            take_logs(log_ref, rows, pair),
            context_ref[rows, cols],
            grad_ref[rows, cols],
        )
        dq_ref[rows, cols] = dq
        dkv_ref[keys, pl.ds(pl.multiple_of(grad_start + pair * PAIR, PAIR), PAIR)] = dk
        dkv_ref[keys, pl.ds(pl.multiple_of(grad_start + width + pair * PAIR, PAIR), PAIR)] = dv
        return 0

    in_parts(step, width // PAIR, between)


def allowed_bias(allowed):
    return jnp.where(allowed, 0.0, masked_score).astype(full)


def key_positions(me, bands, rows):
    lane = lax.broadcasted_iota(jnp.int32, (1, bands * rows), 1)
    part = sum((lane >= s * rows).astype(jnp.int32) for s in range(1, bands))
    band = lax.rem(me - part + bands, bands)
    return band * rows + lane - part * rows


def window_live(first, count, scalars, page_width):
    token = first + lax.broadcasted_iota(jnp.int32, (1, count), 1)
    window = lax.div(token, WIN * WIN)
    column = lax.rem(token, WIN) + WIN * lax.rem(window, page_width // WIN)
    return lax.rem(column + SHIFT, page_width) < scalars[1]


def copies_in(pairs, sems):
    copies = [pltpu.make_async_copy(src, dst, sems.at[i]) for i, (src, dst) in enumerate(pairs)]
    for copy in copies:
        copy.start()
    return copies


def low_shape(*shape):
    return jax.ShapeDtypeStruct(shape, bfloat)


def full_shape(*shape):
    return jax.ShapeDtypeStruct(shape, full)


def source_order(page_width, band_rows):
    tokens = band_rows * page_width
    token = np.arange(tokens)
    across = page_width // WIN
    window, inside = token // (WIN * WIN), token % (WIN * WIN)
    row = window // across * WIN + inside // WIN
    column = window % across * WIN + inside % WIN
    source = row * page_width + (column + SHIFT) % page_width
    order = np.zeros((tokens, tokens), np.float32)
    order[token, source] = 1.0
    return order


def fill_shifted(own_ref, arriving_ref, rows_ref):
    band_rows, width = own_ref.shape[1], own_ref.shape[2]
    for i in range(band_rows - SHIFT):
        rows_ref[i * width : (i + 1) * width, :] = own_ref[0, i + SHIFT].astype(full)
    for i in range(SHIFT):
        j = band_rows - SHIFT + i
        rows_ref[j * width : (j + 1) * width, :] = arriving_ref[i].astype(full)


def page_scalars(r):
    return None, r.page_cols[0], r.query_len[0], r.prompt_len[0]


def region_vectors(region_ref, w, page_width):
    size = WIN * WIN
    labels = region_ref[0].astype(full)
    band_rows = labels.shape[0]
    across = page_width // WIN
    first_row, first_col = w // across * WIN, w % across * WIN

    def at(shape, token_dim, start, divide):
        token = lax.broadcasted_iota(jnp.int32, shape, token_dim)
        place = lax.div(token, WIN) if divide else lax.rem(token, WIN)
        return place + start == lax.broadcasted_iota(jnp.int32, shape, 1 - token_dim)

    rows = at((size, band_rows), 0, first_row, True).astype(full)
    columns = at((size, page_width), 0, first_col, False)
    column = jnp.sum(jnp.where(columns, dot_nn(rows, labels), 0.0), axis=1, keepdims=True)
    rows = at((band_rows, size), 1, first_row, True).astype(full)
    columns = at((page_width, size), 1, first_col, False)
    row = jnp.sum(jnp.where(columns, dot_tn(labels, rows), 0.0), axis=0, keepdims=True)
    return column, row


def window_bias(scalars, region_ref, w, page_width):
    size = WIN * WIN
    live = window_live(w * size, size, scalars, page_width)
    own = lax.broadcasted_iota(jnp.int32, (size, size), 0)
    other = lax.broadcasted_iota(jnp.int32, (size, size), 1)
    column, row = region_vectors(region_ref, w, page_width)
    bias = allowed_bias((column == row) & ((own == other) | live))
    return jnp.concatenate([bias, bias], axis=0)


def self_bias(me, scalars, rows, bands):
    position = key_positions(me, bands, rows)
    own = me * rows + lax.broadcasted_iota(jnp.int32, (rows, 1), 0)
    bias = allowed_bias(
        (position < scalars[2]) & ((position <= own) | (position < scalars[3]))
    )
    return jnp.concatenate([bias, bias], axis=0)


def look_bias(dims, scalars):
    tokens, bands, page_width = dims["tokens"], dims["bands"], dims["page_width"]
    live = window_live(0, tokens, scalars, page_width)
    return jnp.concatenate([allowed_bias(live)] * bands, axis=1)


def read_bias(me, dims, scalars):
    return allowed_bias(key_positions(me, dims["bands"], dims["rows"]) < scalars[2])


class Kernel:
    def __init__(self, refs, hbm, sems):
        self.__dict__.update(refs)
        self.hbm, self.sems = hbm, sems
        self.coming, self.going = {}, []

    def fetch(self, *names):
        for name in names:
            copy = pltpu.make_async_copy(
                self.hbm[name], getattr(self, name), self.sems[name]
            )
            copy.start()
            self.coming[name] = copy

    def ready(self, *names):
        for name in names:
            self.coming.pop(name).wait()

    def save(self, *names):
        for name in names:
            copy = pltpu.make_async_copy(
                getattr(self, name), self.hbm[name], self.sems[name]
            )
            copy.start()
            self.going.append(copy)

    def finish(self):
        for copy in self.going:
            copy.wait()


def launch(body, given, staged, made, kept, scratch, collective, flops):
    sources = list(given) + list(staged)
    results = list(made) + list(kept)
    moved = list(staged) + list(kept)
    arrays = [given[n][0] for n in given] + [staged[n] for n in staged]
    stages = {n: pltpu.VMEM(staged[n].shape, staged[n].dtype) for n in staged}
    stages.update({n: pltpu.VMEM(kept[n].shape, kept[n].dtype) for n in kept})

    def inner(*refs):
        first, second = len(sources), len(sources) + len(results)
        outer = dict(zip(sources, refs[:first])) | dict(zip(results, refs[first:second]))
        inside = dict(zip(list(stages) + list(scratch), refs[second:-1]))
        sems = {n: refs[-1].at[i] for i, n in enumerate(moved)}
        body(Kernel(outer | inside, {n: outer[n] for n in moved}, sems))

    outs = pl.pallas_call(
        inner,
        out_shape=[made[n][0] for n in made] + [kept[n] for n in kept],
        in_specs=[given[n][1] for n in given] + [ANY] * len(staged),
        out_specs=[made[n][1] for n in made] + [ANY] * len(kept),
        scratch_shapes=list(stages.values())
        + list(scratch.values())
        + [pltpu.SemaphoreType.DMA((max(len(moved), 1),))],
        compiler_params=pltpu.CompilerParams(
            vmem_limit_bytes=62 * 2**20, collective_id=collective, has_side_effects=True
        ),
        cost_estimate=pl.CostEstimate(flops=flops, bytes_accessed=2**24, transcendentals=0),
    )(*arrays)
    return dict(zip(results, outs))


def hand_over(arrays):
    count = len(arrays)
    shapes = [a.shape if a.ndim < 4 else (a.shape[0], a.shape[3], a.shape[1] * a.shape[2]) for a in arrays]

    def body(*refs):
        for source, target in zip(refs[:count], refs[count:]):
            if source.shape == target.shape:
                target[...] = source[...]
            else:
                for k in range(source.shape[0]):
                    target[k] = source[k].reshape(target.shape[2], target.shape[1]).T

    return pl.pallas_call(
        body,
        out_shape=[jax.ShapeDtypeStruct(s, a.dtype) for s, a in zip(shapes, arrays)],
        in_specs=[VMEM] * count,
        out_specs=[VMEM] * count,
        compiler_params=pltpu.CompilerParams(vmem_limit_bytes=62 * 2**20),
    )(*arrays)


def greet(devices):
    barrier = pltpu.get_barrier_semaphore()
    for device in devices:
        pl.semaphore_signal(barrier, inc=1, device_id=device, device_id_type=MESH)
    pl.semaphore_wait(barrier, len(devices))


def band_peers(bands):
    me = lax.axis_index("row")
    return [{"row": lax.rem(me + s, bands)} for s in range(1, bands)]


def gather_start(ref, bands, send, recv):
    copies = []
    for s, peer in enumerate(band_peers(bands), 1):
        copy = pltpu.make_async_remote_copy(
            src_ref=ref.at[0],
            dst_ref=ref.at[s],
            send_sem=send.at[s - 1],
            recv_sem=recv.at[s - 1],
            device_id=peer,
            device_id_type=MESH,
        )
        copy.start()
        copies.append(copy)
    return copies


def front_kernel(dims, r):
    page_width, bands, rows, tokens = (dims[n] for n in ("page_width", "bands", "rows", "tokens"))
    width = r.y0.shape[1]
    me = lax.axis_index("row")
    scalars = page_scalars(r)
    greet(band_peers(bands))
    loads = {}
    for a in range(3):
        for i, (name, ref) in enumerate((("wqkv%d", r.w_qkv), ("wout%d", r.w_out))):
            copy = pltpu.make_async_copy(
                ref.at[a], getattr(r, name % a), r.weight_sems.at[2 * a + i]
            )
            copy.start()
            loads[name % a] = copy
    above = {"row": lax.rem(me + bands - 1, bands)}
    halos = []
    for i, ref in enumerate((r.vis, r.cot)):
        halo = pltpu.make_async_remote_copy(
            src_ref=ref.at[0, 0:SHIFT],
            dst_ref=r.halo.at[i],
            send_sem=r.halo_send.at[i],
            recv_sem=r.halo_recv.at[i],
            device_id=above,
            device_id_type=MESH,
        )
        halo.start()
        halos.append(halo)
    r.hs[0] = norm_forward(r.y0[...].astype(full), r.gain[1:2, :], r.bias[1:2, :])
    self_copies = gather_start(r.hs, bands, r.self_send, r.self_recv)

    r.log0[...] = jnp.zeros_like(r.log0)
    r.log1[...] = jnp.zeros_like(r.log1)
    r.log2[...] = jnp.zeros_like(r.log2)
    halos[0].wait()
    fill_shifted(r.vis, r.halo.at[0], r.cells)
    x0 = dot_nn(r.order[...], r.cells[...].astype(bfloat))
    r.x0[...] = x0.astype(bfloat)
    r.hv[...] = norm_forward(x0, r.gain[0:1, :], r.bias[0:1, :])
    r.save("x0", "hv")
    loads["wqkv0"].wait()
    r.q0[...] = (dot_nn(r.hv[...], r.wqkv0[:, :width]) * SCALE).astype(bfloat)
    matmul_into(r.kv0, r.hv, r.wqkv0.at[:, width:], width)
    r.save("q0", "kv0")
    size = WIN * WIN
    for w in range(tokens // size):
        part = slice(w * size, (w + 1) * size)
        bias = window_bias(scalars, r.region, w, page_width)
        attend_rows(r.q0, r.kv0, r.c0, r.log0, bias, part, part)
    r.save("c0", "log0")
    loads["wout0"].wait()
    x1 = r.x0[...].astype(full) + (dot_nn(r.c0[...], r.wout0[...]) + r.b_out[0:1, :])
    r.x1[...] = x1
    r.hl[0] = norm_forward(x1, r.gain[3:4, :], r.bias[3:4, :])
    look_copies = gather_start(r.hl, bands, r.look_send, r.look_recv)
    r.save("x1")

    halos[1].wait()
    fill_shifted(r.cot, r.halo.at[1], r.cells)
    r.gx3[...] = dot_nn(r.order[...], r.cells[...].astype(bfloat)).astype(bfloat)
    r.save("gx3")
    loads["wqkv1"].wait()
    r.q1[...] = (dot_nn(r.hs[0], r.wqkv1[:, :width]) * SCALE).astype(bfloat)
    for copy in self_copies:
        copy.wait_recv()

    def project_self(s, _):
        part = pl.ds(pl.multiple_of(s * rows, rows), rows)
        r.kv1[part, :] = dot_nn(r.hs[s], r.wqkv1[:, width:]).astype(bfloat)
        return 0

    lax.fori_loop(0, bands, project_self, 0)
    r.save("hs", "q1", "kv1")
    bias = self_bias(me, scalars, rows, bands)
    attend_rows(r.q1, r.kv1, r.c1, r.log1, bias, slice(None), slice(None))
    r.save("c1", "log1")
    loads["wout1"].wait()
    y1 = r.y0[...].astype(full) + (dot_nn(r.c1[...], r.wout1[...]) + r.b_out[1:2, :])
    r.y1[...] = y1
    r.ha[...] = norm_forward(y1, r.gain[2:3, :], r.bias[2:3, :])
    loads["wqkv2"].wait()
    r.q2[...] = (dot_nn(r.ha[...], r.wqkv2[:, :width]) * SCALE).astype(bfloat)
    r.save("y1", "ha", "q2")

    for s in range(bands):
        if s:
            look_copies[s - 1].wait_recv()
        part = slice(s * tokens, (s + 1) * tokens)
        matmul_into(r.kv2.at[part], r.hl.at[s], r.wqkv2.at[:, width:], width)
    r.save("hl", "kv2")
    attend_rows(r.q2, r.kv2, r.c2, r.log2, look_bias(dims, scalars), slice(None), slice(None))
    loads["wout2"].wait()
    y2 = r.y1[...] + (dot_nn(r.c2[...], r.wout2[...]) + r.b_out[2:3, :])
    r.y2[...] = y2
    r.hm[...] = norm_forward(y2, r.gain[4:5, :], r.bias[4:5, :])
    r.save("c2", "log2", "y2", "hm")
    for copy in self_copies + look_copies:
        copy.wait_send()
    r.finish()


def split_blocks(dims, tile, grad, core):
    slab = dims["slab"]
    for block in range(dims["pages"]):
        tile[lax.rem(block + core, 2), block // 2] = grad[block * slab : (block + 1) * slab]


RING = 3


def page_place():
    page = lax.axis_index("page")
    core, x, y = lax.rem(page, 2), lax.rem(page // 2, 2), page // 4
    partners = (page + 1 - 2 * core, page + 2 - 4 * x, page + 4 - 8 * y)
    return (core, x, y), [{"page": p} for p in partners]


def remote(src, dst, send, recv, device):
    return pltpu.make_async_remote_copy(
        src_ref=src,
        dst_ref=dst,
        send_sem=send,
        recv_sem=recv,
        device_id=device,
        device_id_type=MESH,
    )


class Loads:
    def __init__(self, sems):
        self.sems, self.used = sems, 0

    def __call__(self, src, dst):
        copy = pltpu.make_async_copy(src, dst, self.sems.at[self.used])
        self.used += 1
        copy.start()
        return copy


class Reducer:
    def __init__(self, dims, r, loads):
        self.dims, self.r, self.loads = dims, r, loads
        (self.core, self.x, self.y), (self.other, self.along_x, self.along_y) = page_place()
        bands = dims["bands"]
        me = lax.axis_index("row")
        self.me = me
        self.next = me + 1 - 2 * lax.rem(me, 2)
        self.far = lax.rem(me + 2, bands)
        self.across = bands - 1 - me
        self.units, self.sent, self.outs, self.stages = 0, {}, {}, {}
        self.total_units = 32
        self.loading = {}


    def unit(self, fill):
        r, u = self.r, self.units
        slot = u % RING
        for copy in self.outs.pop(slot, []):
            copy.wait()
        fill(r.tile.at[slot])
        if u >= RING:
            pl.semaphore_wait(r.core_free, 1)
        self.sent[slot] = self.exchange(slot)
        self.sent[slot].start()
        self.units += 1
        return u

    def exchange(self, slot):
        r = self.r
        return remote(
            r.tile.at[slot, 1],
            r.landed.at[slot],
            r.core_send.at[slot],
            r.core_recv.at[slot],
            self.other,
        )

    def settle(self, u, targets):
        r, slot = self.r, u % RING
        self.sent.pop(slot).wait()
        r.tile[slot, 0] = r.tile[slot, 0] + r.landed[slot]
        if u + RING < self.total_units:
            pl.semaphore_signal(r.core_free, inc=1, device_id=self.other, device_id_type=MESH)
        outs = []
        for i, (part, target) in enumerate(targets):
            copy = pltpu.make_async_copy(r.tile.at[slot, 0, part], target, r.core_out.at[slot, i])
            copy.start()
            outs.append(copy)
        self.outs[slot] = outs

    def slab_targets(self, b, j):
        slab = self.dims["slab"]
        rows = pl.ds(j * slab, slab)
        return [(pl.ds(2 * y, 2), self.r.bags.at[b].at[y, :, rows]) for y in range(2)]

    def block_targets(self, b, j):
        slab = self.dims["slab"]
        return [
            (k, self.r.bags.at[b].at[j // 2, j % 2, pl.ds(k * slab, slab)])
            for k in range(self.dims["bands"])
        ]

    def flush(self, units=None):
        for slot in list(self.outs):
            if units is None or slot in [u % RING for u in units]:
                for copy in self.outs.pop(slot):
                    copy.wait()


    def start(self, b, stage, parts, which=(0, 1)):
        r = self.r
        for i, (src, dst, device) in enumerate(parts):
            if i in which:
                at = (b, 2 * stage + i)
                copy = remote(src, dst, r.stage_send.at[at], r.stage_recv.at[at], device)
                copy.start()
                self.stages.setdefault((b, stage), []).append(copy)

    def arrived(self, b, stage):
        for copy in self.stages.pop((b, stage)):
            copy.wait()

    def halves(self):
        height = self.r.recv1.shape[3]
        return pl.ds(0, height), pl.ds(height, height)

    def landing1(self, b, half):
        r = self.r
        if b < 7:
            return r.recv1.at[b, half]
        return r.arena.at[2 * half : 2 * half + 2, : r.recv1.shape[3]]

    def landing2(self, b, half):
        r = self.r
        height = r.recv1.shape[3]
        if b < 7:
            return r.recv2.at[b, half]
        return r.arena.at[half, height : 2 * height]

    def came2(self, b):
        if b < 7:
            return [self.r.came.at[b % 2, half, 0] for half in range(2)]
        return [self.landing2(b, half) for half in range(2)]

    def load_own(self, b):
        r, slot = self.r, b % 2
        top, bottom = self.halves()
        bag = r.bags.at[b]
        self.loading[b] = [
            self.loads(bag.at[:, self.x, top], r.sums.at[slot, 0]),
            self.loads(bag.at[self.y, :, bottom], r.sums.at[slot, 1]),
        ]

    def first(self, b, half=None):
        r = self.r
        top, bottom = self.halves()
        bag = r.bags.at[b]
        parts = [
            (bag.at[:, 1 - self.x, top], self.landing1(b, 0), self.along_x),
            (bag.at[1 - self.y, :, bottom], self.landing1(b, 1), self.along_y),
        ]
        self.start(b, 0, parts, [0, 1] if half is None else [half])

    def load_second(self, *bags):
        r = self.r
        for b in bags:
            if b not in self.loading:
                self.load_own(b)
            self.arrived(b, 0)
            if b < 7:
                self.loading[b].append(self.loads(r.recv1.at[b], r.came.at[b % 2]))

    def second(self, *bags):
        r = self.r
        for b in bags:
            slot = b % 2
            wait_all(self.loading.pop(b))
            if b < 7:
                r.sums[slot] = r.sums[slot] + r.came[slot]
            else:
                for half in range(2):
                    r.sums[slot, half] = r.sums[slot, half] + self.landing1(b, half)[...]
            self.start(
                b,
                1,
                [
                    (r.sums.at[slot, 0, 1 - self.y], self.landing2(b, 0), self.along_y),
                    (r.sums.at[slot, 1, 1 - self.x], self.landing2(b, 1), self.along_x),
                ],
            )

    def load_third(self, *bags):
        r = self.r
        for b in bags:
            self.arrived(b, 1)
            self.loading[b] = []
            if b < 7:
                self.loading[b].append(self.loads(r.recv2.at[b], r.came.at[b % 2, :, 0]))

    def third(self, *bags):
        r = self.r
        for b in bags:
            slot = b % 2
            wait_all(self.loading.pop(b))
            top, bottom = self.came2(b)
            self.cut(b, r.sums[slot, 0, self.y] + top[...], r.sums[slot, 1, self.x] + bottom[...])
            self.start(
                b,
                2,
                [
                    (r.pieces.at[b % 4, self.next], r.recv3.at[b, 0], {"row": self.next}),
                    (r.pieces.at[b % 4, self.across], r.recv3.at[b, 1], {"row": self.next}),
                ],
            )

    def cut(self, b, top, bottom):
        r, slab, bands = self.r, self.dims["slab"], self.dims["bands"]
        width = top.shape[1]
        size = width // bands
        parts = [half[k * slab : (k + 1) * slab] for half in (top, bottom) for k in range(2)]
        if b in (0, 2):
            made = parts
        elif b in (1, 3):
            made = [
                jnp.concatenate([p[:, z * size : (z + 1) * size] for p in parts], axis=1)
                for z in range(bands)
            ]
        else:
            rest = jnp.concatenate(parts[1:], axis=1)
            made = [
                jnp.concatenate(
                    [
                        parts[0][:, z * size : (z + 1) * size],
                        rest[:, 3 * z * size : 3 * (z + 1) * size],
                    ],
                    axis=1,
                )
                for z in range(bands)
            ]
        for z in range(bands):
            r.pieces[b % 4, z] = made[z]

    def fourth(self, *bags):
        r = self.r
        for b in bags:
            slot = b % 2
            self.arrived(b, 2)
            r.last[slot, 0] = r.pieces[b % 4, self.me] + r.recv3[b, 0]
            r.last[slot, 1] = r.pieces[b % 4, self.far] + r.recv3[b, 1]
            self.start(b, 3, [(r.last.at[slot, 1], r.recv4.at[b], {"row": self.far})], [0])

    def store(self, name, target, value):
        scratch = getattr(self.r, name)
        for copy in self.loading.pop(name, ()):
            copy.wait()
        scratch[...] = value
        self.loading[name] = [self.loads(scratch, target)]

    def end(self, *bags):
        r, slab, bands = self.r, self.dims["slab"], self.dims["bands"]
        for b in bags:
            self.arrived(b, 3)
            total = r.last[b % 2, 0].astype(full) + r.recv4[b].astype(full)
            size = total.shape[1] // bands
            if b in (0, 2):
                self.store("final_up", r.wup.at[1 - b // 2], total)
            elif b in (1, 3):
                parts = [total[:, k * size : (k + 1) * size] for k in range(bands)]
                self.store("final_down", r.wdown.at[1 - b // 2], jnp.stack(parts))
            else:
                self.store("final_out", r.wout.at[7 - b], total[:, :size])
                self.store("final_qkv", r.wqkv.at[7 - b], total[:, size:])

    def finish(self):
        for copies in self.loading.values():
            wait_all(copies)


def layer_loads(r, loads, layer, arena):
    width = arena.shape[1]
    copies = [
        loads(r.w_qkv.at[layer, :, i * width : (i + 1) * width], arena.at[i]) for i in range(3)
    ]
    return copies + [loads(r.w_out.at[layer], arena.at[3])]


def wait_all(copies):
    for copy in copies:
        copy.wait()


def project_pair_into(kv_ref, into_ref, arena, start, count):
    width = arena.shape[1]
    part = slice(start, start + count)
    kv_ref[part, :width] = dot_nn(into_ref[part, :], arena[1]).astype(bfloat)
    kv_ref[part, width:] = dot_nn(into_ref[part, :], arena[2]).astype(bfloat)


class Quarters:
    def __init__(self, r, loads, arena):
        self.r, self.loads, self.arena = r, loads, arena
        self.coming = {}

    def load(self, stream, j):
        r, width = self.r, self.arena.shape[1]
        cols = pl.ds(j * width, width)
        pair = 2 * (j % 2)
        self.coming[stream, j] = [
            self.loads(r.w_up.at[stream, :, cols], self.arena.at[pair]),
            self.loads(r.w_down.at[stream, cols, :], self.arena.at[pair + 1]),
        ]

    def ready(self, stream, j):
        wait_all(self.coming.pop((stream, j)))
        pair = 2 * (j % 2)
        return self.arena.at[pair], self.arena.at[pair + 1]


def feed_both_ways(dims, r, red, quarters, stream, norm, values, cot, hidden_ref, total, back, kept, after):
    bands = dims["bands"]
    width = values.shape[1]
    row_out, row_up, row_down, row_gain, row_bias = vec_rows(dims)
    hidden_ref[...] = norm_forward(values[...], r.gain[norm : norm + 1, :], r.bias[norm : norm + 1, :])
    total[...] = values[...] + r.b_down[stream : stream + 1, :]
    back[...] = jnp.zeros_like(back)
    r.vec[row_down + stream : row_down + stream + 1, :] = jnp.sum(
        cot[...].astype(full), axis=0, keepdims=True
    )
    row_up = row_up + stream * bands
    units = FeedUnits(dims, red, 2 * (1 - stream))
    for j in range(bands):
        up, down = quarters.ready(stream, j)
        z = dot_nn(hidden_ref[...], up[...]) + r.b_up[stream : stream + 1, j * width : (j + 1) * width]
        square = z * z
        bend = jnp.tanh(0.7978845608028654 * (z + 0.044715 * (square * z)))
        half = 0.5 * (1.0 + bend)
        slope = half + (0.5 * z) * (1.0 - bend * bend) * (
            0.7978845608028654 * (1.0 + 0.134145 * square)
        )
        active = (z * half).astype(bfloat)
        total[...] += dot_nn(active, down[...])
        dz = dot_nt(cot[...], down[...]) * slope
        r.vec[row_up + j : row_up + j + 1, :] = jnp.sum(dz, axis=0, keepdims=True)
        dz = dz.astype(bfloat)
        back[...] += dot_nt(dz, up[...])
        if j + 2 < bands:
            quarters.load(stream, j + 2)
        if kept is None:
            units.quarter(j, hidden_ref[...], dz, active, cot[...])
        else:
            kept[j][0][...] = dz
            kept[j][1][...] = active
        after(j)
    if kept is None:
        units.finish()


class FeedUnits:
    def __init__(self, dims, red, bag):
        self.dims, self.red, self.bag = dims, red, bag
        self.waiting = []

    def quarter(self, j, hidden, dz, active, low_grad):
        dims, red = self.dims, self.red
        bands, slab = dims["bands"], dims["slab"]
        deep = bands * slab
        up_grad = dot_tn(hidden, dz).astype(bfloat)
        unit = red.unit(lambda tile: split_blocks(dims, tile, up_grad, red.core))
        self.waiting.append((unit, red.slab_targets(self.bag, j)))
        if len(self.waiting) > 1:
            red.settle(*self.waiting.pop(0))
        down_grad = dot_tn(active, low_grad).astype(bfloat)

        def fill(tile):
            for side in range(2):
                part = down_grad[side * deep : (side + 1) * deep]
                for k in range(bands):
                    tile[lax.rem(side + red.core, 2), k] = part[k * slab : (k + 1) * slab]

        unit = red.unit(fill)
        self.waiting.append((unit, red.block_targets(self.bag + 1, j)))
        red.settle(*self.waiting.pop(0))

    def finish(self):
        for item in self.waiting:
            self.red.settle(*item)
        self.red.flush()


def feed_end(dims, r, norm, values, cot, back):
    row_out, row_up, row_down, row_gain, row_bias = vec_rows(dims)
    pull, gain, bias = norm_backward(back[...], values[...], r.gain[norm : norm + 1, :])
    r.vec[row_gain + norm : row_gain + norm + 1, :] = gain
    r.vec[row_bias + norm : row_bias + norm + 1, :] = bias
    return cot[...].astype(full) + pull


def pair_back(dkv_ref, arena, start, count):
    width = arena.shape[1]
    part = slice(start, start + count)
    return dot_nt(dkv_ref[part, :width], arena[1]) + dot_nt(dkv_ref[part, width:], arena[2])


def scatter_back(r, bands, dkv_ref, arena, count, parts, landing, send, recv):
    me = lax.axis_index("row")
    copies = []
    for s in (2, 1, 3):
        parts[s - 1] = pair_back(dkv_ref, arena, s * count, count).astype(bfloat)
        copy = remote(
            parts.at[s - 1],
            landing.at[s - 1],
            send.at[s - 1],
            recv.at[s - 1],
            {"row": lax.rem(me + bands - s, bands)},
        )
        copy.start()
        copies.append(copy)
    return pair_back(dkv_ref, arena, 0, count), copies


def weight_units(dims, r, red, b, context, low, from_rows, into_rows, dq, dkv, begin=True):
    width = r.tile.shape[-1]
    sides = [
        lambda: dot_tn(context[...], low[...]),
        lambda: dot_tn(from_rows[...], dq[...]),
        lambda: dot_tn(into_rows[...], dkv[:, :width]),
        lambda: dot_tn(into_rows[...], dkv[:, width:]),
    ]
    units = []
    for j, side in enumerate(sides):
        grad = side().astype(bfloat)
        units.append(red.unit(lambda tile: split_blocks(dims, tile, grad, red.core)))
        if j:
            red.settle(units[j - 1], red.slab_targets(b, j - 1))
        if j == 3 and begin:
            red.flush(units[:2])
            red.first(b, 0)
    red.settle(units[-1], red.slab_targets(b, 3))
    red.flush()
    if begin:
        red.first(b, 1)


def vec_rows(dims):
    quarters = dims["bands"]
    return 0, 4, 4 + 2 * quarters, 6 + 2 * quarters, 13 + 2 * quarters


def put_vectors(dims, r):
    bands, slab, pages = dims["bands"], dims["slab"], dims["pages"]
    row_out, row_up, row_down, row_gain, row_bias = vec_rows(dims)
    width = r.vec.shape[1]
    page = lax.axis_index("page")
    own = pltpu.roll(r.vec[...], lax.rem(width - page * slab, width), 1)[:, :slab]
    r.bout[...] = own[row_out:row_up]
    r.bdown[...] = own[row_down:row_gain]
    r.gain_grad[...] = own[row_gain:row_bias]
    r.bias_grad[...] = own[row_bias : row_bias + 7]
    hidden = bands * slab
    per_row = pages // bands
    row, shift = page // per_row, lax.rem(page, per_row) * hidden
    for stream in range(2):
        start = row_up + stream * bands
        chosen = jnp.zeros((1, width), full)
        for k in range(bands):
            chosen = chosen + jnp.where(row == k, r.vec[start + k : start + k + 1, :], 0.0)
        r.bup[stream : stream + 1, :] = jnp.where(
            shift == 0, chosen[:, :hidden], chosen[:, width - hidden :]
        )


def back_kernel(dims, r):
    page_width, bands, rows, tokens = (dims[n] for n in ("page_width", "bands", "rows", "tokens"))
    slab = dims["slab"]
    width = r.f1.shape[1]
    me = lax.axis_index("row")
    scalars = page_scalars(r)
    loads = Loads(r.load_sems)
    red = Reducer(dims, r, loads)
    row_out, row_up, row_down, row_gain, row_bias = vec_rows(dims)
    hm_load = loads(r.hm_hbm, r.into.at[0:rows])
    y2_load = [loads(r.y2_hbm, r.y2), loads(r.gy3_hbm, r.dq_s)]
    quarters = Quarters(r, loads, r.arena)
    quarters.load(1, 0)
    quarters.load(1, 1)
    greet(band_peers(bands) + [red.other, red.along_x, red.along_y])
    hm_load.wait()
    memo_copies = []
    for s, peer in enumerate(band_peers(bands), 1):
        copy = remote(
            r.into.at[0:rows],
            r.into.at[s * rows : (s + 1) * rows],
            r.hm_send.at[s - 1],
            r.hm_recv.at[s - 1],
            peer,
        )
        copy.start()
        memo_copies.append(copy)
    weights3 = layer_loads(r, loads, 3, r.att)
    hl_load = loads(r.hl_hbm.at[0], r.from_rows)
    x1_load = loads(r.x1_hbm, r.f1)
    gx3_load = loads(r.gx3_hbm, r.cot)
    small = [
        loads(src, dst)
        for src, dst in (
            (r.q2_hbm, r.q2),
            (r.c2_hbm, r.c2),
            (r.log2_hbm, r.log2),
            (r.q1_hbm, r.q1),
            (r.c1_hbm, r.c1),
            (r.log1_hbm, r.log1),
            (r.ha_hbm, r.ha),
            (r.y1_hbm, r.y1),
        )
    ]
    r.vec[...] = jnp.zeros_like(r.vec)

    wait_all(y2_load)

    def after_query(j):
        if j == 2:
            red.flush()
            red.first(0, 0)

    feed_both_ways(
        dims, r, red, quarters, 1, 6, r.y2, r.dq_s, r.grad_s, r.own_m, r.gy, None, after_query
    )
    red.first(0, 1)
    red.first(1)
    quarters.load(0, 0)
    quarters.load(0, 1)
    r.query_out[...] = r.own_m[...].astype(bfloat)
    r.gy[...] = feed_end(dims, r, 6, r.y2, r.dq_s, r.gy)

    every = slice(None)
    few = slice(0, bands * rows)
    hl_load.wait()
    wait_all(weights3)
    r.q[...] = (dot_nn(r.from_rows[...], r.att[0]) * SCALE).astype(bfloat)
    project_pair_into(r.kv, r.into, r.att, 0, rows)
    for s in range(1, bands):
        memo_copies[s - 1].wait()
        project_pair_into(r.kv, r.into, r.att, s * rows, rows)
    bias = read_bias(me, dims, scalars)
    r.log[...] = jnp.zeros_like(r.log)
    attend_rows(r.q, r.kv, r.context, r.log, bias, every, few)
    x1_load.wait()
    r.f2[...] = r.f1[...] + (dot_nn(r.context[...], r.att[3]) + r.b_out[3:4, :])

    gx3_load.wait()

    def after_patches(j):
        if j == 1:
            red.load_second(0)
        if j == 2:
            red.second(0)
            red.load_second(1)

    spare = slice(bands * rows, bands * rows + tokens)
    places = [r.parts_l.at[0], r.parts_l.at[1], r.parts_l.at[2], r.into.at[spare]]
    for ref in (r.kv, r.dkv):
        places += [ref.at[spare, :width], ref.at[spare, width:]]
    kept = [(places[2 * j], places[2 * j + 1]) for j in range(bands)]
    feed_both_ways(
        dims, r, red, quarters, 0, 5, r.f2, r.cot, r.hidden, r.f3, r.f4, kept, after_patches
    )
    red.second(1)
    weights2 = layer_loads(r, loads, 2, r.arena)
    to_right = {"row": lax.rem(me + 1, bands)}
    moved = dot_tn(r.order[...], r.f3[...].astype(bfloat)).astype(bfloat)
    stay = tokens - SHIFT * page_width
    r.vis_out[tokens - stay :, :] = moved[:stay]
    r.halo_low[...] = moved[stay:]
    halo = remote(
        r.halo_low, r.vis_out.at[: tokens - stay], r.halo_send.at[0], r.halo_recv.at[0], to_right
    )
    halo.start()
    gx2 = feed_end(dims, r, 5, r.f2, r.cot, r.f4)
    r.f5[...] = gx2
    red.load_third(0)

    low = gx2.astype(bfloat)
    r.low[...] = low
    r.vec[row_out + 3 : row_out + 4, :] = jnp.sum(low.astype(full), axis=0, keepdims=True)
    r.grad[...] = dot_nt(low, r.att[3]).astype(bfloat)
    between = (lambda: (red.third(0), red.load_third(1)), lambda: red.third(1))
    attend_rows_back(r.q, r.kv, r.context, r.log, r.grad, r.dq, r.dkv, bias, every, few, between)
    own, memo_sends = scatter_back(
        r, bands, r.dkv, r.att, rows, r.parts_m, r.got_m, r.memo_send, r.memo_recv
    )
    r.own_m[...] = own
    r.f4[...] = dot_nt(r.dq[...], r.att[0])
    weights0 = layer_loads(r, loads, 0, r.att)
    few_dkv, few_into = r.dkv.at[0 : bands * rows], r.into.at[0 : bands * rows]
    units = FeedUnits(dims, red, 2)
    for j in range(bands):
        units.quarter(j, r.hidden[...], kept[j][0][...], kept[j][1][...], r.cot[...])
        if j == 2:
            red.flush()
            red.first(2, 0)
    units.finish()
    red.first(2, 1)
    red.first(3)
    kv_load = loads(r.kv2_hbm, r.kv)
    weight_units(dims, r, red, 4, r.context, r.low, r.from_rows, few_into, r.dq, few_dkv, False)
    late = [
        loads(r.hl_all_hbm, r.into),
        loads(r.q0_hbm, r.q),
        loads(r.c0_hbm, r.context),
        loads(r.log0_hbm, r.log),
        loads(r.hv_hbm, r.from_rows),
        loads(r.x1_hbm, r.f1),
        loads(r.x0_hbm, r.cot),
    ]

    wait_all(small)
    wait_all(memo_sends)
    red.fourth(0, 1)
    pull, gain4, bias4 = norm_backward(
        r.own_m[...] + sum(r.got_m[s].astype(full) for s in range(bands - 1)),
        r.y2[...],
        r.gain[4:5, :],
    )
    r.vec[row_gain + 4 : row_gain + 5, :] = gain4
    r.vec[row_bias + 4 : row_bias + 5, :] = bias4
    gy = r.gy[...] + pull
    r.gy[...] = gy
    low = gy.astype(bfloat)
    r.low_s[...] = low
    r.vec[row_out + 2 : row_out + 3, :] = jnp.sum(low.astype(full), axis=0, keepdims=True)
    wait_all(weights2)
    r.grad_s[...] = dot_nt(low, r.arena[3]).astype(bfloat)
    kv_load.wait()
    attend_rows_back(
        r.q2,
        r.kv,
        r.c2,
        r.log2,
        r.grad_s,
        r.dq_s,
        r.dkv,
        look_bias(dims, scalars),
        every,
        every,
        (lambda: red.load_second(2), lambda: (red.second(2), red.load_second(3))),
    )
    red.second(3)
    red.first(4)
    red.end(0, 1)
    kv_load = loads(r.kv1_hbm, r.kv.at[0 : bands * rows])
    own, look_sends = scatter_back(
        r, bands, r.dkv, r.arena, tokens, r.parts_l, r.got_l, r.look_send, r.look_recv
    )
    r.f4[...] += own
    pull, gain2, bias2 = norm_backward(dot_nt(r.dq_s[...], r.arena[0]), r.y1[...], r.gain[2:3, :])
    r.vec[row_gain + 2 : row_gain + 3, :] = gain2
    r.vec[row_bias + 2 : row_bias + 3, :] = bias2
    r.gy[...] += pull
    weights1 = layer_loads(r, loads, 1, r.arena)
    wait_all(late)
    weight_units(dims, r, red, 5, r.c2, r.low_s, r.ha, r.into, r.dq_s, r.dkv)
    hidden_load = loads(r.hs_hbm, r.into.at[0 : bands * rows])
    red.load_third(2, 3)

    low = r.gy[...].astype(bfloat)
    r.low_s[...] = low
    r.vec[row_out + 1 : row_out + 2, :] = jnp.sum(low.astype(full), axis=0, keepdims=True)
    wait_all(weights1)
    r.grad_s[...] = dot_nt(low, r.arena[3]).astype(bfloat)
    kv_load.wait()
    bias = self_bias(me, scalars, rows, bands)
    between = (lambda: (red.third(2, 3), red.load_second(4)), lambda: red.second(4))
    attend_rows_back(
        r.q1, r.kv, r.c1, r.log1, r.grad_s, r.dq_s, r.dkv, bias, every, few, between
    )
    kv_load = loads(r.kv0_hbm, r.kv.at[0:tokens])
    own, self_sends = scatter_back(
        r, bands, r.dkv, r.arena, rows, r.parts_m, r.got_s, r.self_send, r.self_recv
    )
    r.own_m[...] = own + dot_nt(r.dq_s[...], r.arena[0])
    hidden_load.wait()
    weight_units(
        dims, r, red, 6, r.c1, r.low_s, r.into.at[0:rows], few_into, r.dq_s, few_dkv
    )

    red.load_second(5)
    red.load_third(4)
    red.second(5)
    wait_all(look_sends)
    red.third(4)
    pull, gain3, bias3 = norm_backward(
        r.f4[...] + sum(r.got_l[s].astype(full) for s in range(bands - 1)),
        r.f1[...],
        r.gain[3:4, :],
    )
    r.vec[row_gain + 3 : row_gain + 4, :] = gain3
    r.vec[row_bias + 3 : row_bias + 4, :] = bias3
    gx1 = r.f5[...] + pull
    r.f5[...] = gx1
    low = gx1.astype(bfloat)
    r.low[...] = low
    r.vec[row_out : row_out + 1, :] = jnp.sum(low.astype(full), axis=0, keepdims=True)
    wait_all(weights0)
    r.grad[...] = dot_nt(low, r.att[3]).astype(bfloat)
    kv_load.wait()
    size = WIN * WIN
    for w in range(tokens // size):
        part = slice(w * size, (w + 1) * size)
        bias = window_bias(scalars, r.region, w, page_width)
        attend_rows_back(
            r.q, r.kv, r.context, r.log, r.grad, r.dq, r.dkv, bias, part, part
        )
        if w == 0:
            red.load_third(5)
        else:
            red.third(5)
            red.load_second(6)
    dr = pair_back(r.dkv, r.att, 0, tokens) + dot_nt(r.dq[...], r.att[0])
    pull, gain0, bias0 = norm_backward(dr, r.cot[...].astype(full), r.gain[0:1, :])
    r.vec[row_gain : row_gain + 1, :] = gain0
    r.vec[row_bias : row_bias + 1, :] = bias0
    gx0 = r.f5[...] + pull
    high = gx0.astype(bfloat)
    rest = (gx0 - high.astype(full)).astype(bfloat)
    moved = dot_tn(r.order[...], high) + dot_tn(r.order[...], rest)
    r.vis_grad[tokens - stay :, :] = moved[:stay]
    r.f2[: tokens - stay, :] = moved[stay:]
    halo_back = remote(
        r.f2.at[: tokens - stay], r.vis_grad.at[: tokens - stay], r.halo_send.at[1], r.halo_recv.at[1], to_right
    )
    halo_back.start()
    red.second(6)
    weight_units(
        dims, r, red, 7, r.context, r.low, r.from_rows, r.from_rows, r.dq, r.dkv.at[0:tokens]
    )
    red.load_own(7)
    red.load_third(6)

    wait_all(self_sends)
    pull, gain1, bias1 = norm_backward(
        r.own_m[...] + sum(r.got_s[s].astype(full) for s in range(bands - 1)),
        r.y0[...].astype(full),
        r.gain[1:2, :],
    )
    r.query_grad[...] = r.gy[...] + pull
    r.vec[row_gain + 1 : row_gain + 2, :] = gain1
    r.vec[row_bias + 1 : row_bias + 2, :] = bias1

    def swap(i, device):
        copy = remote(r.vec, r.vec_in.at[i], r.vec_send.at[i], r.vec_recv.at[i], device)
        copy.start()
        return copy

    def add(i, copy):
        copy.wait()
        r.vec[...] = r.vec[...] + r.vec_in[i]

    red.fourth(2, 3)
    red.third(6)
    copy = swap(0, red.other)
    red.end(2, 3)
    add(0, copy)
    copy = swap(1, {"row": red.next})
    red.fourth(4, 5)
    add(1, copy)
    copy = swap(2, {"row": red.far})
    red.load_second(7)
    red.second(7)
    add(2, copy)
    copy = swap(3, red.along_x)
    red.end(4, 5)
    red.fourth(6)
    add(3, copy)
    copy = swap(4, red.along_y)
    red.load_third(7)
    red.third(7)
    add(4, copy)
    put_vectors(dims, r)
    red.end(6)
    red.fourth(7)
    red.end(7)
    halo.wait()
    halo_back.wait()
    red.finish()


def shards(
    vis_stream,
    query_stream,
    w_qkv,
    w_out,
    b_out,
    w_up,
    b_up,
    w_down,
    b_down,
    norm_gain,
    norm_bias,
    page_cols,
    query_len,
    prompt_len,
    region_ids,
    vis_cotangent,
    query_cotangent,
):
    band_rows, page_width, width = vis_stream.shape[1:]
    tokens = band_rows * page_width
    rows = query_stream.shape[1]
    bands, pages = lax.axis_size("row"), lax.axis_size("page")
    me = lax.axis_index("row")
    hidden_units = w_up.shape[2]
    slab = width // pages
    dims = dict(
        page_width=page_width,
        bands=bands,
        tokens=tokens,
        rows=rows,
        pages=pages,
        slab=slab,
    )
    qkv_any, out_any = (w_qkv, ANY), (w_out, ANY)
    log_lanes = full_shape(tokens, PAIR)
    y0, gy3 = query_stream[0], query_cotangent[0]
    lengths = dict(
        page_cols=(page_cols, SMEM), query_len=(query_len, SMEM), prompt_len=(prompt_len, SMEM)
    )
    order = jnp.asarray(source_order(page_width, band_rows), bfloat)

    given = dict(
        **lengths,
        vis=(vis_stream, VMEM),
        cot=(vis_cotangent, VMEM),
        y0=(y0, VMEM),
        order=(order, VMEM),
        region=(region_ids, VMEM),
        gain=(norm_gain, VMEM),
        bias=(norm_bias, VMEM),
        b_out=(b_out, VMEM),
        w_qkv=qkv_any,
        w_out=out_any,
    )
    weight = {}
    for a in range(3):
        weight["wqkv%d" % a] = pltpu.VMEM((width, 3 * width), bfloat)
        weight["wout%d" % a] = pltpu.VMEM((width, width), bfloat)
    pair_sems = pltpu.SemaphoreType.DMA((2,))
    peer_sems = pltpu.SemaphoreType.DMA((bands - 1,))
    front = launch(
        partial(front_kernel, dims),
        given,
        {},
        {},
        dict(
            x0=low_shape(tokens, width),
            hv=low_shape(tokens, width),
            q0=low_shape(tokens, width),
            kv0=low_shape(tokens, 2 * width),
            c0=low_shape(tokens, width),
            log0=log_lanes,
            x1=full_shape(tokens, width),
            gx3=low_shape(tokens, width),
            hs=low_shape(bands, rows, width),
            q1=low_shape(rows, width),
            kv1=low_shape(bands * rows, 2 * width),
            c1=low_shape(rows, width),
            log1=full_shape(rows, PAIR),
            y1=full_shape(rows, width),
            ha=low_shape(rows, width),
            q2=low_shape(rows, width),
            hl=low_shape(bands, tokens, width),
            kv2=low_shape(bands * tokens, 2 * width),
            c2=low_shape(rows, width),
            log2=full_shape(rows, PAIR),
            y2=full_shape(rows, width),
            hm=low_shape(rows, width),
        ),
        dict(
            cells=pltpu.VMEM((tokens, width), full),
            halo=pltpu.VMEM((2, SHIFT, page_width, width), bfloat),
            halo_send=pair_sems,
            halo_recv=pair_sems,
            self_send=peer_sems,
            self_recv=peer_sems,
            look_send=peer_sems,
            look_recv=peer_sems,
            weight_sems=pltpu.SemaphoreType.DMA((6,)),
            **weight,
        ),
        0,
        40 * tokens * width * width,
    )
    hbm = {
        "x1_hbm": front["x1"],
        "x0_hbm": front["x0"],
        "gx3_hbm": front["gx3"],
        "hv_hbm": front["hv"],
        "hl_hbm": front["hl"],
        "hl_all_hbm": front["hl"].reshape(bands * tokens, width),
        "hs_hbm": front["hs"].reshape(bands * rows, width),
        "ha_hbm": front["ha"],
        "hm_hbm": front["hm"],
        "y1_hbm": front["y1"],
        "y2_hbm": front["y2"],
        "gy3_hbm": gy3,
        "w_qkv": w_qkv,
        "w_out": w_out,
        "w_up": w_up,
        "w_down": w_down,
    }
    for a in range(3):
        for name in ("q", "kv", "c", "log"):
            hbm["%s%d_hbm" % (name, a)] = front["%s%d" % (name, a)]
    near = dict(
        y0=y0,
        order=order,
        region=region_ids,
        gain=norm_gain,
        bias=norm_bias,
        b_out=b_out,
        b_up=b_up,
        b_down=b_down,
    )
    height = bands * slab
    halo_rows = SHIFT * page_width
    vec_shape = full_shape(vec_rows(dims)[-1] + 11, width)
    wide = lambda count: pltpu.VMEM((count, width), full)
    narrow = lambda count: pltpu.VMEM((count, width), bfloat)
    dma = pltpu.SemaphoreType.DMA
    scratch = dict(
        att=pltpu.VMEM((4, width, width), bfloat),
        arena=pltpu.VMEM((4, width, width), bfloat),
        tile=pltpu.VMEM((RING, 2, pages // 2, slab, width), bfloat),
        landed=pltpu.VMEM((RING, pages // 2, slab, width), bfloat),
        sums=pltpu.VMEM((2, 2, 2, height // 2, width), bfloat),
        came=pltpu.VMEM((2, 2, 2, height // 2, width), bfloat),
        pieces=pltpu.VMEM((4, bands, slab, width), bfloat),
        last=pltpu.VMEM((2, 2, slab, width), bfloat),
        hidden=narrow(tokens),
        recv3=pltpu.VMEM((8, 2, slab, width), bfloat),
        recv4=pltpu.VMEM((8, slab, width), bfloat),
        final_up=wide(slab),
        final_down=pltpu.VMEM((bands, slab, width // bands), full),
        final_out=pltpu.VMEM((slab, width // bands), full),
        final_qkv=pltpu.VMEM((slab, 3 * width // bands), full),
        q=narrow(tokens),
        kv=pltpu.VMEM((bands * tokens, 2 * width), bfloat),
        context=narrow(tokens),
        log=pltpu.VMEM((tokens, PAIR), full),
        grad=narrow(tokens),
        dq=narrow(tokens),
        dkv=pltpu.VMEM((bands * tokens, 2 * width), bfloat),
        low=narrow(tokens),
        cot=narrow(tokens),
        from_rows=narrow(tokens),
        into=narrow(bands * tokens),
        f1=wide(tokens),
        f2=wide(tokens),
        f3=wide(tokens),
        f4=wide(tokens),
        f5=wide(tokens),
        q2=narrow(rows),
        c2=narrow(rows),
        q1=narrow(rows),
        c1=narrow(rows),
        log2=pltpu.VMEM((rows, PAIR), full),
        log1=pltpu.VMEM((rows, PAIR), full),
        ha=narrow(rows),
        low_s=narrow(rows),
        grad_s=narrow(rows),
        dq_s=narrow(rows),
        y1=wide(rows),
        y2=wide(rows),
        gy=wide(rows),
        own_m=wide(rows),
        parts_m=pltpu.VMEM((bands - 1, rows, width), bfloat),
        parts_l=pltpu.VMEM((bands - 1, tokens, width), bfloat),
        got_m=pltpu.VMEM((bands - 1, rows, width), bfloat),
        got_l=pltpu.VMEM((bands - 1, tokens, width), bfloat),
        got_s=pltpu.VMEM((bands - 1, rows, width), bfloat),
        halo_low=narrow(halo_rows),
        vec=pltpu.VMEM(vec_shape.shape, full),
        vec_in=pltpu.VMEM((5,) + vec_shape.shape, full),
        load_sems=dma((192,)),
        core_send=dma((RING,)),
        core_recv=dma((RING,)),
        core_out=dma((RING, bands)),
        core_free=pltpu.SemaphoreType.REGULAR,
        stage_send=dma((8, 8)),
        stage_recv=dma((8, 8)),
        halo_send=pair_sems,
        halo_recv=pair_sems,
        hm_send=peer_sems,
        hm_recv=peer_sems,
        memo_send=peer_sems,
        memo_recv=peer_sems,
        look_send=peer_sems,
        look_recv=peer_sems,
        self_send=peer_sems,
        self_recv=peer_sems,
        vec_send=dma((5,)),
        vec_recv=dma((5,)),
    )
    result = launch(
        partial(back_kernel, dims),
        lengths
        | {n: (v, VMEM) for n, v in near.items()}
        | {n: (v, ANY) for n, v in hbm.items()},
        {},
        dict(
            vis_out=(low_shape(tokens, width), VMEM),
            vis_grad=(full_shape(tokens, width), VMEM),
            query_grad=(full_shape(rows, width), VMEM),
            query_out=(low_shape(rows, width), VMEM),
            bout=(full_shape(4, slab), VMEM),
            bup=(full_shape(2, height), VMEM),
            bdown=(full_shape(2, slab), VMEM),
            gain_grad=(full_shape(7, slab), VMEM),
            bias_grad=(full_shape(7, slab), VMEM),
            wqkv=(full_shape(4, slab, 3 * width // bands), ANY),
            wout=(full_shape(4, slab, width // bands), ANY),
            wup=(full_shape(2, slab, width), ANY),
            wdown=(full_shape(2, bands, slab, width // bands), ANY),
            bags=(low_shape(8, 2, 2, height, width), ANY),
            recv1=(low_shape(8, 2, 2, height // 2, width), ANY),
            recv2=(low_shape(8, 2, height // 2, width), ANY),
        ),
        {},
        scratch,
        1,
        100 * tokens * width * width,
    )

    names = (
        ("vis_out", "query_out", "vis_grad", "query_grad", "wqkv", "wout", "bout")
        + ("wup", "bup", "wdown", "bdown", "gain_grad", "bias_grad")
    )
    final = dict(zip(names, hand_over([result[n] for n in names])))
    grid_shape = (1, band_rows, page_width, width)
    final["vis_out"] = final["vis_out"].reshape(grid_shape)
    final["vis_grad"] = final["vis_grad"].reshape(grid_shape)
    final["query_out"] = final["query_out"][None]
    final["query_grad"] = final["query_grad"][None]
    final["wdown"] = jnp.swapaxes(final["wdown"], 1, 2)
    return tuple(final[n] for n in names)


def plain_ring(count, distance):
    return [(i, (i + distance) % count) for i in range(count)]


def plain_flipped(count, bit):
    return [(i, i ^ bit) for i in range(count)]


def plain_mat_dot(left, right):
    return jnp.dot(left, right, preferred_element_type=jnp.float32)


def plain_mat_left(left, right):
    return lax.dot_general(
        left, right, (((0,), (0,)), ((), ())), preferred_element_type=jnp.float32
    )


def plain_mat_right(left, right):
    return lax.dot_general(
        left, right, (((1,), (1,)), ((), ())), preferred_element_type=jnp.float32
    )


def plain_norm_forward(values, gain_row, bias_row):
    average = jnp.mean(values, axis=-1, keepdims=True)
    centred = values - average
    spread = jnp.mean(centred * centred, axis=-1, keepdims=True)
    inverse = lax.rsqrt(spread + norm_eps)
    normal = centred * inverse
    return ((normal * gain_row + bias_row).astype(bfloat), normal, inverse)


def plain_norm_backward(grad_result, normal, inverse, gain_row):
    grad_normal = grad_result * gain_row
    first_mean = jnp.mean(grad_normal, axis=-1, keepdims=True)
    second_mean = jnp.mean(grad_normal * normal, axis=-1, keepdims=True)
    grad_input = inverse * (grad_normal - first_mean - normal * second_mean)
    return (grad_input, jnp.sum(grad_result * normal, axis=0), jnp.sum(grad_result, axis=0))


def plain_to_windows(grid_cells):
    row_count, col_count = (grid_cells.shape[0], grid_cells.shape[1])
    trailing = grid_cells.shape[2:]
    carved = grid_cells.reshape((row_count // WIN, WIN, col_count // WIN, WIN) + trailing)
    return jnp.swapaxes(carved, 1, 2).reshape((-1, WIN * WIN) + trailing)


def plain_from_windows(blocks, row_count, col_count):
    trailing = blocks.shape[2:]
    carved = blocks.reshape((row_count // WIN, col_count // WIN, WIN, WIN) + trailing)
    return jnp.swapaxes(carved, 1, 2).reshape((row_count, col_count) + trailing)


def plain_to_shifted(grid_cells):
    count = lax.axis_size("row")
    arriving = lax.ppermute(grid_cells[:SHIFT], "row", plain_ring(count, -1))
    rolled = jnp.concatenate([grid_cells[SHIFT:], arriving], axis=0)
    return plain_to_windows(jnp.roll(rolled, -SHIFT, axis=1)).reshape(-1, grid_cells.shape[2])


def plain_from_shifted(tokens, row_count, col_count):
    count = lax.axis_size("row")
    cells = plain_from_windows(tokens.reshape(-1, WIN * WIN, tokens.shape[1]), row_count, col_count)
    rolled = jnp.roll(cells, SHIFT, axis=1)
    arriving = lax.ppermute(rolled[row_count - SHIFT :], "row", plain_ring(count, 1))
    return jnp.concatenate([arriving, rolled[: row_count - SHIFT]], axis=0)


def plain_gather_row(values):
    count = lax.axis_size("row")
    parts = [values] + [lax.ppermute(values, "row", plain_ring(count, s)) for s in range(1, count)]
    return jnp.concatenate(parts, axis=0)


def plain_scatter_row(partial_sums):
    count = lax.axis_size("row")
    parts = jnp.split(partial_sums.astype(bfloat), count, axis=0)
    total = jnp.split(partial_sums, count, axis=0)[0]
    for s in range(1, count):
        total = total + lax.ppermute(parts[s], "row", plain_ring(count, -s)).astype(jnp.float32)
    return total


def plain_halve(blocks, bit, slot):
    count = lax.axis_size("page")
    mine = (lax.axis_index("page") // bit) % 2
    kept = lax.dynamic_index_in_dim(blocks, mine, slot, keepdims=False)
    sent = lax.dynamic_index_in_dim(blocks, 1 - mine, slot, keepdims=False)
    return kept + lax.ppermute(sent, "page", plain_flipped(count, bit))


def plain_reduce_matrix(grad):
    pages = lax.axis_size("page")
    rows = lax.axis_size("row")
    bits = []
    while 2 ** len(bits) < pages:
        bits.append(2 ** len(bits))
    height, width = grad.shape
    blocks = grad.astype(bfloat).reshape((2,) * len(bits) + (height // pages, width))
    if bits:
        blocks = plain_halve(blocks, 1, len(bits) - 1)
    left, right = jnp.split(blocks, 2, axis=-1)
    rest = bits[1:]
    for bit in rest:
        left = plain_halve(left, bit, left.ndim - 3)
    for bit in reversed(rest):
        right = plain_halve(right, bit, 0)
    share = jnp.concatenate([left, right], axis=-1)
    me = lax.axis_index("row")
    pieces = share.reshape(share.shape[0], rows, width // rows)
    total = lax.dynamic_index_in_dim(pieces, me, 1, keepdims=False).astype(jnp.float32)
    for s in range(1, rows):
        sent = lax.dynamic_index_in_dim(pieces, (me + s) % rows, 1, keepdims=False)
        total = total + lax.ppermute(sent, "row", plain_ring(rows, s)).astype(jnp.float32)
    return total


def plain_reduce_vectors(stack):
    pages = lax.axis_size("page")
    rows = lax.axis_size("row")
    bit = 1
    while bit < pages:
        stack = stack.reshape(-1, 2, stack.shape[-1])
        stack = plain_halve(stack, bit, 1)
        bit *= 2
    vector = stack.reshape(-1)
    total = vector
    for s in range(1, rows):
        total = total + lax.ppermute(vector, "row", plain_ring(rows, s))
    return total


def plain_split_heads(values):
    return values.reshape(values.shape[0], values.shape[1], -1, HDIM)


def plain_masked_scores(queries, key_rows, allowed):
    scores = jnp.einsum(
        "gqhd,gkhd->ghqk",
        plain_split_heads(queries),
        plain_split_heads(key_rows),
        preferred_element_type=jnp.float32,
    ) * HDIM ** (-0.5)
    return jnp.where(allowed[:, None], scores, masked_score)


def plain_attend_forward(queries, key_rows, value_rows, allowed):
    scores = plain_masked_scores(queries, key_rows, allowed)
    row_max = jnp.max(scores, axis=-1, keepdims=True)
    raised = jnp.exp(scores - row_max)
    row_total = jnp.sum(raised, axis=-1, keepdims=True)
    probs_low = (raised / row_total).astype(bfloat)
    context = jnp.einsum(
        "ghqk,gkhd->gqhd", probs_low, plain_split_heads(value_rows), preferred_element_type=jnp.float32
    )
    return (context.reshape(queries.shape).astype(bfloat), row_max + jnp.log(row_total))


def plain_attend_backward(queries, key_rows, value_rows, allowed, log_total, grad_context):
    probs = jnp.exp(plain_masked_scores(queries, key_rows, allowed) - log_total)
    probs_low = probs.astype(bfloat)
    grad_heads = plain_split_heads(grad_context)
    grad_values = jnp.einsum(
        "ghqk,gqhd->gkhd", probs_low, grad_heads, preferred_element_type=jnp.float32
    )
    grad_probs = jnp.einsum(
        "gqhd,gkhd->ghqk", grad_heads, plain_split_heads(value_rows), preferred_element_type=jnp.float32
    )
    row_delta = jnp.sum(probs * grad_probs, axis=-1, keepdims=True)
    grad_scores = (probs * (grad_probs - row_delta)).astype(bfloat)
    grad_queries = jnp.einsum(
        "ghqk,gkhd->gqhd", grad_scores, plain_split_heads(key_rows), preferred_element_type=jnp.float32
    ) * HDIM ** (-0.5)
    grad_keys = jnp.einsum(
        "ghqk,gqhd->gkhd", grad_scores, plain_split_heads(queries), preferred_element_type=jnp.float32
    ) * HDIM ** (-0.5)
    return (
        grad_queries.reshape(queries.shape).astype(bfloat),
        grad_keys.reshape(key_rows.shape).astype(bfloat),
        grad_values.reshape(value_rows.shape).astype(bfloat),
    )


def plain_project(from_rows, to_rows, weight):
    width = weight.shape[0]
    queries = plain_mat_dot(from_rows, weight[:, :width]).astype(bfloat)
    paired = plain_mat_dot(to_rows, weight[:, width:]).astype(bfloat)
    return (queries, paired[:, :width], paired[:, width:])


def plain_project_back(from_rows, to_rows, weight, dq, dk, dv):
    width = weight.shape[0]
    pair = jnp.concatenate([dk, dv], axis=1)
    weight_grad = jnp.concatenate([plain_mat_left(from_rows, dq), plain_mat_left(to_rows, pair)], axis=1)
    return (weight_grad, plain_mat_right(dq, weight[:, :width]), plain_mat_right(pair, weight[:, width:]))


def plain_output_back(context_low, weight, grad_residual):
    grad_low = grad_residual.astype(bfloat)
    return (
        plain_mat_left(context_low, grad_low),
        jnp.sum(grad_low, axis=0, dtype=jnp.float32),
        plain_mat_right(grad_low, weight).astype(bfloat),
    )


def plain_feed_forward(values, gain_row, bias_row, up_weight, up_bias, down_weight, down_bias):
    hidden, normal, inverse = plain_norm_forward(values, gain_row, bias_row)
    upward = plain_mat_dot(hidden, up_weight) + up_bias
    active = jax.nn.gelu(upward, approximate=True).astype(bfloat)
    return (
        values + (plain_mat_dot(active, down_weight) + down_bias),
        (hidden, normal, inverse, upward, active),
    )


def plain_feed_backward(grad_residual, kept_values, gain_row, up_weight, down_weight):
    hidden, normal, inverse, upward, active = kept_values
    grad_low = grad_residual.astype(bfloat)
    grad_down = plain_mat_left(active, grad_low)
    grad_down_bias = jnp.sum(grad_low, axis=0, dtype=jnp.float32)
    grad_active = plain_mat_right(grad_low, down_weight)
    gelu_pull = jax.vjp(partial(jax.nn.gelu, approximate=True), upward)[1]
    grad_up_low = gelu_pull(grad_active)[0].astype(bfloat)
    grad_up = plain_mat_left(hidden, grad_up_low)
    grad_up_bias = jnp.sum(grad_up_low, axis=0, dtype=jnp.float32)
    grad_input, gain_grad, bias_grad = plain_norm_backward(
        plain_mat_right(grad_up_low, up_weight), normal, inverse, gain_row
    )
    return (
        grad_residual + grad_input,
        (grad_up, grad_up_bias, grad_down, grad_down_bias, gain_grad, bias_grad),
    )


def plain_shards(
    vis_stream,
    query_stream,
    w_qkv,
    w_out,
    b_out,
    w_up,
    b_up,
    w_down,
    b_down,
    norm_gain,
    norm_bias,
    page_cols,
    query_len,
    prompt_len,
    region_ids,
    vis_cotangent,
    query_cotangent,
):
    band_rows, page_width, width = vis_stream.shape[1:]
    tokens = band_rows * page_width
    query_rows = query_stream.shape[1]
    bands = lax.axis_size("row")
    me = lax.axis_index("row")
    pages = lax.axis_size("page")
    x0 = plain_to_shifted(vis_stream[0]).astype(jnp.float32)
    gx3 = plain_to_shifted(vis_cotangent[0]).astype(jnp.float32)
    y0 = query_stream[0].astype(jnp.float32)
    gy3 = query_cotangent[0].astype(jnp.float32)
    col_limit, query_limit, prompt_limit = page_cols[0], query_len[0], prompt_len[0]

    own_positions = me * query_rows + jnp.arange(query_rows)
    all_positions = jnp.concatenate(
        [((me - s) % bands) * query_rows + jnp.arange(query_rows) for s in range(bands)]
    )
    key_live = all_positions < query_limit
    self_allowed = key_live[None, :] & (
        (all_positions[None, :] <= own_positions[:, None]) | (all_positions[None, :] < prompt_limit)
    )
    rolled_live = (jnp.arange(page_width) + SHIFT) % page_width < col_limit
    live_tiles = plain_to_windows(jnp.broadcast_to(rolled_live[None, :], (band_rows, page_width)))
    visual_allowed = jnp.broadcast_to(
        jnp.tile(live_tiles.reshape(-1), bands)[None, :], (query_rows, bands * tokens)
    )
    query_allowed = jnp.broadcast_to(key_live[None, :], (tokens, query_rows * bands))
    region_tiles = plain_to_windows(region_ids[0])
    diagonal = jnp.eye(WIN * WIN, dtype=jnp.bool_)
    window_allowed = (region_tiles[:, :, None] == region_tiles[:, None, :]) & (
        live_tiles[:, None, :] | diagonal[None]
    )
    tile_shape = (tokens // (WIN * WIN), WIN * WIN, width)

    hs, n1, i1 = plain_norm_forward(y0, norm_gain[1], norm_bias[1])
    hs_all = plain_gather_row(hs)
    hv, n0, i0 = plain_norm_forward(x0, norm_gain[0], norm_bias[0])
    qw, kw, vw = (v.reshape(tile_shape) for v in plain_project(hv, hv, w_qkv[0]))
    cw, lw = plain_attend_forward(qw, kw, vw, window_allowed)
    cw = cw.reshape(tokens, width)
    x1 = x0 + (plain_mat_dot(cw, w_out[0]) + b_out[0])
    hl, n3, i3 = plain_norm_forward(x1, norm_gain[3], norm_bias[3])
    hl_all = plain_gather_row(hl)

    qs, ks, vs = plain_project(hs, hs_all, w_qkv[1])
    cs, ls = plain_attend_forward(qs[None], ks[None], vs[None], self_allowed[None])
    cs = cs[0]
    y1 = y0 + (plain_mat_dot(cs, w_out[1]) + b_out[1])
    ha, n2, i2 = plain_norm_forward(y1, norm_gain[2], norm_bias[2])
    qa, kl, vl = plain_project(ha, hl_all, w_qkv[2])
    ca, la = plain_attend_forward(qa[None], kl[None], vl[None], visual_allowed[None])
    ca = ca[0]
    y2 = y1 + (plain_mat_dot(ca, w_out[2]) + b_out[2])
    hm, n4, i4 = plain_norm_forward(y2, norm_gain[4], norm_bias[4])
    hm_all = plain_gather_row(hm)
    y3, kept_query = plain_feed_forward(
        y2, norm_gain[6], norm_bias[6], w_up[1], b_up[1], w_down[1], b_down[1]
    )
    gy2, feed_query = plain_feed_backward(gy3, kept_query, norm_gain[6], w_up[1], w_down[1])
    final_up1 = plain_reduce_matrix(feed_query[0])
    final_down1 = plain_reduce_matrix(feed_query[2])

    qr, km, vm = plain_project(hl, hm_all, w_qkv[3])
    cr, lr = plain_attend_forward(qr[None], km[None], vm[None], query_allowed[None])
    cr = cr[0]
    x2 = x1 + (plain_mat_dot(cr, w_out[3]) + b_out[3])
    x3, kept_vis = plain_feed_forward(
        x2, norm_gain[5], norm_bias[5], w_up[0], b_up[0], w_down[0], b_down[0]
    )
    gx2, feed_vis = plain_feed_backward(gx3, kept_vis, norm_gain[5], w_up[0], w_down[0])
    final_up0 = plain_reduce_matrix(feed_vis[0])
    final_down0 = plain_reduce_matrix(feed_vis[2])

    wout3, bout3, dcr = plain_output_back(cr, w_out[3], gx2)
    dqr, dkm, dvm = plain_attend_backward(
        qr[None], km[None], vm[None], query_allowed[None], lr, dcr[None]
    )
    qkv3, dhl, dhm = plain_project_back(hl, hm_all, w_qkv[3], dqr[0], dkm[0], dvm[0])
    gy_memo, gain4, bias4 = plain_norm_backward(plain_scatter_row(dhm), n4, i4, norm_gain[4])
    gy2 = gy2 + gy_memo
    final_out3 = plain_reduce_matrix(wout3)
    final_qkv3 = plain_reduce_matrix(qkv3)

    wout2, bout2, dca = plain_output_back(ca, w_out[2], gy2)
    dqa, dkl, dvl = plain_attend_backward(
        qa[None], kl[None], vl[None], visual_allowed[None], la, dca[None]
    )
    qkv2, dha, dhl_all = plain_project_back(ha, hl_all, w_qkv[2], dqa[0], dkl[0], dvl[0])
    gy_ask, gain2, bias2 = plain_norm_backward(dha, n2, i2, norm_gain[2])
    gy1 = gy2 + gy_ask
    gx_look, gain3, bias3 = plain_norm_backward(dhl + plain_scatter_row(dhl_all), n3, i3, norm_gain[3])
    gx1 = gx2 + gx_look
    final_out2 = plain_reduce_matrix(wout2)
    final_qkv2 = plain_reduce_matrix(qkv2)

    wout1, bout1, dcs = plain_output_back(cs, w_out[1], gy1)
    dqs, dks, dvs = plain_attend_backward(qs[None], ks[None], vs[None], self_allowed[None], ls, dcs[None])
    qkv1, dhs, dhs_all = plain_project_back(hs, hs_all, w_qkv[1], dqs[0], dks[0], dvs[0])
    gy_self, gain1, bias1 = plain_norm_backward(dhs + plain_scatter_row(dhs_all), n1, i1, norm_gain[1])
    gy0 = gy1 + gy_self
    final_out1 = plain_reduce_matrix(wout1)
    final_qkv1 = plain_reduce_matrix(qkv1)

    wout0, bout0, dcw = plain_output_back(cw, w_out[0], gx1)
    dqw, dkw, dvw = plain_attend_backward(qw, kw, vw, window_allowed, lw, dcw.reshape(tile_shape))
    dqw, dkw, dvw = (v.reshape(tokens, width) for v in (dqw, dkw, dvw))
    qkv0, dr_from, dr_into = plain_project_back(hv, hv, w_qkv[0], dqw, dkw, dvw)
    gx_win, gain0, bias0 = plain_norm_backward(dr_from + dr_into, n0, i0, norm_gain[0])
    gx0 = gx1 + gx_win
    final_out0 = plain_reduce_matrix(wout0)
    final_qkv0 = plain_reduce_matrix(qkv0)

    vectors = [
        jnp.stack([bout0, bout1, bout2, bout3]),
        jnp.stack([feed_vis[1], feed_query[1]]),
        jnp.stack([feed_vis[3], feed_query[3]]),
        jnp.stack([gain0, gain1, gain2, gain3, gain4, feed_vis[4], feed_query[4]]),
        jnp.stack([bias0, bias1, bias2, bias3, bias4, feed_vis[5], feed_query[5]]),
    ]
    blocks = [
        jnp.swapaxes(v.reshape(v.shape[0], pages, -1), 0, 1).reshape(pages, -1) for v in vectors
    ]
    reduced = plain_reduce_vectors(jnp.concatenate(blocks, axis=1))
    finals, start = [], 0
    for v in vectors:
        size = v.size // pages
        finals.append(reduced[start : start + size].reshape(v.shape[0], -1))
        start += size

    return (
        plain_from_shifted(x3.astype(bfloat), band_rows, page_width)[None],
        y3[None].astype(bfloat),
        plain_from_shifted(gx0, band_rows, page_width)[None],
        gy0[None],
        jnp.stack([final_qkv0, final_qkv1, final_qkv2, final_qkv3]),
        jnp.stack([final_out0, final_out1, final_out2, final_out3]),
        finals[0],
        jnp.stack([final_up0, final_up1]),
        finals[1],
        jnp.stack([final_down0, final_down1]),
        finals[2],
        finals[3],
        finals[4],
    )


def solution(mesh):
    planned = mesh.shape["page"] == 8 and mesh.shape["row"] == 4
    return jax.shard_map(
        shards if planned else plain_shards,
        mesh=mesh,
        in_specs=(
            P("page", "row", None, None),
            P("page", "row", None),
            P(),
            P(),
            P(),
            P(),
            P(),
            P(),
            P(),
            P(),
            P(),
            P("page"),
            P("page"),
            P("page"),
            P("page", "row", None),
            P("page", "row", None, None),
            P("page", "row", None),
        ),
        out_specs=(
            P("page", "row", None, None),
            P("page", "row", None),
            P("page", "row", None, None),
            P("page", "row", None),
            P(None, "page", "row"),
            P(None, "page", "row"),
            P(None, "page"),
            P(None, "page", "row"),
            P(None, "page"),
            P(None, "page", "row"),
            P(None, "page"),
            P(None, "page"),
            P(None, "page"),
        ),
        check_vma=False,
    )
```

```python
from functools import partial

import jax
import jax.numpy as jnp
import numpy as np
from jax import lax
from jax.experimental import pallas as pl
from jax.experimental.pallas import tpu as pltpu
from jax.sharding import PartitionSpec as P

HDIM = 64
WIN = 12
SHIFT = 6
PAIR = 2 * HDIM
SCALE = HDIM ** (-0.5)

masked_score = -1e30
norm_eps = 1e-05
bfloat = jnp.bfloat16
full = jnp.float32
ANY = pl.BlockSpec(memory_space=pl.ANY)
VMEM = pl.BlockSpec(memory_space=pltpu.VMEM)
SMEM = pl.BlockSpec(memory_space=pltpu.SMEM)
MESH = pl.DeviceIdType.MESH


def ring(count, distance):
    return [(i, (i + distance) % count) for i in range(count)]


def flipped(count, bit):
    return [(i, i ^ bit) for i in range(count)]


def dot_nn(left, right):
    return jnp.dot(left, right, preferred_element_type=full)


def dot_nt(left, right):
    return lax.dot_general(left, right, (((1,), (1,)), ((), ())), preferred_element_type=full)


def dot_tn(left, right):
    return lax.dot_general(left, right, (((0,), (0,)), ((), ())), preferred_element_type=full)


def normalise(values):
    centred = values - jnp.mean(values, axis=-1, keepdims=True)
    spread = jnp.mean(centred * centred, axis=-1, keepdims=True)
    inverse = lax.rsqrt(spread + norm_eps)
    return centred * inverse, inverse


def norm_forward(values, gain_row, bias_row):
    return (normalise(values)[0] * gain_row + bias_row).astype(bfloat)


def norm_backward(grad, values, gain_row):
    normal, inverse = normalise(values)
    grad_normal = grad * gain_row
    first = jnp.mean(grad_normal, axis=-1, keepdims=True)
    second = jnp.mean(grad_normal * normal, axis=-1, keepdims=True)
    return (
        inverse * (grad_normal - first - normal * second),
        jnp.sum(grad * normal, axis=0, keepdims=True),
        jnp.sum(grad, axis=0, keepdims=True),
    )


def tile_cols(index, size):
    return pl.ds(pl.multiple_of(index * size, size), size)


def matmul_into(out_ref, left_ref, weight_ref, size):
    def step(i, _):
        cols = tile_cols(i, size)
        out_ref[:, cols] = dot_nn(left_ref[...], weight_ref[:, cols]).astype(out_ref.dtype)
        return 0

    lax.fori_loop(0, weight_ref.shape[1] // size, step, 0)


def two_heads(values):
    lane = lax.broadcasted_iota(jnp.int32, values.shape, 1)
    zero = jnp.zeros_like(values)
    return jnp.concatenate(
        [jnp.where(lane < HDIM, values, zero), jnp.where(lane < HDIM, zero, values)], axis=0
    )


def one_pair(stacked):
    count = stacked.shape[0] // 2
    lane = lax.broadcasted_iota(jnp.int32, (count, PAIR), 1)
    return jnp.where(lane < HDIM, stacked[:count], stacked[count:])


def attend_pair(queries, key_rows, value_rows, bias):
    scores = dot_nt(two_heads(queries), key_rows) + bias
    top = jnp.max(scores, axis=-1, keepdims=True)
    raised = jnp.exp(scores - top)
    total = jnp.sum(raised, axis=-1, keepdims=True)
    context = dot_nn(raised.astype(bfloat), value_rows) / total
    return one_pair(context).astype(bfloat), top + jnp.log(total)


def attend_pair_back(queries, key_rows, value_rows, bias, log_total, context, grad_context):
    both = two_heads(queries)
    grad_both = two_heads(grad_context)
    probs = jnp.exp(dot_nt(both, key_rows) + bias - log_total)
    grad_probs = dot_nt(grad_both, value_rows)
    delta = jnp.sum(
        grad_both.astype(full) * jnp.concatenate([context, context], axis=0).astype(full),
        axis=-1,
        keepdims=True,
    )
    grad_scores = (probs * (grad_probs - delta)).astype(bfloat)
    grad_queries = one_pair(dot_nn(grad_scores, key_rows)) * SCALE
    grad_keys = dot_tn(grad_scores, both)
    grad_values = dot_tn(probs.astype(bfloat), grad_both)
    return grad_queries.astype(bfloat), grad_keys.astype(bfloat), grad_values.astype(bfloat)


def put_logs(log_ref, rows, pair, log_total):
    count = log_total.shape[0] // 2
    lane = lax.broadcasted_iota(jnp.int32, (count, PAIR), 1)
    kept = log_ref[rows, :]
    kept = jnp.where(lane == 2 * pair, log_total[:count], kept)
    log_ref[rows, :] = jnp.where(lane == 2 * pair + 1, log_total[count:], kept)


def take_logs(log_ref, rows, pair):
    kept = log_ref[rows, :]
    lane = lax.broadcasted_iota(jnp.int32, kept.shape, 1)
    parts = [
        jnp.sum(jnp.where(lane == 2 * pair + i, kept, 0.0), axis=-1, keepdims=True)
        for i in range(2)
    ]
    return jnp.concatenate(parts, axis=0)


def in_parts(step, count, between):
    parts = len(between) + 1
    for i in range(parts):
        lax.fori_loop(count * i // parts, count * (i + 1) // parts, step, 0)
        if i < len(between):
            between[i]()


def attend_rows(q_ref, kv_ref, context_ref, log_ref, bias, rows, keys, between=()):
    width = q_ref.shape[1]
    key_start = kv_ref.shape[1] - 2 * width

    def step(pair, _):
        cols = tile_cols(pair, PAIR)
        key_cols = pl.ds(pl.multiple_of(key_start + pair * PAIR, PAIR), PAIR)
        value_cols = pl.ds(pl.multiple_of(key_start + width + pair * PAIR, PAIR), PAIR)
        context, log_total = attend_pair(
            q_ref[rows, cols], kv_ref[keys, key_cols], kv_ref[keys, value_cols], bias
        )
        context_ref[rows, cols] = context
        put_logs(log_ref, rows, pair, log_total)
        return 0

    in_parts(step, width // PAIR, between)


def attend_rows_back(
    q_ref, kv_ref, context_ref, log_ref, grad_ref, dq_ref, dkv_ref, bias, rows, keys, between=()
):
    width = q_ref.shape[1]
    key_start = kv_ref.shape[1] - 2 * width
    grad_start = dkv_ref.shape[1] - 2 * width

    def step(pair, _):
        cols = tile_cols(pair, PAIR)
        key_cols = pl.ds(pl.multiple_of(key_start + pair * PAIR, PAIR), PAIR)
        value_cols = pl.ds(pl.multiple_of(key_start + width + pair * PAIR, PAIR), PAIR)
        dq, dk, dv = attend_pair_back(
            q_ref[rows, cols],
            kv_ref[keys, key_cols],
            kv_ref[keys, value_cols],
            bias,
            take_logs(log_ref, rows, pair),
            context_ref[rows, cols],
            grad_ref[rows, cols],
        )
        dq_ref[rows, cols] = dq
        dkv_ref[keys, pl.ds(pl.multiple_of(grad_start + pair * PAIR, PAIR), PAIR)] = dk
        dkv_ref[keys, pl.ds(pl.multiple_of(grad_start + width + pair * PAIR, PAIR), PAIR)] = dv
        return 0

    in_parts(step, width // PAIR, between)


def allowed_bias(allowed):
    return jnp.where(allowed, 0.0, masked_score).astype(full)


def key_positions(me, bands, rows):
    lane = lax.broadcasted_iota(jnp.int32, (1, bands * rows), 1)
    part = sum((lane >= s * rows).astype(jnp.int32) for s in range(1, bands))
    return (part ^ me) * rows + lane - part * rows


def window_live(first, count, scalars, page_width):
    token = first + lax.broadcasted_iota(jnp.int32, (1, count), 1)
    window = lax.div(token, WIN * WIN)
    column = lax.rem(token, WIN) + WIN * lax.rem(window, page_width // WIN)
    return lax.rem(column + SHIFT, page_width) < scalars[1]


def copies_in(pairs, sems):
    copies = [pltpu.make_async_copy(src, dst, sems.at[i]) for i, (src, dst) in enumerate(pairs)]
    for copy in copies:
        copy.start()
    return copies


def low_shape(*shape):
    return jax.ShapeDtypeStruct(shape, bfloat)


def full_shape(*shape):
    return jax.ShapeDtypeStruct(shape, full)


def source_order(page_width, band_rows):
    tokens = band_rows * page_width
    token = np.arange(tokens)
    across = page_width // WIN
    window, inside = token // (WIN * WIN), token % (WIN * WIN)
    row = window // across * WIN + inside // WIN
    column = window % across * WIN + inside % WIN
    source = row * page_width + (column + SHIFT) % page_width
    order = np.zeros((tokens, tokens), np.float32)
    order[token, source] = 1.0
    return order


def fill_shifted(own_ref, arriving_ref, rows_ref):
    band_rows, width = own_ref.shape[1], own_ref.shape[2]
    for i in range(band_rows - SHIFT):
        rows_ref[i * width : (i + 1) * width, :] = own_ref[0, i + SHIFT].astype(full)
    for i in range(SHIFT):
        j = band_rows - SHIFT + i
        rows_ref[j * width : (j + 1) * width, :] = arriving_ref[i].astype(full)


def page_scalars(r):
    return None, r.page_cols[0], r.query_len[0], r.prompt_len[0]


def region_vectors(region_ref, w, page_width):
    size = WIN * WIN
    labels = region_ref[0].astype(full)
    band_rows = labels.shape[0]
    across = page_width // WIN
    first_row, first_col = w // across * WIN, w % across * WIN

    def at(shape, token_dim, start, divide):
        token = lax.broadcasted_iota(jnp.int32, shape, token_dim)
        place = lax.div(token, WIN) if divide else lax.rem(token, WIN)
        return place + start == lax.broadcasted_iota(jnp.int32, shape, 1 - token_dim)

    rows = at((size, band_rows), 0, first_row, True).astype(full)
    columns = at((size, page_width), 0, first_col, False)
    column = jnp.sum(jnp.where(columns, dot_nn(rows, labels), 0.0), axis=1, keepdims=True)
    rows = at((band_rows, size), 1, first_row, True).astype(full)
    columns = at((page_width, size), 1, first_col, False)
    row = jnp.sum(jnp.where(columns, dot_tn(labels, rows), 0.0), axis=0, keepdims=True)
    return column, row


def window_bias(scalars, region_ref, w, page_width):
    size = WIN * WIN
    live = window_live(w * size, size, scalars, page_width)
    own = lax.broadcasted_iota(jnp.int32, (size, size), 0)
    other = lax.broadcasted_iota(jnp.int32, (size, size), 1)
    column, row = region_vectors(region_ref, w, page_width)
    bias = allowed_bias((column == row) & ((own == other) | live))
    return jnp.concatenate([bias, bias], axis=0)


def self_bias(me, scalars, rows, bands):
    position = key_positions(me, bands, rows)
    own = me * rows + lax.broadcasted_iota(jnp.int32, (rows, 1), 0)
    bias = allowed_bias(
        (position < scalars[2]) & ((position <= own) | (position < scalars[3]))
    )
    return jnp.concatenate([bias, bias], axis=0)


def look_bias(dims, scalars):
    tokens, bands, page_width = dims["tokens"], dims["bands"], dims["page_width"]
    live = window_live(0, tokens, scalars, page_width)
    return jnp.concatenate([allowed_bias(live)] * bands, axis=1)


def read_bias(me, dims, scalars):
    return allowed_bias(key_positions(me, dims["bands"], dims["rows"]) < scalars[2])


class Kernel:
    def __init__(self, refs, hbm, sems):
        self.__dict__.update(refs)
        self.hbm, self.sems = hbm, sems
        self.coming, self.going = {}, []

    def fetch(self, *names):
        for name in names:
            copy = pltpu.make_async_copy(
                self.hbm[name], getattr(self, name), self.sems[name]
            )
            copy.start()
            self.coming[name] = copy

    def ready(self, *names):
        for name in names:
            self.coming.pop(name).wait()

    def save(self, *names):
        for name in names:
            copy = pltpu.make_async_copy(
                getattr(self, name), self.hbm[name], self.sems[name]
            )
            copy.start()
            self.going.append(copy)

    def finish(self):
        for copy in self.going:
            copy.wait()


def launch(body, given, staged, made, kept, scratch, collective, flops):
    sources = list(given) + list(staged)
    results = list(made) + list(kept)
    moved = list(staged) + list(kept)
    arrays = [given[n][0] for n in given] + [staged[n] for n in staged]
    stages = {n: pltpu.VMEM(staged[n].shape, staged[n].dtype) for n in staged}
    stages.update({n: pltpu.VMEM(kept[n].shape, kept[n].dtype) for n in kept})

    def inner(*refs):
        first, second = len(sources), len(sources) + len(results)
        outer = dict(zip(sources, refs[:first])) | dict(zip(results, refs[first:second]))
        inside = dict(zip(list(stages) + list(scratch), refs[second:-1]))
        sems = {n: refs[-1].at[i] for i, n in enumerate(moved)}
        body(Kernel(outer | inside, {n: outer[n] for n in moved}, sems))

    outs = pl.pallas_call(
        inner,
        out_shape=[made[n][0] for n in made] + [kept[n] for n in kept],
        in_specs=[given[n][1] for n in given] + [ANY] * len(staged),
        out_specs=[made[n][1] for n in made] + [ANY] * len(kept),
        scratch_shapes=list(stages.values())
        + list(scratch.values())
        + [pltpu.SemaphoreType.DMA((max(len(moved), 1),))],
        compiler_params=pltpu.CompilerParams(
            vmem_limit_bytes=62 * 2**20, collective_id=collective, has_side_effects=True
        ),
        cost_estimate=pl.CostEstimate(flops=flops, bytes_accessed=2**24, transcendentals=0),
    )(*arrays)
    return dict(zip(results, outs))


def hand_over(arrays):
    count = len(arrays)
    shapes = [a.shape if a.ndim < 4 else (a.shape[0], a.shape[3], a.shape[1] * a.shape[2]) for a in arrays]

    def body(*refs):
        for source, target in zip(refs[:count], refs[count:]):
            if source.shape == target.shape:
                target[...] = source[...]
            else:
                for k in range(source.shape[0]):
                    target[k] = source[k].reshape(target.shape[2], target.shape[1]).T

    return pl.pallas_call(
        body,
        out_shape=[jax.ShapeDtypeStruct(s, a.dtype) for s, a in zip(shapes, arrays)],
        in_specs=[VMEM] * count,
        out_specs=[VMEM] * count,
        compiler_params=pltpu.CompilerParams(vmem_limit_bytes=62 * 2**20),
    )(*arrays)


def greet(devices):
    barrier = pltpu.get_barrier_semaphore()
    for device in devices:
        pl.semaphore_signal(barrier, inc=1, device_id=device, device_id_type=MESH)
    pl.semaphore_wait(barrier, len(devices))


def other_band(step):
    me = lax.axis_index("row")
    if step == 1:
        return me + 1 - 2 * lax.rem(me, 2)
    return lax.rem(me + 2, 4) if step == 2 else 3 - me


def band_peers(bands):
    return [{"row": other_band(s)} for s in range(1, bands)]


class Gather:
    def __init__(self, slots, send, recv):
        self.slots, self.sems = slots, (send, recv)
        self.copies, self.waited = {}, set()
        self.copy(2, 0, 2)
        self.copy(1, 0, 1)

    def copy(self, place, source, step):
        send, recv = self.sems
        self.copies[place] = pltpu.make_async_remote_copy(
            src_ref=self.slots[source],
            dst_ref=self.slots[place],
            send_sem=send.at[place - 1],
            recv_sem=recv.at[place - 1],
            device_id={"row": other_band(step)},
            device_id_type=MESH,
        )
        self.copies[place].start()

    def ready(self, place):
        if place not in self.waited:
            self.waited.add(place)
            self.copies[place].wait_recv()

    def forward(self):
        self.ready(2)
        self.copy(3, 2, 1)

    def finish(self):
        for copy in self.copies.values():
            copy.wait_send()


def front_kernel(dims, r):
    page_width, bands, rows, tokens = (dims[n] for n in ("page_width", "bands", "rows", "tokens"))
    width = r.y0.shape[1]
    me = lax.axis_index("row")
    scalars = page_scalars(r)
    greet(band_peers(bands))
    loads = {}
    for a in range(3):
        for i, (name, ref) in enumerate((("wqkv%d", r.w_qkv), ("wout%d", r.w_out))):
            copy = pltpu.make_async_copy(
                ref.at[a], getattr(r, name % a), r.weight_sems.at[2 * a + i]
            )
            copy.start()
            loads[name % a] = copy
    above = {"row": lax.rem(me + bands - 1, bands)}
    halos = []
    for i, ref in enumerate((r.vis, r.cot)):
        halo = pltpu.make_async_remote_copy(
            src_ref=ref.at[0, 0:SHIFT],
            dst_ref=r.halo.at[i],
            send_sem=r.halo_send.at[i],
            recv_sem=r.halo_recv.at[i],
            device_id=above,
            device_id_type=MESH,
        )
        halo.start()
        halos.append(halo)
    r.hs[0] = norm_forward(r.y0[...].astype(full), r.gain[1:2, :], r.bias[1:2, :])
    self_rows = Gather([r.hs.at[s] for s in range(bands)], r.self_send, r.self_recv)

    r.log0[...] = jnp.zeros_like(r.log0)
    r.log1[...] = jnp.zeros_like(r.log1)
    r.log2[...] = jnp.zeros_like(r.log2)
    halos[0].wait()
    fill_shifted(r.vis, r.halo.at[0], r.cells)
    x0 = dot_nn(r.order[...], r.cells[...].astype(bfloat))
    r.x0[...] = x0.astype(bfloat)
    r.hv[...] = norm_forward(x0, r.gain[0:1, :], r.bias[0:1, :])
    r.save("x0", "hv")
    loads["wqkv0"].wait()
    r.q0[...] = (dot_nn(r.hv[...], r.wqkv0[:, :width]) * SCALE).astype(bfloat)
    matmul_into(r.kv0, r.hv, r.wqkv0.at[:, width:], width)
    r.save("q0", "kv0")
    size = WIN * WIN
    for w in range(tokens // size):
        part = slice(w * size, (w + 1) * size)
        bias = window_bias(scalars, r.region, w, page_width)
        attend_rows(r.q0, r.kv0, r.c0, r.log0, bias, part, part)
    self_rows.forward()
    r.save("c0", "log0")
    loads["wout0"].wait()
    x1 = r.x0[...].astype(full) + (dot_nn(r.c0[...], r.wout0[...]) + r.b_out[0:1, :])
    r.x1[...] = x1
    r.hl[0] = norm_forward(x1, r.gain[3:4, :], r.bias[3:4, :])
    look_rows = Gather([r.hl.at[s] for s in range(bands)], r.look_send, r.look_recv)
    r.save("x1")

    halos[1].wait()
    fill_shifted(r.cot, r.halo.at[1], r.cells)
    r.gx3[...] = dot_nn(r.order[...], r.cells[...].astype(bfloat)).astype(bfloat)
    r.save("gx3")
    loads["wqkv1"].wait()
    r.q1[...] = (dot_nn(r.hs[0], r.wqkv1[:, :width]) * SCALE).astype(bfloat)
    for s in range(1, bands):
        self_rows.ready(s)

    def project_self(s, _):
        part = pl.ds(pl.multiple_of(s * rows, rows), rows)
        r.kv1[part, :] = dot_nn(r.hs[s], r.wqkv1[:, width:]).astype(bfloat)
        return 0

    lax.fori_loop(0, bands, project_self, 0)
    r.save("hs", "q1", "kv1")
    bias = self_bias(me, scalars, rows, bands)
    attend_rows(r.q1, r.kv1, r.c1, r.log1, bias, slice(None), slice(None))
    look_rows.forward()
    r.save("c1", "log1")
    loads["wout1"].wait()
    y1 = r.y0[...].astype(full) + (dot_nn(r.c1[...], r.wout1[...]) + r.b_out[1:2, :])
    r.y1[...] = y1
    r.ha[...] = norm_forward(y1, r.gain[2:3, :], r.bias[2:3, :])
    loads["wqkv2"].wait()
    r.q2[...] = (dot_nn(r.ha[...], r.wqkv2[:, :width]) * SCALE).astype(bfloat)
    r.save("y1", "ha", "q2")

    for s in range(bands):
        if s:
            look_rows.ready(s)
        part = slice(s * tokens, (s + 1) * tokens)
        matmul_into(r.kv2.at[part], r.hl.at[s], r.wqkv2.at[:, width:], width)
    r.save("hl", "kv2")
    attend_rows(r.q2, r.kv2, r.c2, r.log2, look_bias(dims, scalars), slice(None), slice(None))
    loads["wout2"].wait()
    y2 = r.y1[...] + (dot_nn(r.c2[...], r.wout2[...]) + r.b_out[2:3, :])
    r.y2[...] = y2
    r.hm[...] = norm_forward(y2, r.gain[4:5, :], r.bias[4:5, :])
    r.save("c2", "log2", "y2", "hm")
    self_rows.finish()
    look_rows.finish()
    r.finish()


def split_blocks(dims, tile, grad, core):
    slab = dims["slab"]
    for block in range(dims["pages"]):
        tile[lax.rem(block + core, 2), block // 2] = grad[block * slab : (block + 1) * slab]


RING = 3


def page_place():
    page = lax.axis_index("page")
    core, x, y = lax.rem(page, 2), lax.rem(page // 2, 2), page // 4
    partners = (page + 1 - 2 * core, page + 2 - 4 * x, page + 4 - 8 * y)
    return (core, x, y), [{"page": p} for p in partners]


def remote(src, dst, send, recv, device):
    return pltpu.make_async_remote_copy(
        src_ref=src,
        dst_ref=dst,
        send_sem=send,
        recv_sem=recv,
        device_id=device,
        device_id_type=MESH,
    )


class Loads:
    def __init__(self, sems):
        self.sems, self.used = sems, 0

    def __call__(self, src, dst):
        copy = pltpu.make_async_copy(src, dst, self.sems.at[self.used])
        self.used += 1
        copy.start()
        return copy


class Reducer:
    def __init__(self, dims, r, loads):
        self.dims, self.r, self.loads = dims, r, loads
        (self.core, self.x, self.y), (self.other, self.along_x, self.along_y) = page_place()
        bands = dims["bands"]
        me = lax.axis_index("row")
        self.me = me
        self.next = me + 1 - 2 * lax.rem(me, 2)
        self.far = lax.rem(me + 2, bands)
        self.across = bands - 1 - me
        self.units, self.sent, self.outs, self.stages = 0, {}, {}, {}
        self.total_units = 32
        self.loading = {}


    def unit(self, fill):
        r, u = self.r, self.units
        slot = u % RING
        for copy in self.outs.pop(slot, []):
            copy.wait()
        fill(r.tile.at[slot])
        if u >= RING:
            pl.semaphore_wait(r.core_free, 1)
        self.sent[slot] = self.exchange(slot)
        self.sent[slot].start()
        self.units += 1
        return u

    def exchange(self, slot):
        r = self.r
        return remote(
            r.tile.at[slot, 1],
            r.landed.at[slot],
            r.core_send.at[slot],
            r.core_recv.at[slot],
            self.other,
        )

    def settle(self, u, targets):
        r, slot = self.r, u % RING
        self.sent.pop(slot).wait()
        r.tile[slot, 0] = r.tile[slot, 0] + r.landed[slot]
        if u + RING < self.total_units:
            pl.semaphore_signal(r.core_free, inc=1, device_id=self.other, device_id_type=MESH)
        outs = []
        for i, (part, target) in enumerate(targets):
            copy = pltpu.make_async_copy(r.tile.at[slot, 0, part], target, r.core_out.at[slot, i])
            copy.start()
            outs.append(copy)
        self.outs[slot] = outs

    def slab_targets(self, b, j):
        slab = self.dims["slab"]
        rows = pl.ds(j * slab, slab)
        return [(pl.ds(2 * y, 2), self.r.bags.at[b].at[y, :, rows]) for y in range(2)]

    def block_targets(self, b, j):
        slab = self.dims["slab"]
        return [
            (k, self.r.bags.at[b].at[j // 2, j % 2, pl.ds(k * slab, slab)])
            for k in range(self.dims["bands"])
        ]

    def flush(self, units=None):
        for slot in list(self.outs):
            if units is None or slot in [u % RING for u in units]:
                for copy in self.outs.pop(slot):
                    copy.wait()


    def start(self, b, stage, parts, which=(0, 1)):
        r = self.r
        for i, (src, dst, device) in enumerate(parts):
            if i in which:
                at = (b, 2 * stage + i)
                copy = remote(src, dst, r.stage_send.at[at], r.stage_recv.at[at], device)
                copy.start()
                self.stages.setdefault((b, stage), []).append(copy)

    def arrived(self, b, stage):
        for copy in self.stages.pop((b, stage)):
            copy.wait()

    def halves(self):
        height = self.r.recv1.shape[3]
        return pl.ds(0, height), pl.ds(height, height)

    def landing1(self, b, half):
        r = self.r
        if b < 7:
            return r.recv1.at[b, half]
        return r.arena.at[2 * half : 2 * half + 2, : r.recv1.shape[3]]

    def landing2(self, b, half):
        r = self.r
        height = r.recv1.shape[3]
        if b < 7:
            return r.recv2.at[b, half]
        return r.arena.at[half, height : 2 * height]

    def came2(self, b):
        if b < 7:
            return [self.r.came.at[b % 2, half, 0] for half in range(2)]
        return [self.landing2(b, half) for half in range(2)]

    def load_own(self, b):
        r, slot = self.r, b % 2
        top, bottom = self.halves()
        bag = r.bags.at[b]
        self.loading[b] = [
            self.loads(bag.at[:, self.x, top], r.sums.at[slot, 0]),
            self.loads(bag.at[self.y, :, bottom], r.sums.at[slot, 1]),
        ]

    def free_arena(self):
        for i, device in enumerate((self.along_x, self.along_y)):
            pl.semaphore_signal(
                self.r.arena_free.at[i], inc=1, device_id=device, device_id_type=MESH
            )

    def first(self, b, half=None):
        r = self.r
        if b == 7:
            for i in (0, 1) if half is None else (half,):
                pl.semaphore_wait(r.arena_free.at[i], 1)
        top, bottom = self.halves()
        bag = r.bags.at[b]
        parts = [
            (bag.at[:, 1 - self.x, top], self.landing1(b, 0), self.along_x),
            (bag.at[1 - self.y, :, bottom], self.landing1(b, 1), self.along_y),
        ]
        self.start(b, 0, parts, [0, 1] if half is None else [half])

    def load_second(self, *bags):
        r = self.r
        for b in bags:
            if b not in self.loading:
                self.load_own(b)
            self.arrived(b, 0)
            if b < 7:
                self.loading[b].append(self.loads(r.recv1.at[b], r.came.at[b % 2]))

    def second(self, *bags):
        r = self.r
        for b in bags:
            slot = b % 2
            wait_all(self.loading.pop(b))
            if b < 7:
                r.sums[slot] = r.sums[slot] + r.came[slot]
            else:
                for half in range(2):
                    r.sums[slot, half] = r.sums[slot, half] + self.landing1(b, half)[...]
            self.start(
                b,
                1,
                [
                    (r.sums.at[slot, 0, 1 - self.y], self.landing2(b, 0), self.along_y),
                    (r.sums.at[slot, 1, 1 - self.x], self.landing2(b, 1), self.along_x),
                ],
            )

    def load_third(self, *bags):
        r = self.r
        for b in bags:
            self.arrived(b, 1)
            self.loading[b] = []
            if b < 7:
                self.loading[b].append(self.loads(r.recv2.at[b], r.came.at[b % 2, :, 0]))

    def third(self, *bags):
        r = self.r
        for b in bags:
            slot = b % 2
            wait_all(self.loading.pop(b))
            top, bottom = self.came2(b)
            self.cut(b, r.sums[slot, 0, self.y] + top[...], r.sums[slot, 1, self.x] + bottom[...])
            self.start(
                b,
                2,
                [
                    (r.pieces.at[b % 4, self.next], r.recv3.at[b, 0], {"row": self.next}),
                    (r.pieces.at[b % 4, self.across], r.recv3.at[b, 1], {"row": self.next}),
                ],
            )

    def cut(self, b, top, bottom):
        r, slab, bands = self.r, self.dims["slab"], self.dims["bands"]
        width = top.shape[1]
        size = width // bands
        parts = [half[k * slab : (k + 1) * slab] for half in (top, bottom) for k in range(2)]
        if b in (0, 2):
            made = parts
        elif b in (1, 3):
            made = [
                jnp.concatenate([p[:, z * size : (z + 1) * size] for p in parts], axis=1)
                for z in range(bands)
            ]
        else:
            rest = jnp.concatenate(parts[1:], axis=1)
            made = [
                jnp.concatenate(
                    [
                        parts[0][:, z * size : (z + 1) * size],
                        rest[:, 3 * z * size : 3 * (z + 1) * size],
                    ],
                    axis=1,
                )
                for z in range(bands)
            ]
        for z in range(bands):
            r.pieces[b % 4, z] = made[z]

    def fourth(self, *bags):
        r = self.r
        for b in bags:
            slot = b % 2
            self.arrived(b, 2)
            r.last[b % 4, 0] = r.pieces[b % 4, self.me] + r.recv3[b, 0]
            r.last[b % 4, 1] = r.pieces[b % 4, self.far] + r.recv3[b, 1]
            self.start(b, 3, [(r.last.at[b % 4, 1], r.recv4.at[b], {"row": self.far})], [0])

    def store(self, name, target, value):
        scratch = getattr(self.r, name)
        for copy in self.loading.pop(name, ()):
            copy.wait()
        scratch[...] = value
        self.loading[name] = [self.loads(scratch, target)]

    def end(self, *bags):
        r, slab, bands = self.r, self.dims["slab"], self.dims["bands"]
        for b in bags:
            self.arrived(b, 3)
            total = r.last[b % 4, 0].astype(full) + r.recv4[b].astype(full)
            size = total.shape[1] // bands
            if b in (0, 2):
                self.store("final_up", r.wup.at[1 - b // 2], total)
            elif b in (1, 3):
                parts = [total[:, k * size : (k + 1) * size] for k in range(bands)]
                self.store("final_down", r.wdown.at[1 - b // 2], jnp.stack(parts))
            else:
                self.store("final_out", r.wout.at[7 - b], total[:, :size])
                self.store("final_qkv", r.wqkv.at[7 - b], total[:, size:])

    def finish(self):
        for copies in self.loading.values():
            wait_all(copies)


def layer_loads(r, loads, layer, arena):
    width = arena.shape[1]
    copies = [
        loads(r.w_qkv.at[layer, :, i * width : (i + 1) * width], arena.at[i]) for i in range(3)
    ]
    return copies + [loads(r.w_out.at[layer], arena.at[3])]


def wait_all(copies):
    for copy in copies:
        copy.wait()


def project_pair_into(kv_ref, into_ref, arena, start, count):
    width = arena.shape[1]
    part = slice(start, start + count)
    kv_ref[part, :width] = dot_nn(into_ref[part, :], arena[1]).astype(bfloat)
    kv_ref[part, width:] = dot_nn(into_ref[part, :], arena[2]).astype(bfloat)


class Quarters:
    def __init__(self, r, loads, arena):
        self.r, self.loads, self.arena = r, loads, arena
        self.coming = {}

    def load(self, stream, j):
        r, width = self.r, self.arena.shape[1]
        cols = pl.ds(j * width, width)
        pair = 2 * (j % 2)
        self.coming[stream, j] = [
            self.loads(r.w_up.at[stream, :, cols], self.arena.at[pair]),
            self.loads(r.w_down.at[stream, cols, :], self.arena.at[pair + 1]),
        ]

    def ready(self, stream, j):
        wait_all(self.coming.pop((stream, j)))
        pair = 2 * (j % 2)
        return self.arena.at[pair], self.arena.at[pair + 1]


def feed_both_ways(dims, r, red, quarters, stream, norm, values, cot, hidden_ref, total, back, kept, after):
    bands = dims["bands"]
    width = values.shape[1]
    row_out, row_up, row_down, row_gain, row_bias = vec_rows(dims)
    hidden_ref[...] = norm_forward(values[...], r.gain[norm : norm + 1, :], r.bias[norm : norm + 1, :])
    total[...] = values[...] + r.b_down[stream : stream + 1, :]
    back[...] = jnp.zeros_like(back)
    r.vec[row_down + stream : row_down + stream + 1, :] = jnp.sum(
        cot[...].astype(full), axis=0, keepdims=True
    )
    row_up = row_up + stream * bands
    units = FeedUnits(dims, red, 2 * (1 - stream))
    for j in range(bands):
        up, down = quarters.ready(stream, j)
        z = dot_nn(hidden_ref[...], up[...]) + r.b_up[stream : stream + 1, j * width : (j + 1) * width]
        square = z * z
        bend = jnp.tanh(0.7978845608028654 * (z + 0.044715 * (square * z)))
        half = 0.5 * (1.0 + bend)
        slope = half + (0.5 * z) * (1.0 - bend * bend) * (
            0.7978845608028654 * (1.0 + 0.134145 * square)
        )
        active = (z * half).astype(bfloat)
        total[...] += dot_nn(active, down[...])
        dz = dot_nt(cot[...], down[...]) * slope
        r.vec[row_up + j : row_up + j + 1, :] = jnp.sum(dz, axis=0, keepdims=True)
        dz = dz.astype(bfloat)
        back[...] += dot_nt(dz, up[...])
        if j + 2 < bands:
            quarters.load(stream, j + 2)
        if kept is None:
            units.quarter(j, hidden_ref[...], dz, active, cot[...])
        else:
            kept[j][0][...] = dz
            kept[j][1][...] = active
        after(j)
    if kept is None:
        units.finish()


class FeedUnits:
    def __init__(self, dims, red, bag):
        self.dims, self.red, self.bag = dims, red, bag
        self.waiting = []

    def quarter(self, j, hidden, dz, active, low_grad):
        dims, red = self.dims, self.red
        bands, slab = dims["bands"], dims["slab"]
        deep = bands * slab
        up_grad = dot_tn(hidden, dz).astype(bfloat)
        unit = red.unit(lambda tile: split_blocks(dims, tile, up_grad, red.core))
        self.waiting.append((unit, red.slab_targets(self.bag, j)))
        if len(self.waiting) > 1:
            red.settle(*self.waiting.pop(0))
        down_grad = dot_tn(active, low_grad).astype(bfloat)

        def fill(tile):
            for side in range(2):
                part = down_grad[side * deep : (side + 1) * deep]
                for k in range(bands):
                    tile[lax.rem(side + red.core, 2), k] = part[k * slab : (k + 1) * slab]

        unit = red.unit(fill)
        self.waiting.append((unit, red.block_targets(self.bag + 1, j)))
        red.settle(*self.waiting.pop(0))

    def finish(self):
        for item in self.waiting:
            self.red.settle(*item)
        self.red.flush()


def feed_end(dims, r, norm, values, cot, back):
    row_out, row_up, row_down, row_gain, row_bias = vec_rows(dims)
    pull, gain, bias = norm_backward(back[...], values[...], r.gain[norm : norm + 1, :])
    r.vec[row_gain + norm : row_gain + norm + 1, :] = gain
    r.vec[row_bias + norm : row_bias + norm + 1, :] = bias
    return cot[...].astype(full) + pull


def pair_back(dkv_ref, arena, start, count):
    width = arena.shape[1]
    part = slice(start, start + count)
    return dot_nt(dkv_ref[part, :width], arena[1]) + dot_nt(dkv_ref[part, width:], arena[2])


class Scatter:
    def __init__(self, dkv_ref, arena, count, parts, landing, send, recv):
        self.parts, self.landing, self.sems = parts, landing, (send, recv)
        self.copies = []
        parts[2] = pair_back(dkv_ref, arena, 3 * count, count).astype(bfloat)
        self.copy(2, 2, 1)
        parts[0] = pair_back(dkv_ref, arena, count, count).astype(bfloat)
        self.copy(0, 0, 1)
        parts[1] = pair_back(dkv_ref, arena, 2 * count, count).astype(bfloat)
        self.own = lambda: pair_back(dkv_ref, arena, 0, count)

    def copy(self, part, place, step):
        send, recv = self.sems
        copy = remote(
            self.parts.at[part],
            self.landing.at[place],
            send.at[place],
            recv.at[place],
            {"row": other_band(step)},
        )
        copy.start()
        self.copies.append(copy)

    def forward(self):
        self.copies.pop(0).wait()
        self.parts[1] = self.parts[1] + self.landing[2]
        self.copy(1, 1, 2)

    def total(self, own):
        wait_all(self.copies)
        return own + self.landing[0].astype(full) + self.landing[1].astype(full)


def weight_units(dims, r, red, b, context, low, from_rows, into_rows, dq, dkv, between=None):
    width = r.tile.shape[-1]
    sides = [
        lambda: dot_tn(context[...], low[...]),
        lambda: dot_tn(from_rows[...], dq[...]),
        lambda: dot_tn(into_rows[...], dkv[:, :width]),
        lambda: dot_tn(into_rows[...], dkv[:, width:]),
    ]
    units = []
    for j, side in enumerate(sides):
        grad = side().astype(bfloat)
        units.append(red.unit(lambda tile: split_blocks(dims, tile, grad, red.core)))
        if j:
            red.settle(units[j - 1], red.slab_targets(b, j - 1))
        if j == 2 and between:
            between()
        if j == 3:
            red.flush(units[:2])
            red.first(b, 0)
    red.settle(units[-1], red.slab_targets(b, 3))
    red.flush()
    red.first(b, 1)


def vec_rows(dims):
    quarters = dims["bands"]
    return 0, 4, 4 + 2 * quarters, 6 + 2 * quarters, 13 + 2 * quarters


def put_vectors(dims, r):
    bands, slab, pages = dims["bands"], dims["slab"], dims["pages"]
    row_out, row_up, row_down, row_gain, row_bias = vec_rows(dims)
    width = r.vec.shape[1]
    page = lax.axis_index("page")
    own = pltpu.roll(r.vec[...], lax.rem(width - page * slab, width), 1)[:, :slab]
    r.bout[...] = own[row_out:row_up]
    r.bdown[...] = own[row_down:row_gain]
    r.gain_grad[...] = own[row_gain:row_bias]
    r.bias_grad[...] = own[row_bias : row_bias + 7]
    hidden = bands * slab
    per_row = pages // bands
    row, shift = page // per_row, lax.rem(page, per_row) * hidden
    for stream in range(2):
        start = row_up + stream * bands
        chosen = jnp.zeros((1, width), full)
        for k in range(bands):
            chosen = chosen + jnp.where(row == k, r.vec[start + k : start + k + 1, :], 0.0)
        r.bup[stream : stream + 1, :] = jnp.where(
            shift == 0, chosen[:, :hidden], chosen[:, width - hidden :]
        )


def back_kernel(dims, r):
    page_width, bands, rows, tokens = (dims[n] for n in ("page_width", "bands", "rows", "tokens"))
    slab = dims["slab"]
    width = r.f1.shape[1]
    me = lax.axis_index("row")
    scalars = page_scalars(r)
    loads = Loads(r.load_sems)
    red = Reducer(dims, r, loads)
    row_out, row_up, row_down, row_gain, row_bias = vec_rows(dims)
    hm_load = loads(r.hm_hbm, r.into.at[0:rows])
    y2_load = [loads(r.y2_hbm, r.y2), loads(r.gy3_hbm, r.dq_s)]
    quarters = Quarters(r, loads, r.arena)
    quarters.load(1, 0)
    quarters.load(1, 1)
    greet(band_peers(bands) + [red.other, red.along_x, red.along_y])
    hm_load.wait()
    memo = Gather([r.into.at[s * rows : (s + 1) * rows] for s in range(bands)], r.hm_send, r.hm_recv)
    weights3 = layer_loads(r, loads, 3, r.att)
    hl_load = loads(r.hl_hbm.at[0], r.from_rows)
    x1_load = loads(r.x1_hbm, r.f1)
    gx3_load = loads(r.gx3_hbm, r.cot)
    small = [
        loads(src, dst)
        for src, dst in (
            (r.q2_hbm, r.q2),
            (r.c2_hbm, r.c2),
            (r.log2_hbm, r.log2),
            (r.q1_hbm, r.q1),
            (r.c1_hbm, r.c1),
            (r.log1_hbm, r.log1),
            (r.ha_hbm, r.ha),
            (r.y1_hbm, r.y1),
        )
    ]
    r.vec[...] = jnp.zeros_like(r.vec)

    wait_all(y2_load)

    def after_query(j):
        if j == 2:
            memo.forward()
            red.flush()
            red.first(0, 0)

    feed_both_ways(
        dims, r, red, quarters, 1, 6, r.y2, r.dq_s, r.grad_s, r.own_m, r.gy, None, after_query
    )
    red.first(0, 1)
    red.first(1)
    quarters.load(0, 0)
    quarters.load(0, 1)
    r.query_out[...] = r.own_m[...].astype(bfloat)
    r.gy[...] = feed_end(dims, r, 6, r.y2, r.dq_s, r.gy)

    every = slice(None)
    few = slice(0, bands * rows)
    hl_load.wait()
    wait_all(weights3)
    r.q[...] = (dot_nn(r.from_rows[...], r.att[0]) * SCALE).astype(bfloat)
    project_pair_into(r.kv, r.into, r.att, 0, rows)
    for s in range(1, bands):
        memo.ready(s)
        project_pair_into(r.kv, r.into, r.att, s * rows, rows)
    bias = read_bias(me, dims, scalars)
    memo.finish()
    r.log[...] = jnp.zeros_like(r.log)
    attend_rows(r.q, r.kv, r.context, r.log, bias, every, few)
    x1_load.wait()
    r.f2[...] = r.f1[...] + (dot_nn(r.context[...], r.att[3]) + r.b_out[3:4, :])

    gx3_load.wait()

    def after_patches(j):
        if j == bands - 1:
            red.load_second(0, 1)

    spare = slice(bands * rows, bands * rows + tokens)
    places = [r.parts_l.at[0], r.parts_l.at[1], r.parts_l.at[2], r.into.at[spare]]
    for ref in (r.kv, r.dkv):
        places += [ref.at[spare, :width], ref.at[spare, width:]]
    kept = [(places[2 * j], places[2 * j + 1]) for j in range(bands)]
    feed_both_ways(
        dims, r, red, quarters, 0, 5, r.f2, r.cot, r.hidden, r.f3, r.f4, kept, after_patches
    )
    red.second(0, 1)
    weights2 = layer_loads(r, loads, 2, r.arena)
    to_right = {"row": lax.rem(me + 1, bands)}
    moved = dot_tn(r.order[...], r.f3[...].astype(bfloat)).astype(bfloat)
    stay = tokens - SHIFT * page_width
    r.vis_out[tokens - stay :, :] = moved[:stay]
    r.halo_low[...] = moved[stay:]
    halo = remote(
        r.halo_low, r.vis_out.at[: tokens - stay], r.halo_send.at[0], r.halo_recv.at[0], to_right
    )
    halo.start()
    gx2 = feed_end(dims, r, 5, r.f2, r.cot, r.f4)
    r.f5[...] = gx2

    low = gx2.astype(bfloat)
    r.low[...] = low
    r.vec[row_out + 3 : row_out + 4, :] = jnp.sum(low.astype(full), axis=0, keepdims=True)
    r.grad[...] = dot_nt(low, r.att[3]).astype(bfloat)
    attend_rows_back(r.q, r.kv, r.context, r.log, r.grad, r.dq, r.dkv, bias, every, few)
    memo_back = Scatter(r.dkv, r.att, rows, r.parts_m, r.got_m, r.memo_send, r.memo_recv)
    r.own_m[...] = memo_back.own()
    r.f4[...] = dot_nt(r.dq[...], r.att[0])
    weights0 = layer_loads(r, loads, 0, r.att)
    few_dkv, few_into = r.dkv.at[0 : bands * rows], r.into.at[0 : bands * rows]
    units = FeedUnits(dims, red, 2)
    for j in range(bands):
        if j == 0:
            red.load_third(0, 1)
        units.quarter(j, r.hidden[...], kept[j][0][...], kept[j][1][...], r.cot[...])
        if j < 2:
            red.third(j)
        if j == 2:
            memo_back.forward()
            red.flush()
            red.first(2, 0)
    units.finish()
    red.first(2, 1)
    red.first(3)
    kv_load = loads(r.kv2_hbm, r.kv)
    weight_units(dims, r, red, 4, r.context, r.low, r.from_rows, few_into, r.dq, few_dkv)
    late = [
        loads(r.hl_all_hbm, r.into),
        loads(r.q0_hbm, r.q),
        loads(r.c0_hbm, r.context),
        loads(r.log0_hbm, r.log),
        loads(r.hv_hbm, r.from_rows),
        loads(r.x1_hbm, r.f1),
        loads(r.x0_hbm, r.cot),
    ]

    wait_all(small)
    dhm = memo_back.total(r.own_m[...])
    red.fourth(0, 1)
    pull, gain4, bias4 = norm_backward(
        dhm,
        r.y2[...],
        r.gain[4:5, :],
    )
    r.vec[row_gain + 4 : row_gain + 5, :] = gain4
    r.vec[row_bias + 4 : row_bias + 5, :] = bias4
    gy = r.gy[...] + pull
    r.gy[...] = gy
    low = gy.astype(bfloat)
    r.low_s[...] = low
    r.vec[row_out + 2 : row_out + 3, :] = jnp.sum(low.astype(full), axis=0, keepdims=True)
    wait_all(weights2)
    r.grad_s[...] = dot_nt(low, r.arena[3]).astype(bfloat)
    kv_load.wait()
    attend_rows_back(
        r.q2,
        r.kv,
        r.c2,
        r.log2,
        r.grad_s,
        r.dq_s,
        r.dkv,
        look_bias(dims, scalars),
        every,
        every,
    )
    kv_load = loads(r.kv1_hbm, r.kv.at[0 : bands * rows])
    look_back = Scatter(r.dkv, r.arena, tokens, r.parts_l, r.got_l, r.look_send, r.look_recv)
    r.f4[...] += look_back.own()
    pull, gain2, bias2 = norm_backward(dot_nt(r.dq_s[...], r.arena[0]), r.y1[...], r.gain[2:3, :])
    r.vec[row_gain + 2 : row_gain + 3, :] = gain2
    r.vec[row_bias + 2 : row_bias + 3, :] = bias2
    r.gy[...] += pull
    weights1 = layer_loads(r, loads, 1, r.arena)
    wait_all(late)
    red.end(0, 1)
    weight_units(
        dims, r, red, 5, r.c2, r.low_s, r.ha, r.into, r.dq_s, r.dkv, lambda: red.load_second(2, 3)
    )
    red.second(2, 3)
    hidden_load = loads(r.hs_hbm, r.into.at[0 : bands * rows])
    look_back.forward()

    low = r.gy[...].astype(bfloat)
    r.low_s[...] = low
    r.vec[row_out + 1 : row_out + 2, :] = jnp.sum(low.astype(full), axis=0, keepdims=True)
    wait_all(weights1)
    r.grad_s[...] = dot_nt(low, r.arena[3]).astype(bfloat)
    kv_load.wait()
    bias = self_bias(me, scalars, rows, bands)
    attend_rows_back(r.q1, r.kv, r.c1, r.log1, r.grad_s, r.dq_s, r.dkv, bias, every, few)
    kv_load = loads(r.kv0_hbm, r.kv.at[0:tokens])
    self_back = Scatter(r.dkv, r.arena, rows, r.parts_m, r.got_s, r.self_send, r.self_recv)
    r.own_m[...] = self_back.own() + dot_nt(r.dq_s[...], r.arena[0])
    red.free_arena()
    hidden_load.wait()
    weight_units(
        dims, r, red, 6, r.c1, r.low_s, r.into.at[0:rows], few_into, r.dq_s, few_dkv
    )

    self_back.forward()
    red.load_third(2, 3)
    red.third(2, 3)
    red.load_second(4)
    dhl = look_back.total(r.f4[...])
    red.second(4)
    pull, gain3, bias3 = norm_backward(
        dhl,
        r.f1[...],
        r.gain[3:4, :],
    )
    r.vec[row_gain + 3 : row_gain + 4, :] = gain3
    r.vec[row_bias + 3 : row_bias + 4, :] = bias3
    gx1 = r.f5[...] + pull
    r.f5[...] = gx1
    low = gx1.astype(bfloat)
    r.low[...] = low
    r.vec[row_out : row_out + 1, :] = jnp.sum(low.astype(full), axis=0, keepdims=True)
    wait_all(weights0)
    r.grad[...] = dot_nt(low, r.att[3]).astype(bfloat)
    kv_load.wait()
    size = WIN * WIN
    for w in range(tokens // size):
        part = slice(w * size, (w + 1) * size)
        bias = window_bias(scalars, r.region, w, page_width)
        attend_rows_back(
            r.q, r.kv, r.context, r.log, r.grad, r.dq, r.dkv, bias, part, part
        )
    red.load_second(5)
    dr = pair_back(r.dkv, r.att, 0, tokens) + dot_nt(r.dq[...], r.att[0])
    pull, gain0, bias0 = norm_backward(dr, r.cot[...].astype(full), r.gain[0:1, :])
    r.vec[row_gain : row_gain + 1, :] = gain0
    r.vec[row_bias : row_bias + 1, :] = bias0
    gx0 = r.f5[...] + pull
    high = gx0.astype(bfloat)
    rest = (gx0 - high.astype(full)).astype(bfloat)
    moved = dot_tn(r.order[...], high) + dot_tn(r.order[...], rest)
    r.vis_grad[tokens - stay :, :] = moved[:stay]
    r.f2[: tokens - stay, :] = moved[stay:]
    halo_back = remote(
        r.f2.at[: tokens - stay], r.vis_grad.at[: tokens - stay], r.halo_send.at[1], r.halo_recv.at[1], to_right
    )
    halo_back.start()
    red.second(5)
    weight_units(
        dims, r, red, 7, r.context, r.low, r.from_rows, r.from_rows, r.dq, r.dkv.at[0:tokens]
    )
    red.fourth(2, 3)

    pull, gain1, bias1 = norm_backward(
        self_back.total(r.own_m[...]),
        r.y0[...].astype(full),
        r.gain[1:2, :],
    )
    r.query_grad[...] = r.gy[...] + pull
    r.vec[row_gain + 1 : row_gain + 2, :] = gain1
    r.vec[row_bias + 1 : row_bias + 2, :] = bias1

    def swap(i, device):
        copy = remote(r.vec, r.vec_in.at[i], r.vec_send.at[i], r.vec_recv.at[i], device)
        copy.start()
        return copy

    def add(i, copy):
        copy.wait()
        r.vec[...] = r.vec[...] + r.vec_in[i]

    copy = swap(0, red.other)
    red.load_third(4)
    red.third(4)
    add(0, copy)
    copy = swap(1, {"row": red.next})
    red.load_second(6)
    red.second(6)
    add(1, copy)
    copy = swap(2, {"row": red.far})
    red.load_third(5)
    red.third(5)
    red.load_own(7)
    add(2, copy)
    copy = swap(3, red.along_x)
    red.fourth(4)
    red.end(2, 3)
    red.load_second(7)
    red.second(7)
    add(3, copy)
    copy = swap(4, red.along_y)
    red.fourth(5)
    red.load_third(6)
    red.third(6)
    red.end(4)
    add(4, copy)
    put_vectors(dims, r)
    red.fourth(6)
    red.load_third(7)
    red.third(7)
    red.end(5)
    red.fourth(7)
    red.end(6)
    red.end(7)
    halo.wait()
    halo_back.wait()
    red.finish()


def shards(
    vis_stream,
    query_stream,
    w_qkv,
    w_out,
    b_out,
    w_up,
    b_up,
    w_down,
    b_down,
    norm_gain,
    norm_bias,
    page_cols,
    query_len,
    prompt_len,
    region_ids,
    vis_cotangent,
    query_cotangent,
):
    band_rows, page_width, width = vis_stream.shape[1:]
    tokens = band_rows * page_width
    rows = query_stream.shape[1]
    bands, pages = lax.axis_size("row"), lax.axis_size("page")
    me = lax.axis_index("row")
    hidden_units = w_up.shape[2]
    slab = width // pages
    dims = dict(
        page_width=page_width,
        bands=bands,
        tokens=tokens,
        rows=rows,
        pages=pages,
        slab=slab,
    )
    qkv_any, out_any = (w_qkv, ANY), (w_out, ANY)
    log_lanes = full_shape(tokens, PAIR)
    y0, gy3 = query_stream[0], query_cotangent[0]
    lengths = dict(
        page_cols=(page_cols, SMEM), query_len=(query_len, SMEM), prompt_len=(prompt_len, SMEM)
    )
    order = jnp.asarray(source_order(page_width, band_rows), bfloat)

    given = dict(
        **lengths,
        vis=(vis_stream, VMEM),
        cot=(vis_cotangent, VMEM),
        y0=(y0, VMEM),
        order=(order, VMEM),
        region=(region_ids, VMEM),
        gain=(norm_gain, VMEM),
        bias=(norm_bias, VMEM),
        b_out=(b_out, VMEM),
        w_qkv=qkv_any,
        w_out=out_any,
    )
    weight = {}
    for a in range(3):
        weight["wqkv%d" % a] = pltpu.VMEM((width, 3 * width), bfloat)
        weight["wout%d" % a] = pltpu.VMEM((width, width), bfloat)
    pair_sems = pltpu.SemaphoreType.DMA((2,))
    peer_sems = pltpu.SemaphoreType.DMA((bands - 1,))
    front = launch(
        partial(front_kernel, dims),
        given,
        {},
        {},
        dict(
            x0=low_shape(tokens, width),
            hv=low_shape(tokens, width),
            q0=low_shape(tokens, width),
            kv0=low_shape(tokens, 2 * width),
            c0=low_shape(tokens, width),
            log0=log_lanes,
            x1=full_shape(tokens, width),
            gx3=low_shape(tokens, width),
            hs=low_shape(bands, rows, width),
            q1=low_shape(rows, width),
            kv1=low_shape(bands * rows, 2 * width),
            c1=low_shape(rows, width),
            log1=full_shape(rows, PAIR),
            y1=full_shape(rows, width),
            ha=low_shape(rows, width),
            q2=low_shape(rows, width),
            hl=low_shape(bands, tokens, width),
            kv2=low_shape(bands * tokens, 2 * width),
            c2=low_shape(rows, width),
            log2=full_shape(rows, PAIR),
            y2=full_shape(rows, width),
            hm=low_shape(rows, width),
        ),
        dict(
            cells=pltpu.VMEM((tokens, width), full),
            halo=pltpu.VMEM((2, SHIFT, page_width, width), bfloat),
            halo_send=pair_sems,
            halo_recv=pair_sems,
            self_send=peer_sems,
            self_recv=peer_sems,
            look_send=peer_sems,
            look_recv=peer_sems,
            weight_sems=pltpu.SemaphoreType.DMA((6,)),
            **weight,
        ),
        0,
        40 * tokens * width * width,
    )
    hbm = {
        "x1_hbm": front["x1"],
        "x0_hbm": front["x0"],
        "gx3_hbm": front["gx3"],
        "hv_hbm": front["hv"],
        "hl_hbm": front["hl"],
        "hl_all_hbm": front["hl"].reshape(bands * tokens, width),
        "hs_hbm": front["hs"].reshape(bands * rows, width),
        "ha_hbm": front["ha"],
        "hm_hbm": front["hm"],
        "y1_hbm": front["y1"],
        "y2_hbm": front["y2"],
        "gy3_hbm": gy3,
        "w_qkv": w_qkv,
        "w_out": w_out,
        "w_up": w_up,
        "w_down": w_down,
    }
    for a in range(3):
        for name in ("q", "kv", "c", "log"):
            hbm["%s%d_hbm" % (name, a)] = front["%s%d" % (name, a)]
    near = dict(
        y0=y0,
        order=order,
        region=region_ids,
        gain=norm_gain,
        bias=norm_bias,
        b_out=b_out,
        b_up=b_up,
        b_down=b_down,
    )
    height = bands * slab
    halo_rows = SHIFT * page_width
    vec_shape = full_shape(vec_rows(dims)[-1] + 11, width)
    wide = lambda count: pltpu.VMEM((count, width), full)
    narrow = lambda count: pltpu.VMEM((count, width), bfloat)
    dma = pltpu.SemaphoreType.DMA
    scratch = dict(
        att=pltpu.VMEM((4, width, width), bfloat),
        arena=pltpu.VMEM((4, width, width), bfloat),
        tile=pltpu.VMEM((RING, 2, pages // 2, slab, width), bfloat),
        landed=pltpu.VMEM((RING, pages // 2, slab, width), bfloat),
        sums=pltpu.VMEM((2, 2, 2, height // 2, width), bfloat),
        came=pltpu.VMEM((2, 2, 2, height // 2, width), bfloat),
        pieces=pltpu.VMEM((4, bands, slab, width), bfloat),
        last=pltpu.VMEM((4, 2, slab, width), bfloat),
        hidden=narrow(tokens),
        recv3=pltpu.VMEM((8, 2, slab, width), bfloat),
        recv4=pltpu.VMEM((8, slab, width), bfloat),
        final_up=wide(slab),
        final_down=pltpu.VMEM((bands, slab, width // bands), full),
        final_out=pltpu.VMEM((slab, width // bands), full),
        final_qkv=pltpu.VMEM((slab, 3 * width // bands), full),
        q=narrow(tokens),
        kv=pltpu.VMEM((bands * tokens, 2 * width), bfloat),
        context=narrow(tokens),
        log=pltpu.VMEM((tokens, PAIR), full),
        grad=narrow(tokens),
        dq=narrow(tokens),
        dkv=pltpu.VMEM((bands * tokens, 2 * width), bfloat),
        low=narrow(tokens),
        cot=narrow(tokens),
        from_rows=narrow(tokens),
        into=narrow(bands * tokens),
        f1=wide(tokens),
        f2=wide(tokens),
        f3=wide(tokens),
        f4=wide(tokens),
        f5=wide(tokens),
        q2=narrow(rows),
        c2=narrow(rows),
        q1=narrow(rows),
        c1=narrow(rows),
        log2=pltpu.VMEM((rows, PAIR), full),
        log1=pltpu.VMEM((rows, PAIR), full),
        ha=narrow(rows),
        low_s=narrow(rows),
        grad_s=narrow(rows),
        dq_s=narrow(rows),
        y1=wide(rows),
        y2=wide(rows),
        gy=wide(rows),
        own_m=wide(rows),
        parts_m=pltpu.VMEM((bands - 1, rows, width), bfloat),
        parts_l=pltpu.VMEM((bands - 1, tokens, width), bfloat),
        got_m=pltpu.VMEM((bands - 1, rows, width), bfloat),
        got_l=pltpu.VMEM((bands - 1, tokens, width), bfloat),
        got_s=pltpu.VMEM((bands - 1, rows, width), bfloat),
        halo_low=narrow(halo_rows),
        vec=pltpu.VMEM(vec_shape.shape, full),
        vec_in=pltpu.VMEM((5,) + vec_shape.shape, full),
        load_sems=dma((192,)),
        core_send=dma((RING,)),
        core_recv=dma((RING,)),
        core_out=dma((RING, bands)),
        core_free=pltpu.SemaphoreType.REGULAR,
        arena_free=pltpu.SemaphoreType.REGULAR((2,)),
        stage_send=dma((8, 8)),
        stage_recv=dma((8, 8)),
        halo_send=pair_sems,
        halo_recv=pair_sems,
        hm_send=peer_sems,
        hm_recv=peer_sems,
        memo_send=peer_sems,
        memo_recv=peer_sems,
        look_send=peer_sems,
        look_recv=peer_sems,
        self_send=peer_sems,
        self_recv=peer_sems,
        vec_send=dma((5,)),
        vec_recv=dma((5,)),
    )
    result = launch(
        partial(back_kernel, dims),
        lengths
        | {n: (v, VMEM) for n, v in near.items()}
        | {n: (v, ANY) for n, v in hbm.items()},
        {},
        dict(
            vis_out=(low_shape(tokens, width), VMEM),
            vis_grad=(full_shape(tokens, width), VMEM),
            query_grad=(full_shape(rows, width), VMEM),
            query_out=(low_shape(rows, width), VMEM),
            bout=(full_shape(4, slab), VMEM),
            bup=(full_shape(2, height), VMEM),
            bdown=(full_shape(2, slab), VMEM),
            gain_grad=(full_shape(7, slab), VMEM),
            bias_grad=(full_shape(7, slab), VMEM),
            wqkv=(full_shape(4, slab, 3 * width // bands), ANY),
            wout=(full_shape(4, slab, width // bands), ANY),
            wup=(full_shape(2, slab, width), ANY),
            wdown=(full_shape(2, bands, slab, width // bands), ANY),
            bags=(low_shape(8, 2, 2, height, width), ANY),
            recv1=(low_shape(8, 2, 2, height // 2, width), ANY),
            recv2=(low_shape(8, 2, height // 2, width), ANY),
        ),
        {},
        scratch,
        1,
        100 * tokens * width * width,
    )

    names = (
        ("vis_out", "query_out", "vis_grad", "query_grad", "wqkv", "wout", "bout")
        + ("wup", "bup", "wdown", "bdown", "gain_grad", "bias_grad")
    )
    final = dict(zip(names, hand_over([result[n] for n in names])))
    grid_shape = (1, band_rows, page_width, width)
    final["vis_out"] = final["vis_out"].reshape(grid_shape)
    final["vis_grad"] = final["vis_grad"].reshape(grid_shape)
    final["query_out"] = final["query_out"][None]
    final["query_grad"] = final["query_grad"][None]
    final["wdown"] = jnp.swapaxes(final["wdown"], 1, 2)
    return tuple(final[n] for n in names)


def plain_ring(count, distance):
    return [(i, (i + distance) % count) for i in range(count)]


def plain_flipped(count, bit):
    return [(i, i ^ bit) for i in range(count)]


def plain_mat_dot(left, right):
    return jnp.dot(left, right, preferred_element_type=jnp.float32)


def plain_mat_left(left, right):
    return lax.dot_general(
        left, right, (((0,), (0,)), ((), ())), preferred_element_type=jnp.float32
    )


def plain_mat_right(left, right):
    return lax.dot_general(
        left, right, (((1,), (1,)), ((), ())), preferred_element_type=jnp.float32
    )


def plain_norm_forward(values, gain_row, bias_row):
    average = jnp.mean(values, axis=-1, keepdims=True)
    centred = values - average
    spread = jnp.mean(centred * centred, axis=-1, keepdims=True)
    inverse = lax.rsqrt(spread + norm_eps)
    normal = centred * inverse
    return ((normal * gain_row + bias_row).astype(bfloat), normal, inverse)


def plain_norm_backward(grad_result, normal, inverse, gain_row):
    grad_normal = grad_result * gain_row
    first_mean = jnp.mean(grad_normal, axis=-1, keepdims=True)
    second_mean = jnp.mean(grad_normal * normal, axis=-1, keepdims=True)
    grad_input = inverse * (grad_normal - first_mean - normal * second_mean)
    return (grad_input, jnp.sum(grad_result * normal, axis=0), jnp.sum(grad_result, axis=0))


def plain_to_windows(grid_cells):
    row_count, col_count = (grid_cells.shape[0], grid_cells.shape[1])
    trailing = grid_cells.shape[2:]
    carved = grid_cells.reshape((row_count // WIN, WIN, col_count // WIN, WIN) + trailing)
    return jnp.swapaxes(carved, 1, 2).reshape((-1, WIN * WIN) + trailing)


def plain_from_windows(blocks, row_count, col_count):
    trailing = blocks.shape[2:]
    carved = blocks.reshape((row_count // WIN, col_count // WIN, WIN, WIN) + trailing)
    return jnp.swapaxes(carved, 1, 2).reshape((row_count, col_count) + trailing)


def plain_to_shifted(grid_cells):
    count = lax.axis_size("row")
    arriving = lax.ppermute(grid_cells[:SHIFT], "row", plain_ring(count, -1))
    rolled = jnp.concatenate([grid_cells[SHIFT:], arriving], axis=0)
    return plain_to_windows(jnp.roll(rolled, -SHIFT, axis=1)).reshape(-1, grid_cells.shape[2])


def plain_from_shifted(tokens, row_count, col_count):
    count = lax.axis_size("row")
    cells = plain_from_windows(tokens.reshape(-1, WIN * WIN, tokens.shape[1]), row_count, col_count)
    rolled = jnp.roll(cells, SHIFT, axis=1)
    arriving = lax.ppermute(rolled[row_count - SHIFT :], "row", plain_ring(count, 1))
    return jnp.concatenate([arriving, rolled[: row_count - SHIFT]], axis=0)


def plain_gather_row(values):
    count = lax.axis_size("row")
    parts = [values] + [lax.ppermute(values, "row", plain_ring(count, s)) for s in range(1, count)]
    return jnp.concatenate(parts, axis=0)


def plain_scatter_row(partial_sums):
    count = lax.axis_size("row")
    parts = jnp.split(partial_sums.astype(bfloat), count, axis=0)
    total = jnp.split(partial_sums, count, axis=0)[0]
    for s in range(1, count):
        total = total + lax.ppermute(parts[s], "row", plain_ring(count, -s)).astype(jnp.float32)
    return total


def plain_halve(blocks, bit, slot):
    count = lax.axis_size("page")
    mine = (lax.axis_index("page") // bit) % 2
    kept = lax.dynamic_index_in_dim(blocks, mine, slot, keepdims=False)
    sent = lax.dynamic_index_in_dim(blocks, 1 - mine, slot, keepdims=False)
    return kept + lax.ppermute(sent, "page", plain_flipped(count, bit))


def plain_reduce_matrix(grad):
    pages = lax.axis_size("page")
    rows = lax.axis_size("row")
    bits = []
    while 2 ** len(bits) < pages:
        bits.append(2 ** len(bits))
    height, width = grad.shape
    blocks = grad.astype(bfloat).reshape((2,) * len(bits) + (height // pages, width))
    if bits:
        blocks = plain_halve(blocks, 1, len(bits) - 1)
    left, right = jnp.split(blocks, 2, axis=-1)
    rest = bits[1:]
    for bit in rest:
        left = plain_halve(left, bit, left.ndim - 3)
    for bit in reversed(rest):
        right = plain_halve(right, bit, 0)
    share = jnp.concatenate([left, right], axis=-1)
    me = lax.axis_index("row")
    pieces = share.reshape(share.shape[0], rows, width // rows)
    total = lax.dynamic_index_in_dim(pieces, me, 1, keepdims=False).astype(jnp.float32)
    for s in range(1, rows):
        sent = lax.dynamic_index_in_dim(pieces, (me + s) % rows, 1, keepdims=False)
        total = total + lax.ppermute(sent, "row", plain_ring(rows, s)).astype(jnp.float32)
    return total


def plain_reduce_vectors(stack):
    pages = lax.axis_size("page")
    rows = lax.axis_size("row")
    bit = 1
    while bit < pages:
        stack = stack.reshape(-1, 2, stack.shape[-1])
        stack = plain_halve(stack, bit, 1)
        bit *= 2
    vector = stack.reshape(-1)
    total = vector
    for s in range(1, rows):
        total = total + lax.ppermute(vector, "row", plain_ring(rows, s))
    return total


def plain_split_heads(values):
    return values.reshape(values.shape[0], values.shape[1], -1, HDIM)


def plain_masked_scores(queries, key_rows, allowed):
    scores = jnp.einsum(
        "gqhd,gkhd->ghqk",
        plain_split_heads(queries),
        plain_split_heads(key_rows),
        preferred_element_type=jnp.float32,
    ) * HDIM ** (-0.5)
    return jnp.where(allowed[:, None], scores, masked_score)


def plain_attend_forward(queries, key_rows, value_rows, allowed):
    scores = plain_masked_scores(queries, key_rows, allowed)
    row_max = jnp.max(scores, axis=-1, keepdims=True)
    raised = jnp.exp(scores - row_max)
    row_total = jnp.sum(raised, axis=-1, keepdims=True)
    probs_low = (raised / row_total).astype(bfloat)
    context = jnp.einsum(
        "ghqk,gkhd->gqhd", probs_low, plain_split_heads(value_rows), preferred_element_type=jnp.float32
    )
    return (context.reshape(queries.shape).astype(bfloat), row_max + jnp.log(row_total))


def plain_attend_backward(queries, key_rows, value_rows, allowed, log_total, grad_context):
    probs = jnp.exp(plain_masked_scores(queries, key_rows, allowed) - log_total)
    probs_low = probs.astype(bfloat)
    grad_heads = plain_split_heads(grad_context)
    grad_values = jnp.einsum(
        "ghqk,gqhd->gkhd", probs_low, grad_heads, preferred_element_type=jnp.float32
    )
    grad_probs = jnp.einsum(
        "gqhd,gkhd->ghqk", grad_heads, plain_split_heads(value_rows), preferred_element_type=jnp.float32
    )
    row_delta = jnp.sum(probs * grad_probs, axis=-1, keepdims=True)
    grad_scores = (probs * (grad_probs - row_delta)).astype(bfloat)
    grad_queries = jnp.einsum(
        "ghqk,gkhd->gqhd", grad_scores, plain_split_heads(key_rows), preferred_element_type=jnp.float32
    ) * HDIM ** (-0.5)
    grad_keys = jnp.einsum(
        "ghqk,gqhd->gkhd", grad_scores, plain_split_heads(queries), preferred_element_type=jnp.float32
    ) * HDIM ** (-0.5)
    return (
        grad_queries.reshape(queries.shape).astype(bfloat),
        grad_keys.reshape(key_rows.shape).astype(bfloat),
        grad_values.reshape(value_rows.shape).astype(bfloat),
    )


def plain_project(from_rows, to_rows, weight):
    width = weight.shape[0]
    queries = plain_mat_dot(from_rows, weight[:, :width]).astype(bfloat)
    paired = plain_mat_dot(to_rows, weight[:, width:]).astype(bfloat)
    return (queries, paired[:, :width], paired[:, width:])


def plain_project_back(from_rows, to_rows, weight, dq, dk, dv):
    width = weight.shape[0]
    pair = jnp.concatenate([dk, dv], axis=1)
    weight_grad = jnp.concatenate([plain_mat_left(from_rows, dq), plain_mat_left(to_rows, pair)], axis=1)
    return (weight_grad, plain_mat_right(dq, weight[:, :width]), plain_mat_right(pair, weight[:, width:]))


def plain_output_back(context_low, weight, grad_residual):
    grad_low = grad_residual.astype(bfloat)
    return (
        plain_mat_left(context_low, grad_low),
        jnp.sum(grad_low, axis=0, dtype=jnp.float32),
        plain_mat_right(grad_low, weight).astype(bfloat),
    )


def plain_feed_forward(values, gain_row, bias_row, up_weight, up_bias, down_weight, down_bias):
    hidden, normal, inverse = plain_norm_forward(values, gain_row, bias_row)
    upward = plain_mat_dot(hidden, up_weight) + up_bias
    active = jax.nn.gelu(upward, approximate=True).astype(bfloat)
    return (
        values + (plain_mat_dot(active, down_weight) + down_bias),
        (hidden, normal, inverse, upward, active),
    )


def plain_feed_backward(grad_residual, kept_values, gain_row, up_weight, down_weight):
    hidden, normal, inverse, upward, active = kept_values
    grad_low = grad_residual.astype(bfloat)
    grad_down = plain_mat_left(active, grad_low)
    grad_down_bias = jnp.sum(grad_low, axis=0, dtype=jnp.float32)
    grad_active = plain_mat_right(grad_low, down_weight)
    gelu_pull = jax.vjp(partial(jax.nn.gelu, approximate=True), upward)[1]
    grad_up_low = gelu_pull(grad_active)[0].astype(bfloat)
    grad_up = plain_mat_left(hidden, grad_up_low)
    grad_up_bias = jnp.sum(grad_up_low, axis=0, dtype=jnp.float32)
    grad_input, gain_grad, bias_grad = plain_norm_backward(
        plain_mat_right(grad_up_low, up_weight), normal, inverse, gain_row
    )
    return (
        grad_residual + grad_input,
        (grad_up, grad_up_bias, grad_down, grad_down_bias, gain_grad, bias_grad),
    )


def plain_shards(
    vis_stream,
    query_stream,
    w_qkv,
    w_out,
    b_out,
    w_up,
    b_up,
    w_down,
    b_down,
    norm_gain,
    norm_bias,
    page_cols,
    query_len,
    prompt_len,
    region_ids,
    vis_cotangent,
    query_cotangent,
):
    band_rows, page_width, width = vis_stream.shape[1:]
    tokens = band_rows * page_width
    query_rows = query_stream.shape[1]
    bands = lax.axis_size("row")
    me = lax.axis_index("row")
    pages = lax.axis_size("page")
    x0 = plain_to_shifted(vis_stream[0]).astype(jnp.float32)
    gx3 = plain_to_shifted(vis_cotangent[0]).astype(jnp.float32)
    y0 = query_stream[0].astype(jnp.float32)
    gy3 = query_cotangent[0].astype(jnp.float32)
    col_limit, query_limit, prompt_limit = page_cols[0], query_len[0], prompt_len[0]

    own_positions = me * query_rows + jnp.arange(query_rows)
    all_positions = jnp.concatenate(
        [((me - s) % bands) * query_rows + jnp.arange(query_rows) for s in range(bands)]
    )
    key_live = all_positions < query_limit
    self_allowed = key_live[None, :] & (
        (all_positions[None, :] <= own_positions[:, None]) | (all_positions[None, :] < prompt_limit)
    )
    rolled_live = (jnp.arange(page_width) + SHIFT) % page_width < col_limit
    live_tiles = plain_to_windows(jnp.broadcast_to(rolled_live[None, :], (band_rows, page_width)))
    visual_allowed = jnp.broadcast_to(
        jnp.tile(live_tiles.reshape(-1), bands)[None, :], (query_rows, bands * tokens)
    )
    query_allowed = jnp.broadcast_to(key_live[None, :], (tokens, query_rows * bands))
    region_tiles = plain_to_windows(region_ids[0])
    diagonal = jnp.eye(WIN * WIN, dtype=jnp.bool_)
    window_allowed = (region_tiles[:, :, None] == region_tiles[:, None, :]) & (
        live_tiles[:, None, :] | diagonal[None]
    )
    tile_shape = (tokens // (WIN * WIN), WIN * WIN, width)

    hs, n1, i1 = plain_norm_forward(y0, norm_gain[1], norm_bias[1])
    hs_all = plain_gather_row(hs)
    hv, n0, i0 = plain_norm_forward(x0, norm_gain[0], norm_bias[0])
    qw, kw, vw = (v.reshape(tile_shape) for v in plain_project(hv, hv, w_qkv[0]))
    cw, lw = plain_attend_forward(qw, kw, vw, window_allowed)
    cw = cw.reshape(tokens, width)
    x1 = x0 + (plain_mat_dot(cw, w_out[0]) + b_out[0])
    hl, n3, i3 = plain_norm_forward(x1, norm_gain[3], norm_bias[3])
    hl_all = plain_gather_row(hl)

    qs, ks, vs = plain_project(hs, hs_all, w_qkv[1])
    cs, ls = plain_attend_forward(qs[None], ks[None], vs[None], self_allowed[None])
    cs = cs[0]
    y1 = y0 + (plain_mat_dot(cs, w_out[1]) + b_out[1])
    ha, n2, i2 = plain_norm_forward(y1, norm_gain[2], norm_bias[2])
    qa, kl, vl = plain_project(ha, hl_all, w_qkv[2])
    ca, la = plain_attend_forward(qa[None], kl[None], vl[None], visual_allowed[None])
    ca = ca[0]
    y2 = y1 + (plain_mat_dot(ca, w_out[2]) + b_out[2])
    hm, n4, i4 = plain_norm_forward(y2, norm_gain[4], norm_bias[4])
    hm_all = plain_gather_row(hm)
    y3, kept_query = plain_feed_forward(
        y2, norm_gain[6], norm_bias[6], w_up[1], b_up[1], w_down[1], b_down[1]
    )
    gy2, feed_query = plain_feed_backward(gy3, kept_query, norm_gain[6], w_up[1], w_down[1])
    final_up1 = plain_reduce_matrix(feed_query[0])
    final_down1 = plain_reduce_matrix(feed_query[2])

    qr, km, vm = plain_project(hl, hm_all, w_qkv[3])
    cr, lr = plain_attend_forward(qr[None], km[None], vm[None], query_allowed[None])
    cr = cr[0]
    x2 = x1 + (plain_mat_dot(cr, w_out[3]) + b_out[3])
    x3, kept_vis = plain_feed_forward(
        x2, norm_gain[5], norm_bias[5], w_up[0], b_up[0], w_down[0], b_down[0]
    )
    gx2, feed_vis = plain_feed_backward(gx3, kept_vis, norm_gain[5], w_up[0], w_down[0])
    final_up0 = plain_reduce_matrix(feed_vis[0])
    final_down0 = plain_reduce_matrix(feed_vis[2])

    wout3, bout3, dcr = plain_output_back(cr, w_out[3], gx2)
    dqr, dkm, dvm = plain_attend_backward(
        qr[None], km[None], vm[None], query_allowed[None], lr, dcr[None]
    )
    qkv3, dhl, dhm = plain_project_back(hl, hm_all, w_qkv[3], dqr[0], dkm[0], dvm[0])
    gy_memo, gain4, bias4 = plain_norm_backward(plain_scatter_row(dhm), n4, i4, norm_gain[4])
    gy2 = gy2 + gy_memo
    final_out3 = plain_reduce_matrix(wout3)
    final_qkv3 = plain_reduce_matrix(qkv3)

    wout2, bout2, dca = plain_output_back(ca, w_out[2], gy2)
    dqa, dkl, dvl = plain_attend_backward(
        qa[None], kl[None], vl[None], visual_allowed[None], la, dca[None]
    )
    qkv2, dha, dhl_all = plain_project_back(ha, hl_all, w_qkv[2], dqa[0], dkl[0], dvl[0])
    gy_ask, gain2, bias2 = plain_norm_backward(dha, n2, i2, norm_gain[2])
    gy1 = gy2 + gy_ask
    gx_look, gain3, bias3 = plain_norm_backward(dhl + plain_scatter_row(dhl_all), n3, i3, norm_gain[3])
    gx1 = gx2 + gx_look
    final_out2 = plain_reduce_matrix(wout2)
    final_qkv2 = plain_reduce_matrix(qkv2)

    wout1, bout1, dcs = plain_output_back(cs, w_out[1], gy1)
    dqs, dks, dvs = plain_attend_backward(qs[None], ks[None], vs[None], self_allowed[None], ls, dcs[None])
    qkv1, dhs, dhs_all = plain_project_back(hs, hs_all, w_qkv[1], dqs[0], dks[0], dvs[0])
    gy_self, gain1, bias1 = plain_norm_backward(dhs + plain_scatter_row(dhs_all), n1, i1, norm_gain[1])
    gy0 = gy1 + gy_self
    final_out1 = plain_reduce_matrix(wout1)
    final_qkv1 = plain_reduce_matrix(qkv1)

    wout0, bout0, dcw = plain_output_back(cw, w_out[0], gx1)
    dqw, dkw, dvw = plain_attend_backward(qw, kw, vw, window_allowed, lw, dcw.reshape(tile_shape))
    dqw, dkw, dvw = (v.reshape(tokens, width) for v in (dqw, dkw, dvw))
    qkv0, dr_from, dr_into = plain_project_back(hv, hv, w_qkv[0], dqw, dkw, dvw)
    gx_win, gain0, bias0 = plain_norm_backward(dr_from + dr_into, n0, i0, norm_gain[0])
    gx0 = gx1 + gx_win
    final_out0 = plain_reduce_matrix(wout0)
    final_qkv0 = plain_reduce_matrix(qkv0)

    vectors = [
        jnp.stack([bout0, bout1, bout2, bout3]),
        jnp.stack([feed_vis[1], feed_query[1]]),
        jnp.stack([feed_vis[3], feed_query[3]]),
        jnp.stack([gain0, gain1, gain2, gain3, gain4, feed_vis[4], feed_query[4]]),
        jnp.stack([bias0, bias1, bias2, bias3, bias4, feed_vis[5], feed_query[5]]),
    ]
    blocks = [
        jnp.swapaxes(v.reshape(v.shape[0], pages, -1), 0, 1).reshape(pages, -1) for v in vectors
    ]
    reduced = plain_reduce_vectors(jnp.concatenate(blocks, axis=1))
    finals, start = [], 0
    for v in vectors:
        size = v.size // pages
        finals.append(reduced[start : start + size].reshape(v.shape[0], -1))
        start += size

    return (
        plain_from_shifted(x3.astype(bfloat), band_rows, page_width)[None],
        y3[None].astype(bfloat),
        plain_from_shifted(gx0, band_rows, page_width)[None],
        gy0[None],
        jnp.stack([final_qkv0, final_qkv1, final_qkv2, final_qkv3]),
        jnp.stack([final_out0, final_out1, final_out2, final_out3]),
        finals[0],
        jnp.stack([final_up0, final_up1]),
        finals[1],
        jnp.stack([final_down0, final_down1]),
        finals[2],
        finals[3],
        finals[4],
    )


def solution(mesh):
    planned = mesh.shape["page"] == 8 and mesh.shape["row"] == 4
    return jax.shard_map(
        shards if planned else plain_shards,
        mesh=mesh,
        in_specs=(
            P("page", "row", None, None),
            P("page", "row", None),
            P(),
            P(),
            P(),
            P(),
            P(),
            P(),
            P(),
            P(),
            P(),
            P("page"),
            P("page"),
            P("page"),
            P("page", "row", None),
            P("page", "row", None, None),
            P("page", "row", None),
        ),
        out_specs=(
            P("page", "row", None, None),
            P("page", "row", None),
            P("page", "row", None, None),
            P("page", "row", None),
            P(None, "page", "row"),
            P(None, "page", "row"),
            P(None, "page"),
            P(None, "page", "row"),
            P(None, "page"),
            P(None, "page", "row"),
            P(None, "page"),
            P(None, "page"),
            P(None, "page"),
        ),
        check_vma=False,
    )
```

```python
from functools import partial

import jax
import jax.numpy as jnp
import numpy as np
from jax import lax
from jax.experimental import pallas as pl
from jax.experimental.pallas import tpu as pltpu
from jax.sharding import PartitionSpec as P

HDIM = 64
WIN = 12
SHIFT = 6
PAIR = 2 * HDIM
SCALE = HDIM ** (-0.5)

masked_score = -1e30
norm_eps = 1e-05
bfloat = jnp.bfloat16
full = jnp.float32
ANY = pl.BlockSpec(memory_space=pl.ANY)
VMEM = pl.BlockSpec(memory_space=pltpu.VMEM)
SMEM = pl.BlockSpec(memory_space=pltpu.SMEM)
MESH = pl.DeviceIdType.MESH


def ring(count, distance):
    return [(i, (i + distance) % count) for i in range(count)]


def flipped(count, bit):
    return [(i, i ^ bit) for i in range(count)]


def dot_nn(left, right):
    return jnp.dot(left, right, preferred_element_type=full)


def dot_nt(left, right):
    return lax.dot_general(left, right, (((1,), (1,)), ((), ())), preferred_element_type=full)


def dot_tn(left, right):
    return lax.dot_general(left, right, (((0,), (0,)), ((), ())), preferred_element_type=full)


def normalise(values):
    centred = values - jnp.mean(values, axis=-1, keepdims=True)
    spread = jnp.mean(centred * centred, axis=-1, keepdims=True)
    inverse = lax.rsqrt(spread + norm_eps)
    return centred * inverse, inverse


def norm_forward(values, gain_row, bias_row):
    return (normalise(values)[0] * gain_row + bias_row).astype(bfloat)


def norm_backward(grad, values, gain_row):
    normal, inverse = normalise(values)
    grad_normal = grad * gain_row
    first = jnp.mean(grad_normal, axis=-1, keepdims=True)
    second = jnp.mean(grad_normal * normal, axis=-1, keepdims=True)
    return (
        inverse * (grad_normal - first - normal * second),
        jnp.sum(grad * normal, axis=0, keepdims=True),
        jnp.sum(grad, axis=0, keepdims=True),
    )


def tile_cols(index, size):
    return pl.ds(pl.multiple_of(index * size, size), size)


def matmul_into(out_ref, left_ref, weight_ref, size):
    def step(i, _):
        cols = tile_cols(i, size)
        out_ref[:, cols] = dot_nn(left_ref[...], weight_ref[:, cols]).astype(out_ref.dtype)
        return 0

    lax.fori_loop(0, weight_ref.shape[1] // size, step, 0)


def two_heads(values):
    lane = lax.broadcasted_iota(jnp.int32, values.shape, 1)
    zero = jnp.zeros_like(values)
    return jnp.concatenate(
        [jnp.where(lane < HDIM, values, zero), jnp.where(lane < HDIM, zero, values)], axis=0
    )


def one_pair(stacked):
    count = stacked.shape[0] // 2
    lane = lax.broadcasted_iota(jnp.int32, (count, PAIR), 1)
    return jnp.where(lane < HDIM, stacked[:count], stacked[count:])


def attend_pair(queries, key_rows, value_rows, bias):
    scores = dot_nt(two_heads(queries), key_rows) + bias
    top = jnp.max(scores, axis=-1, keepdims=True)
    raised = jnp.exp(scores - top)
    total = jnp.sum(raised, axis=-1, keepdims=True)
    context = dot_nn(raised.astype(bfloat), value_rows) / total
    return one_pair(context).astype(bfloat), top + jnp.log(total)


def attend_pair_back(queries, key_rows, value_rows, bias, log_total, context, grad_context):
    both = two_heads(queries)
    grad_both = two_heads(grad_context)
    probs = jnp.exp(dot_nt(both, key_rows) + bias - log_total)
    grad_probs = dot_nt(grad_both, value_rows)
    delta = jnp.sum(
        grad_both.astype(full) * jnp.concatenate([context, context], axis=0).astype(full),
        axis=-1,
        keepdims=True,
    )
    grad_scores = (probs * (grad_probs - delta)).astype(bfloat)
    grad_queries = one_pair(dot_nn(grad_scores, key_rows)) * SCALE
    grad_keys = dot_tn(both, grad_scores).T
    grad_values = dot_tn(grad_both, probs.astype(bfloat)).T
    return grad_queries.astype(bfloat), grad_keys.astype(bfloat), grad_values.astype(bfloat)


def put_logs(log_ref, rows, pair, log_total):
    count = log_total.shape[0] // 2
    lane = lax.broadcasted_iota(jnp.int32, (count, PAIR), 1)
    kept = log_ref[rows, :]
    kept = jnp.where(lane == 2 * pair, log_total[:count], kept)
    log_ref[rows, :] = jnp.where(lane == 2 * pair + 1, log_total[count:], kept)


def take_logs(log_ref, rows, pair):
    kept = log_ref[rows, :]
    lane = lax.broadcasted_iota(jnp.int32, kept.shape, 1)
    parts = [
        jnp.sum(jnp.where(lane == 2 * pair + i, kept, 0.0), axis=-1, keepdims=True)
        for i in range(2)
    ]
    return jnp.concatenate(parts, axis=0)


def in_parts(step, count, between):
    parts = len(between) + 1
    for i in range(parts):
        lax.fori_loop(count * i // parts, count * (i + 1) // parts, step, 0)
        if i < len(between):
            between[i]()


def attend_rows(q_ref, kv_ref, context_ref, log_ref, bias, rows, keys, between=()):
    width = q_ref.shape[1]
    key_start = kv_ref.shape[1] - 2 * width

    def step(pair, _):
        cols = tile_cols(pair, PAIR)
        key_cols = pl.ds(pl.multiple_of(key_start + pair * PAIR, PAIR), PAIR)
        value_cols = pl.ds(pl.multiple_of(key_start + width + pair * PAIR, PAIR), PAIR)
        context, log_total = attend_pair(
            q_ref[rows, cols], kv_ref[keys, key_cols], kv_ref[keys, value_cols], bias
        )
        context_ref[rows, cols] = context
        put_logs(log_ref, rows, pair, log_total)
        return 0

    in_parts(step, width // PAIR, between)


def attend_rows_back(
    q_ref, kv_ref, context_ref, log_ref, grad_ref, dq_ref, dkv_ref, bias, rows, keys, between=()
):
    width = q_ref.shape[1]
    key_start = kv_ref.shape[1] - 2 * width
    grad_start = dkv_ref.shape[1] - 2 * width

    def step(pair, _):
        cols = tile_cols(pair, PAIR)
        key_cols = pl.ds(pl.multiple_of(key_start + pair * PAIR, PAIR), PAIR)
        value_cols = pl.ds(pl.multiple_of(key_start + width + pair * PAIR, PAIR), PAIR)
        dq, dk, dv = attend_pair_back(
            q_ref[rows, cols],
            kv_ref[keys, key_cols],
            kv_ref[keys, value_cols],
            bias,
            take_logs(log_ref, rows, pair),
            context_ref[rows, cols],
            grad_ref[rows, cols],
        )
        dq_ref[rows, cols] = dq
        dkv_ref[keys, pl.ds(pl.multiple_of(grad_start + pair * PAIR, PAIR), PAIR)] = dk
        dkv_ref[keys, pl.ds(pl.multiple_of(grad_start + width + pair * PAIR, PAIR), PAIR)] = dv
        return 0

    in_parts(step, width // PAIR, between)


def allowed_bias(allowed):
    return jnp.where(allowed, 0.0, masked_score).astype(full)


def key_positions(me, bands, rows):
    lane = lax.broadcasted_iota(jnp.int32, (1, bands * rows), 1)
    part = sum((lane >= s * rows).astype(jnp.int32) for s in range(1, bands))
    return (part ^ me) * rows + lane - part * rows


def window_live(first, count, scalars, page_width):
    token = first + lax.broadcasted_iota(jnp.int32, (1, count), 1)
    window = lax.div(token, WIN * WIN)
    column = lax.rem(token, WIN) + WIN * lax.rem(window, page_width // WIN)
    return lax.rem(column + SHIFT, page_width) < scalars[1]


def copies_in(pairs, sems):
    copies = [pltpu.make_async_copy(src, dst, sems.at[i]) for i, (src, dst) in enumerate(pairs)]
    for copy in copies:
        copy.start()
    return copies


def low_shape(*shape):
    return jax.ShapeDtypeStruct(shape, bfloat)


def full_shape(*shape):
    return jax.ShapeDtypeStruct(shape, full)


def source_order(page_width, band_rows):
    tokens = band_rows * page_width
    token = np.arange(tokens)
    across = page_width // WIN
    window, inside = token // (WIN * WIN), token % (WIN * WIN)
    row = window // across * WIN + inside // WIN
    column = window % across * WIN + inside % WIN
    source = row * page_width + (column + SHIFT) % page_width
    order = np.zeros((tokens, tokens), np.float32)
    order[token, source] = 1.0
    return order


def fill_shifted(own_ref, arriving_ref, rows_ref):
    band_rows, width = own_ref.shape[1], own_ref.shape[2]
    for i in range(band_rows - SHIFT):
        rows_ref[i * width : (i + 1) * width, :] = own_ref[0, i + SHIFT].astype(full)
    for i in range(SHIFT):
        j = band_rows - SHIFT + i
        rows_ref[j * width : (j + 1) * width, :] = arriving_ref[i].astype(full)


def page_scalars(r):
    return None, r.page_cols[0], r.query_len[0], r.prompt_len[0]


def region_vectors(region_ref, w, page_width):
    size = WIN * WIN
    labels = region_ref[0].astype(full)
    band_rows = labels.shape[0]
    across = page_width // WIN
    first_row, first_col = w // across * WIN, w % across * WIN

    def at(shape, token_dim, start, divide):
        token = lax.broadcasted_iota(jnp.int32, shape, token_dim)
        place = lax.div(token, WIN) if divide else lax.rem(token, WIN)
        return place + start == lax.broadcasted_iota(jnp.int32, shape, 1 - token_dim)

    rows = at((size, band_rows), 0, first_row, True).astype(full)
    columns = at((size, page_width), 0, first_col, False)
    column = jnp.sum(jnp.where(columns, dot_nn(rows, labels), 0.0), axis=1, keepdims=True)
    rows = at((band_rows, size), 1, first_row, True).astype(full)
    columns = at((page_width, size), 1, first_col, False)
    row = jnp.sum(jnp.where(columns, dot_tn(labels, rows), 0.0), axis=0, keepdims=True)
    return column, row


def window_bias(scalars, region_ref, w, page_width):
    size = WIN * WIN
    live = window_live(w * size, size, scalars, page_width)
    own = lax.broadcasted_iota(jnp.int32, (size, size), 0)
    other = lax.broadcasted_iota(jnp.int32, (size, size), 1)
    column, row = region_vectors(region_ref, w, page_width)
    bias = allowed_bias((column == row) & ((own == other) | live))
    return jnp.concatenate([bias, bias], axis=0)


def self_bias(me, scalars, rows, bands):
    position = key_positions(me, bands, rows)
    own = me * rows + lax.broadcasted_iota(jnp.int32, (rows, 1), 0)
    bias = allowed_bias(
        (position < scalars[2]) & ((position <= own) | (position < scalars[3]))
    )
    return jnp.concatenate([bias, bias], axis=0)


def look_bias(dims, scalars):
    tokens, bands, page_width = dims["tokens"], dims["bands"], dims["page_width"]
    live = window_live(0, tokens, scalars, page_width)
    return jnp.concatenate([allowed_bias(live)] * bands, axis=1)


def read_bias(me, dims, scalars):
    return allowed_bias(key_positions(me, dims["bands"], dims["rows"]) < scalars[2])


class Kernel:
    def __init__(self, refs, hbm, sems):
        self.__dict__.update(refs)
        self.hbm, self.sems = hbm, sems
        self.coming, self.going = {}, []

    def fetch(self, *names):
        for name in names:
            copy = pltpu.make_async_copy(
                self.hbm[name], getattr(self, name), self.sems[name]
            )
            copy.start()
            self.coming[name] = copy

    def ready(self, *names):
        for name in names:
            self.coming.pop(name).wait()

    def save(self, *names):
        for name in names:
            copy = pltpu.make_async_copy(
                getattr(self, name), self.hbm[name], self.sems[name]
            )
            copy.start()
            self.going.append(copy)

    def finish(self):
        for copy in self.going:
            copy.wait()


def launch(body, given, staged, made, kept, scratch, collective, flops):
    sources = list(given) + list(staged)
    results = list(made) + list(kept)
    moved = list(staged) + list(kept)
    arrays = [given[n][0] for n in given] + [staged[n] for n in staged]
    stages = {n: pltpu.VMEM(staged[n].shape, staged[n].dtype) for n in staged}
    stages.update({n: pltpu.VMEM(kept[n].shape, kept[n].dtype) for n in kept})

    def inner(*refs):
        first, second = len(sources), len(sources) + len(results)
        outer = dict(zip(sources, refs[:first])) | dict(zip(results, refs[first:second]))
        inside = dict(zip(list(stages) + list(scratch), refs[second:-1]))
        sems = {n: refs[-1].at[i] for i, n in enumerate(moved)}
        body(Kernel(outer | inside, {n: outer[n] for n in moved}, sems))

    outs = pl.pallas_call(
        inner,
        out_shape=[made[n][0] for n in made] + [kept[n] for n in kept],
        in_specs=[given[n][1] for n in given] + [ANY] * len(staged),
        out_specs=[made[n][1] for n in made] + [ANY] * len(kept),
        scratch_shapes=list(stages.values())
        + list(scratch.values())
        + [pltpu.SemaphoreType.DMA((max(len(moved), 1),))],
        compiler_params=pltpu.CompilerParams(
            vmem_limit_bytes=63 * 2**20, collective_id=collective, has_side_effects=True
        ),
        cost_estimate=pl.CostEstimate(flops=flops, bytes_accessed=2**24, transcendentals=0),
    )(*arrays)
    return dict(zip(results, outs))


def hand_over(arrays):
    count = len(arrays)
    shapes = [a.shape if a.ndim < 4 else (a.shape[0], a.shape[3], a.shape[1] * a.shape[2]) for a in arrays]

    def body(*refs):
        for source, target in zip(refs[:count], refs[count:]):
            if source.shape == target.shape:
                target[...] = source[...]
            else:
                for k in range(source.shape[0]):
                    target[k] = source[k].reshape(target.shape[2], target.shape[1]).T

    return pl.pallas_call(
        body,
        out_shape=[jax.ShapeDtypeStruct(s, a.dtype) for s, a in zip(shapes, arrays)],
        in_specs=[VMEM] * count,
        out_specs=[VMEM] * count,
        compiler_params=pltpu.CompilerParams(vmem_limit_bytes=62 * 2**20),
    )(*arrays)


def greet(devices):
    barrier = pltpu.get_barrier_semaphore()
    for device in devices:
        pl.semaphore_signal(barrier, inc=1, device_id=device, device_id_type=MESH)
    pl.semaphore_wait(barrier, len(devices))


def other_band(step):
    me = lax.axis_index("row")
    if step == 1:
        return me + 1 - 2 * lax.rem(me, 2)
    return lax.rem(me + 2, 4) if step == 2 else 3 - me


def band_peers(bands):
    return [{"row": other_band(s)} for s in range(1, bands)]


class Gather:
    def __init__(self, slots, send, recv):
        self.slots, self.sems = slots, (send, recv)
        self.copies, self.waited = {}, set()
        self.copy(2, 0, 2)
        self.copy(1, 0, 1)

    def copy(self, place, source, step):
        send, recv = self.sems
        self.copies[place] = pltpu.make_async_remote_copy(
            src_ref=self.slots[source],
            dst_ref=self.slots[place],
            send_sem=send.at[place - 1],
            recv_sem=recv.at[place - 1],
            device_id={"row": other_band(step)},
            device_id_type=MESH,
        )
        self.copies[place].start()

    def ready(self, place):
        if place not in self.waited:
            self.waited.add(place)
            self.copies[place].wait_recv()

    def forward(self):
        self.ready(2)
        self.copy(3, 2, 1)

    def finish(self):
        for copy in self.copies.values():
            copy.wait_send()


def look_operands(r, pair, keys):
    width = r.q2.shape[1]
    cols = tile_cols(pair, PAIR)
    value_cols = pl.ds(pl.multiple_of(width + pair * PAIR, PAIR), PAIR)
    return cols, two_heads(r.q2[:, cols]), r.kv2[keys, cols], r.kv2[keys, value_cols]


def put_lane(ref, pair, column):
    lane = lax.broadcasted_iota(jnp.int32, ref.shape, 1)
    ref[...] = jnp.where(lane == pair, column, ref[...])


def take_lane(ref, pair):
    lane = lax.broadcasted_iota(jnp.int32, ref.shape, 1)
    return jnp.sum(jnp.where(lane == pair, ref[...], 0.0), axis=-1, keepdims=True)


def attend_first(r, bias, keys):
    def step(pair, _):
        cols, queries, key_rows, value_rows = look_operands(r, pair, keys)
        scores = dot_nt(queries, key_rows) + bias
        top = jnp.max(scores, axis=-1, keepdims=True)
        raised = jnp.exp(scores - top)
        put_lane(r.tops, pair, top)
        put_lane(r.totals, pair, jnp.sum(raised, axis=-1, keepdims=True))
        r.partial[pair] = dot_nn(raised.astype(bfloat), value_rows)
        return 0

    lax.fori_loop(0, r.q2.shape[1] // PAIR, step, 0)


def attend_last(r, bias, keys):
    def step(pair, _):
        cols, queries, key_rows, value_rows = look_operands(r, pair, keys)
        scores = dot_nt(queries, key_rows) + bias
        before = take_lane(r.tops, pair)
        top = jnp.maximum(before, jnp.max(scores, axis=-1, keepdims=True))
        raised = jnp.exp(scores - top)
        weight = jnp.exp(before - top)
        total = take_lane(r.totals, pair) * weight + jnp.sum(raised, axis=-1, keepdims=True)
        context = (r.partial[pair] * weight + dot_nn(raised.astype(bfloat), value_rows)) / total
        r.c2[:, cols] = one_pair(context).astype(bfloat)
        put_logs(r.log2, slice(None), pair, top + jnp.log(total))
        return 0

    lax.fori_loop(0, r.q2.shape[1] // PAIR, step, 0)


def front_kernel(dims, r):
    page_width, bands, rows, tokens = (dims[n] for n in ("page_width", "bands", "rows", "tokens"))
    width = r.y0.shape[1]
    me = lax.axis_index("row")
    scalars = page_scalars(r)
    greet(band_peers(bands))
    loads = {}
    for a in range(3):
        for i, (name, ref) in enumerate((("wqkv%d", r.w_qkv), ("wout%d", r.w_out))):
            copy = pltpu.make_async_copy(
                ref.at[a], getattr(r, name % a), r.weight_sems.at[2 * a + i]
            )
            copy.start()
            loads[name % a] = copy
    above = {"row": lax.rem(me + bands - 1, bands)}
    halos = []
    for i, ref in enumerate((r.vis, r.cot)):
        halo = pltpu.make_async_remote_copy(
            src_ref=ref.at[0, 0:SHIFT],
            dst_ref=r.halo.at[i],
            send_sem=r.halo_send.at[i],
            recv_sem=r.halo_recv.at[i],
            device_id=above,
            device_id_type=MESH,
        )
        halo.start()
        halos.append(halo)
    r.hs[0] = norm_forward(r.y0[...].astype(full), r.gain[1:2, :], r.bias[1:2, :])
    self_rows = Gather([r.hs.at[s] for s in range(bands)], r.self_send, r.self_recv)

    r.log0[...] = jnp.zeros_like(r.log0)
    r.log1[...] = jnp.zeros_like(r.log1)
    r.log2[...] = jnp.zeros_like(r.log2)
    r.tops[...] = jnp.zeros_like(r.tops)
    r.totals[...] = jnp.zeros_like(r.totals)
    halos[0].wait()
    fill_shifted(r.vis, r.halo.at[0], r.cells)
    x0 = dot_nn(r.order[...], r.cells[...].astype(bfloat))
    r.x0[...] = x0.astype(bfloat)
    r.hv[...] = norm_forward(x0, r.gain[0:1, :], r.bias[0:1, :])
    r.save("x0", "hv")
    loads["wqkv0"].wait()
    r.q0[...] = (dot_nn(r.hv[...], r.wqkv0[:, :width]) * SCALE).astype(bfloat)
    matmul_into(r.kv0, r.hv, r.wqkv0.at[:, width:], width)
    r.save("q0", "kv0")
    size = WIN * WIN
    for w in range(tokens // size):
        part = slice(w * size, (w + 1) * size)
        bias = window_bias(scalars, r.region, w, page_width)
        attend_rows(r.q0, r.kv0, r.c0, r.log0, bias, part, part)
    self_rows.forward()
    r.save("c0", "log0")
    loads["wout0"].wait()
    x1 = r.x0[...].astype(full) + (dot_nn(r.c0[...], r.wout0[...]) + r.b_out[0:1, :])
    r.x1[...] = x1
    r.hl[0] = norm_forward(x1, r.gain[3:4, :], r.bias[3:4, :])
    look_rows = Gather([r.hl.at[s] for s in range(bands)], r.look_send, r.look_recv)
    r.save("x1")

    halos[1].wait()
    fill_shifted(r.cot, r.halo.at[1], r.cells)
    r.gx3[...] = dot_nn(r.order[...], r.cells[...].astype(bfloat)).astype(bfloat)
    r.save("gx3")
    loads["wqkv1"].wait()
    r.q1[...] = (dot_nn(r.hs[0], r.wqkv1[:, :width]) * SCALE).astype(bfloat)
    for s in range(1, bands):
        self_rows.ready(s)

    def project_self(s, _):
        part = pl.ds(pl.multiple_of(s * rows, rows), rows)
        r.kv1[part, :] = dot_nn(r.hs[s], r.wqkv1[:, width:]).astype(bfloat)
        return 0

    lax.fori_loop(0, bands, project_self, 0)
    r.save("hs", "q1", "kv1")
    bias = self_bias(me, scalars, rows, bands)
    attend_rows(r.q1, r.kv1, r.c1, r.log1, bias, slice(None), slice(None))
    look_rows.forward()
    r.save("c1", "log1")
    loads["wout1"].wait()
    y1 = r.y0[...].astype(full) + (dot_nn(r.c1[...], r.wout1[...]) + r.b_out[1:2, :])
    r.y1[...] = y1
    r.ha[...] = norm_forward(y1, r.gain[2:3, :], r.bias[2:3, :])
    loads["wqkv2"].wait()
    r.q2[...] = (dot_nn(r.ha[...], r.wqkv2[:, :width]) * SCALE).astype(bfloat)
    r.save("y1", "ha", "q2")

    live = look_bias(dims, scalars)
    before = (bands - 1) * tokens
    for s in range(bands):
        if s:
            look_rows.ready(s)
        part = slice(s * tokens, (s + 1) * tokens)
        matmul_into(r.kv2.at[part], r.hl.at[s], r.wqkv2.at[:, width:], width)
        if s == bands - 2:
            attend_first(r, live[:, :before], slice(0, before))
    r.save("hl", "kv2")
    attend_last(r, live[:, before:], slice(before, bands * tokens))
    loads["wout2"].wait()
    y2 = r.y1[...] + (dot_nn(r.c2[...], r.wout2[...]) + r.b_out[2:3, :])
    r.y2[...] = y2
    r.hm[...] = norm_forward(y2, r.gain[4:5, :], r.bias[4:5, :])
    r.save("c2", "log2", "y2", "hm")
    self_rows.finish()
    look_rows.finish()
    r.finish()


def split_blocks(dims, tile, grad, core):
    slab = dims["slab"]
    for block in range(dims["pages"]):
        tile[lax.rem(block + core, 2), block // 2] = grad[block * slab : (block + 1) * slab]


RING = 3


def page_place():
    page = lax.axis_index("page")
    core, x, y = lax.rem(page, 2), lax.rem(page // 2, 2), page // 4
    partners = (page + 1 - 2 * core, page + 2 - 4 * x, page + 4 - 8 * y)
    return (core, x, y), [{"page": p} for p in partners]


def remote(src, dst, send, recv, device):
    return pltpu.make_async_remote_copy(
        src_ref=src,
        dst_ref=dst,
        send_sem=send,
        recv_sem=recv,
        device_id=device,
        device_id_type=MESH,
    )


class Loads:
    def __init__(self, sems):
        self.sems, self.used = sems, 0

    def __call__(self, src, dst):
        copy = pltpu.make_async_copy(src, dst, self.sems.at[self.used])
        self.used += 1
        copy.start()
        return copy


class Reducer:
    def __init__(self, dims, r, loads):
        self.dims, self.r, self.loads = dims, r, loads
        (self.core, self.x, self.y), (self.other, self.along_x, self.along_y) = page_place()
        bands = dims["bands"]
        me = lax.axis_index("row")
        self.me = me
        self.next = me + 1 - 2 * lax.rem(me, 2)
        self.far = lax.rem(me + 2, bands)
        self.across = bands - 1 - me
        self.units, self.sent, self.outs, self.stages = 0, {}, {}, {}
        self.total_units = 32
        self.loading = {}


    def unit(self, fill):
        r, u = self.r, self.units
        slot = u % RING
        for copy in self.outs.pop(slot, []):
            copy.wait()
        fill(r.tile.at[slot])
        if u >= RING:
            pl.semaphore_wait(r.core_free, 1)
        self.sent[slot] = self.exchange(slot)
        self.sent[slot].start()
        self.units += 1
        return u

    def exchange(self, slot):
        r = self.r
        return remote(
            r.tile.at[slot, 1],
            r.landed.at[slot],
            r.core_send.at[slot],
            r.core_recv.at[slot],
            self.other,
        )

    def settle(self, u, targets):
        r, slot = self.r, u % RING
        self.sent.pop(slot).wait()
        r.tile[slot, 0] = r.tile[slot, 0] + r.landed[slot]
        if u + RING < self.total_units:
            pl.semaphore_signal(r.core_free, inc=1, device_id=self.other, device_id_type=MESH)
        outs = []
        for i, (part, target) in enumerate(targets):
            copy = pltpu.make_async_copy(r.tile.at[slot, 0, part], target, r.core_out.at[slot, i])
            copy.start()
            outs.append(copy)
        self.outs[slot] = outs

    def slab_targets(self, b, j):
        slab = self.dims["slab"]
        rows = pl.ds(j * slab, slab)
        return [(pl.ds(2 * y, 2), self.r.bags.at[b].at[y, :, rows]) for y in range(2)]

    def block_targets(self, b, j):
        slab = self.dims["slab"]
        return [
            (k, self.r.bags.at[b].at[j // 2, j % 2, pl.ds(k * slab, slab)])
            for k in range(self.dims["bands"])
        ]

    def flush(self, units=None):
        for slot in list(self.outs):
            if units is None or slot in [u % RING for u in units]:
                for copy in self.outs.pop(slot):
                    copy.wait()


    def start(self, b, stage, parts, which=(0, 1)):
        r = self.r
        for i, (src, dst, device) in enumerate(parts):
            if i in which:
                at = (b, 2 * stage + i)
                copy = remote(src, dst, r.stage_send.at[at], r.stage_recv.at[at], device)
                copy.start()
                self.stages.setdefault((b, stage), []).append(copy)

    def arrived(self, b, stage):
        for copy in self.stages.pop((b, stage)):
            copy.wait()

    def halves(self):
        height = self.r.recv1.shape[3]
        return pl.ds(0, height), pl.ds(height, height)

    def landing1(self, b, half):
        r = self.r
        if b < 7:
            return r.recv1.at[b, half]
        return r.arena.at[2 * half : 2 * half + 2, : r.recv1.shape[3]]

    def landing2(self, b, half):
        r = self.r
        height = r.recv1.shape[3]
        if b < 7:
            return r.recv2.at[b, half]
        return r.arena.at[half, height : 2 * height]

    def came2(self, b):
        if b < 7:
            return [self.r.came.at[b % 2, half, 0] for half in range(2)]
        return [self.landing2(b, half) for half in range(2)]

    def load_own(self, b):
        r, slot = self.r, b % 3
        top, bottom = self.halves()
        bag = r.bags.at[b]
        self.loading[b] = [
            self.loads(bag.at[:, self.x, top], r.sums.at[slot, 0]),
            self.loads(bag.at[self.y, :, bottom], r.sums.at[slot, 1]),
        ]

    def free_arena(self):
        for i, device in enumerate((self.along_x, self.along_y)):
            pl.semaphore_signal(
                self.r.arena_free.at[i], inc=1, device_id=device, device_id_type=MESH
            )

    def first(self, b, half=None):
        r = self.r
        if b == 7:
            for i in (0, 1) if half is None else (half,):
                pl.semaphore_wait(r.arena_free.at[i], 1)
        top, bottom = self.halves()
        bag = r.bags.at[b]
        parts = [
            (bag.at[:, 1 - self.x, top], self.landing1(b, 0), self.along_x),
            (bag.at[1 - self.y, :, bottom], self.landing1(b, 1), self.along_y),
        ]
        self.start(b, 0, parts, [0, 1] if half is None else [half])

    def load_second(self, *bags):
        r = self.r
        for b in bags:
            if b not in self.loading:
                self.load_own(b)
            self.arrived(b, 0)
            if b < 7:
                self.loading[b].append(self.loads(r.recv1.at[b], r.came.at[b % 2]))

    def second(self, *bags):
        r = self.r
        for b in bags:
            slot = b % 3
            wait_all(self.loading.pop(b))
            if b < 7:
                r.sums[slot] = r.sums[slot] + r.came[b % 2]
            else:
                for half in range(2):
                    r.sums[slot, half] = r.sums[slot, half] + self.landing1(b, half)[...]
            self.start(
                b,
                1,
                [
                    (r.sums.at[slot, 0, 1 - self.y], self.landing2(b, 0), self.along_y),
                    (r.sums.at[slot, 1, 1 - self.x], self.landing2(b, 1), self.along_x),
                ],
            )

    def load_third(self, *bags):
        r = self.r
        for b in bags:
            self.arrived(b, 1)
            self.loading[b] = []
            if b < 7:
                self.loading[b].append(self.loads(r.recv2.at[b], r.came.at[b % 2, :, 0]))

    def third(self, *bags):
        r = self.r
        for b in bags:
            slot = b % 3
            wait_all(self.loading.pop(b))
            top, bottom = self.came2(b)
            self.cut(b, r.sums[slot, 0, self.y] + top[...], r.sums[slot, 1, self.x] + bottom[...])
            self.start(
                b,
                2,
                [
                    (r.pieces.at[b % 4, self.next], r.recv3.at[b, 0], {"row": self.next}),
                    (r.pieces.at[b % 4, self.across], r.recv3.at[b, 1], {"row": self.next}),
                ],
            )

    def cut(self, b, top, bottom):
        r, slab, bands = self.r, self.dims["slab"], self.dims["bands"]
        width = top.shape[1]
        size = width // bands
        parts = [half[k * slab : (k + 1) * slab] for half in (top, bottom) for k in range(2)]
        if b in (0, 2):
            made = parts
        elif b in (1, 3):
            made = [
                jnp.concatenate([p[:, z * size : (z + 1) * size] for p in parts], axis=1)
                for z in range(bands)
            ]
        else:
            rest = jnp.concatenate(parts[1:], axis=1)
            made = [
                jnp.concatenate(
                    [
                        parts[0][:, z * size : (z + 1) * size],
                        rest[:, 3 * z * size : 3 * (z + 1) * size],
                    ],
                    axis=1,
                )
                for z in range(bands)
            ]
        for z in range(bands):
            r.pieces[b % 4, z] = made[z]

    def fourth(self, *bags):
        r = self.r
        for b in bags:
            slot = b % 2
            self.arrived(b, 2)
            r.last[b % 2, 0] = r.pieces[b % 4, self.me] + r.recv3[b, 0]
            r.last[b % 2, 1] = r.pieces[b % 4, self.far] + r.recv3[b, 1]
            self.start(b, 3, [(r.last.at[b % 2, 1], r.recv4.at[b], {"row": self.far})], [0])

    def store(self, name, target, value):
        scratch = getattr(self.r, name)
        for copy in self.loading.pop(name, ()):
            copy.wait()
        scratch[...] = value
        self.loading[name] = [self.loads(scratch, target)]

    def end(self, *bags):
        r, slab, bands = self.r, self.dims["slab"], self.dims["bands"]
        for b in bags:
            self.arrived(b, 3)
            total = r.last[b % 2, 0].astype(full) + r.recv4[b].astype(full)
            size = total.shape[1] // bands
            if b in (0, 2):
                self.store("final_up", r.wup.at[1 - b // 2], total)
            elif b in (1, 3):
                parts = [total[:, k * size : (k + 1) * size] for k in range(bands)]
                self.store("final_down", r.wdown.at[1 - b // 2], jnp.stack(parts))
            else:
                self.store("final_out", r.wout.at[7 - b], total[:, :size])
                self.store("final_qkv", r.wqkv.at[7 - b], total[:, size:])

    def finish(self):
        for copies in self.loading.values():
            wait_all(copies)


def layer_loads(r, loads, layer, arena):
    width = arena.shape[1]
    copies = [
        loads(r.w_qkv.at[layer, :, i * width : (i + 1) * width], arena.at[i]) for i in range(3)
    ]
    return copies + [loads(r.w_out.at[layer], arena.at[3])]


def wait_all(copies):
    for copy in copies:
        copy.wait()


def project_pair_into(kv_ref, into_ref, arena, start, count):
    width = arena.shape[1]
    part = slice(start, start + count)
    kv_ref[part, :width] = dot_nn(into_ref[part, :], arena[1]).astype(bfloat)
    kv_ref[part, width:] = dot_nn(into_ref[part, :], arena[2]).astype(bfloat)


class Quarters:
    def __init__(self, r, loads, arena):
        self.r, self.loads, self.arena = r, loads, arena
        self.coming = {}

    def load(self, stream, j):
        r, width = self.r, self.arena.shape[1]
        cols = pl.ds(j * width, width)
        pair = 2 * (j % 2)
        self.coming[stream, j] = [
            self.loads(r.w_up.at[stream, :, cols], self.arena.at[pair]),
            self.loads(r.w_down.at[stream, cols, :], self.arena.at[pair + 1]),
        ]

    def ready(self, stream, j):
        wait_all(self.coming.pop((stream, j)))
        pair = 2 * (j % 2)
        return self.arena.at[pair], self.arena.at[pair + 1]


def feed_both_ways(dims, r, red, quarters, stream, norm, values, cot, hidden_ref, total, back, kept, after):
    bands = dims["bands"]
    width = values.shape[1]
    row_out, row_up, row_down, row_gain, row_bias = vec_rows(dims)
    hidden_ref[...] = norm_forward(values[...], r.gain[norm : norm + 1, :], r.bias[norm : norm + 1, :])
    total[...] = values[...] + r.b_down[stream : stream + 1, :]
    back[...] = jnp.zeros_like(back)
    r.vec[row_down + stream : row_down + stream + 1, :] = jnp.sum(
        cot[...].astype(full), axis=0, keepdims=True
    )
    row_up = row_up + stream * bands
    units = FeedUnits(dims, red, 2 * (1 - stream))
    for j in range(bands):
        up, down = quarters.ready(stream, j)
        z = dot_nn(hidden_ref[...], up[...]) + r.b_up[stream : stream + 1, j * width : (j + 1) * width]
        square = z * z
        bend = jnp.tanh(0.7978845608028654 * (z + 0.044715 * (square * z)))
        half = 0.5 * (1.0 + bend)
        slope = half + (0.5 * z) * (1.0 - bend * bend) * (
            0.7978845608028654 * (1.0 + 0.134145 * square)
        )
        active = (z * half).astype(bfloat)
        total[...] += dot_nn(active, down[...])
        dz = dot_nt(cot[...], down[...]) * slope
        r.vec[row_up + j : row_up + j + 1, :] = jnp.sum(dz, axis=0, keepdims=True)
        dz = dz.astype(bfloat)
        back[...] += dot_nt(dz, up[...])
        if j + 2 < bands:
            quarters.load(stream, j + 2)
        if kept is None:
            units.quarter(j, hidden_ref[...], dz, active, cot[...])
        else:
            kept[j][0][...] = dz
            kept[j][1][...] = active
        after(j)
    if kept is None:
        units.finish()


class FeedUnits:
    def __init__(self, dims, red, bag):
        self.dims, self.red, self.bag = dims, red, bag
        self.waiting = []

    def quarter(self, j, hidden, dz, active, low_grad):
        dims, red = self.dims, self.red
        bands, slab = dims["bands"], dims["slab"]
        deep = bands * slab
        up_grad = dot_tn(hidden, dz).astype(bfloat)
        unit = red.unit(lambda tile: split_blocks(dims, tile, up_grad, red.core))
        self.waiting.append((unit, red.slab_targets(self.bag, j)))
        if len(self.waiting) > 1:
            red.settle(*self.waiting.pop(0))
        down_grad = dot_tn(active, low_grad).astype(bfloat)

        def fill(tile):
            for side in range(2):
                part = down_grad[side * deep : (side + 1) * deep]
                for k in range(bands):
                    tile[lax.rem(side + red.core, 2), k] = part[k * slab : (k + 1) * slab]

        unit = red.unit(fill)
        self.waiting.append((unit, red.block_targets(self.bag + 1, j)))
        red.settle(*self.waiting.pop(0))

    def finish(self):
        for item in self.waiting:
            self.red.settle(*item)
        self.red.flush()


def feed_end(dims, r, norm, values, cot, back):
    row_out, row_up, row_down, row_gain, row_bias = vec_rows(dims)
    pull, gain, bias = norm_backward(back[...], values[...], r.gain[norm : norm + 1, :])
    r.vec[row_gain + norm : row_gain + norm + 1, :] = gain
    r.vec[row_bias + norm : row_bias + norm + 1, :] = bias
    return cot[...].astype(full) + pull


def pair_back(dkv_ref, arena, start, count):
    width = arena.shape[1]
    part = slice(start, start + count)
    return dot_nt(dkv_ref[part, :width], arena[1]) + dot_nt(dkv_ref[part, width:], arena[2])


class Scatter:
    def __init__(self, dkv_ref, arena, count, parts, landing, send, recv):
        self.parts, self.landing, self.sems = parts, landing, (send, recv)
        self.copies = []
        parts[2] = pair_back(dkv_ref, arena, 3 * count, count).astype(bfloat)
        self.copy(2, 2, 1)
        parts[0] = pair_back(dkv_ref, arena, count, count).astype(bfloat)
        self.copy(0, 0, 1)
        parts[1] = pair_back(dkv_ref, arena, 2 * count, count).astype(bfloat)
        self.own = lambda: pair_back(dkv_ref, arena, 0, count)

    def copy(self, part, place, step):
        send, recv = self.sems
        copy = remote(
            self.parts.at[part],
            self.landing.at[place],
            send.at[place],
            recv.at[place],
            {"row": other_band(step)},
        )
        copy.start()
        self.copies.append(copy)

    def forward(self):
        self.copies.pop(0).wait()
        self.parts[1] = self.parts[1] + self.landing[2]
        self.copy(1, 1, 2)

    def total(self, own):
        wait_all(self.copies)
        return own + self.landing[0].astype(full) + self.landing[1].astype(full)


def weight_units(dims, r, red, b, context, low, from_rows, into_rows, dq, dkv, between=None):
    width = r.tile.shape[-1]
    sides = [
        lambda: dot_tn(context[...], low[...]),
        lambda: dot_tn(from_rows[...], dq[...]),
        lambda: dot_tn(into_rows[...], dkv[:, :width]),
        lambda: dot_tn(into_rows[...], dkv[:, width:]),
    ]
    units = []
    for j, side in enumerate(sides):
        grad = side().astype(bfloat)
        units.append(red.unit(lambda tile: split_blocks(dims, tile, grad, red.core)))
        if j:
            red.settle(units[j - 1], red.slab_targets(b, j - 1))
        if j == 2 and between:
            between()
        if j == 3:
            red.flush(units[:2])
            red.first(b, 0)
    red.settle(units[-1], red.slab_targets(b, 3))
    red.flush()
    red.first(b, 1)


def vec_rows(dims):
    quarters = dims["bands"]
    return 0, 4, 4 + 2 * quarters, 6 + 2 * quarters, 13 + 2 * quarters


def put_vectors(dims, r):
    bands, slab, pages = dims["bands"], dims["slab"], dims["pages"]
    row_out, row_up, row_down, row_gain, row_bias = vec_rows(dims)
    width = r.vec.shape[1]
    page = lax.axis_index("page")
    own = pltpu.roll(r.vec[...], lax.rem(width - page * slab, width), 1)[:, :slab]
    r.bout[...] = own[row_out:row_up]
    r.bdown[...] = own[row_down:row_gain]
    r.gain_grad[...] = own[row_gain:row_bias]
    r.bias_grad[...] = own[row_bias : row_bias + 7]
    hidden = bands * slab
    per_row = pages // bands
    row, shift = page // per_row, lax.rem(page, per_row) * hidden
    for stream in range(2):
        start = row_up + stream * bands
        chosen = jnp.zeros((1, width), full)
        for k in range(bands):
            chosen = chosen + jnp.where(row == k, r.vec[start + k : start + k + 1, :], 0.0)
        r.bup[stream : stream + 1, :] = jnp.where(
            shift == 0, chosen[:, :hidden], chosen[:, width - hidden :]
        )


def back_kernel(dims, r):
    page_width, bands, rows, tokens = (dims[n] for n in ("page_width", "bands", "rows", "tokens"))
    slab = dims["slab"]
    width = r.f1.shape[1]
    me = lax.axis_index("row")
    scalars = page_scalars(r)
    loads = Loads(r.load_sems)
    red = Reducer(dims, r, loads)
    row_out, row_up, row_down, row_gain, row_bias = vec_rows(dims)
    hm_load = loads(r.hm_hbm, r.into.at[0:rows])
    y2_load = [loads(r.y2_hbm, r.y2), loads(r.gy3_hbm, r.dq_s)]
    quarters = Quarters(r, loads, r.arena)
    quarters.load(1, 0)
    quarters.load(1, 1)
    greet(band_peers(bands) + [red.other, red.along_x, red.along_y])
    hm_load.wait()
    memo = Gather([r.into.at[s * rows : (s + 1) * rows] for s in range(bands)], r.hm_send, r.hm_recv)
    weights3 = layer_loads(r, loads, 3, r.att)
    hl_load = loads(r.hl_hbm.at[0], r.from_rows)
    x1_load = loads(r.x1_hbm, r.f1)
    gx3_load = loads(r.gx3_hbm, r.cot)
    small = [
        loads(src, dst)
        for src, dst in (
            (r.q2_hbm, r.q2),
            (r.c2_hbm, r.c2),
            (r.log2_hbm, r.log2),
            (r.c1_hbm, r.c1),
            (r.ha_hbm, r.ha),
            (r.y1_hbm, r.y1),
        )
    ]
    r.vec[...] = jnp.zeros_like(r.vec)

    wait_all(y2_load)

    def after_query(j):
        if j == 2:
            memo.forward()
            red.flush()
            red.first(0, 0)

    feed_both_ways(
        dims, r, red, quarters, 1, 6, r.y2, r.dq_s, r.grad_s, r.own_m, r.gy, None, after_query
    )
    red.first(0, 1)
    red.first(1)
    quarters.load(0, 0)
    quarters.load(0, 1)
    r.query_out[...] = r.own_m[...].astype(bfloat)
    r.gy[...] = feed_end(dims, r, 6, r.y2, r.dq_s, r.gy)

    every = slice(None)
    few = slice(0, bands * rows)
    hl_load.wait()
    wait_all(weights3)
    r.q[...] = (dot_nn(r.from_rows[...], r.att[0]) * SCALE).astype(bfloat)
    project_pair_into(r.kv, r.into, r.att, 0, rows)
    for s in range(1, bands):
        memo.ready(s)
        project_pair_into(r.kv, r.into, r.att, s * rows, rows)
    bias = read_bias(me, dims, scalars)
    memo.finish()
    r.log[...] = jnp.zeros_like(r.log)
    attend_rows(r.q, r.kv, r.context, r.log, bias, every, few)
    x1_load.wait()
    r.f2[...] = r.f1[...] + (dot_nn(r.context[...], r.att[3]) + r.b_out[3:4, :])

    gx3_load.wait()

    def after_patches(j):
        if j == bands - 1:
            red.load_second(0, 1)

    spare = slice(bands * rows, bands * rows + tokens)
    places = [r.parts_l.at[0], r.parts_l.at[1], r.parts_l.at[2], r.into.at[spare]]
    for ref in (r.kv, r.dkv):
        places += [ref.at[spare, :width], ref.at[spare, width:]]
    kept = [(places[2 * j], places[2 * j + 1]) for j in range(bands)]
    feed_both_ways(
        dims, r, red, quarters, 0, 5, r.f2, r.cot, r.hidden, r.f3, r.f4, kept, after_patches
    )
    red.second(0, 1)
    weights2 = layer_loads(r, loads, 2, r.arena)
    to_right = {"row": lax.rem(me + 1, bands)}
    moved = dot_tn(r.order[...], r.f3[...].astype(bfloat)).astype(bfloat)
    stay = tokens - SHIFT * page_width
    r.vis_out[tokens - stay :, :] = moved[:stay]
    r.halo_low[...] = moved[stay:]
    halo = remote(
        r.halo_low, r.vis_out.at[: tokens - stay], r.halo_send.at[0], r.halo_recv.at[0], to_right
    )
    halo.start()
    gx2 = feed_end(dims, r, 5, r.f2, r.cot, r.f4)
    r.f5[...] = gx2

    low = gx2.astype(bfloat)
    r.low[...] = low
    r.vec[row_out + 3 : row_out + 4, :] = jnp.sum(low.astype(full), axis=0, keepdims=True)
    r.grad[...] = dot_nt(low, r.att[3]).astype(bfloat)
    attend_rows_back(r.q, r.kv, r.context, r.log, r.grad, r.dq, r.dkv, bias, every, few)
    memo_back = Scatter(r.dkv, r.att, rows, r.parts_m, r.got_m, r.memo_send, r.memo_recv)
    r.own_m[...] = memo_back.own()
    r.f4[...] = dot_nt(r.dq[...], r.att[0])
    weights0 = layer_loads(r, loads, 0, r.att)
    few_dkv, few_into = r.dkv.at[0 : bands * rows], r.into.at[0 : bands * rows]
    units = FeedUnits(dims, red, 2)
    for j in range(bands):
        if j == 0:
            red.load_third(0, 1)
        units.quarter(j, r.hidden[...], kept[j][0][...], kept[j][1][...], r.cot[...])
        if j < 2:
            red.third(j)
        if j == 2:
            memo_back.forward()
            red.flush()
            red.first(2, 0)
    units.finish()
    red.first(2, 1)
    red.first(3)
    kv_load = loads(r.kv2_hbm, r.kv)
    weight_units(dims, r, red, 4, r.context, r.low, r.from_rows, few_into, r.dq, few_dkv)
    late = [
        loads(r.hl_all_hbm, r.into),
        loads(r.q0_hbm, r.q),
        loads(r.c0_hbm, r.context),
        loads(r.log0_hbm, r.log),
        loads(r.hv_hbm, r.from_rows),
        loads(r.x1_hbm, r.f1),
        loads(r.x0_hbm, r.cot),
    ]

    wait_all(small)
    dhm = memo_back.total(r.own_m[...])
    red.fourth(0, 1)
    pull, gain4, bias4 = norm_backward(
        dhm,
        r.y2[...],
        r.gain[4:5, :],
    )
    r.vec[row_gain + 4 : row_gain + 5, :] = gain4
    r.vec[row_bias + 4 : row_bias + 5, :] = bias4
    gy = r.gy[...] + pull
    r.gy[...] = gy
    low = gy.astype(bfloat)
    r.low_s[...] = low
    r.vec[row_out + 2 : row_out + 3, :] = jnp.sum(low.astype(full), axis=0, keepdims=True)
    wait_all(weights2)
    r.grad_s[...] = dot_nt(low, r.arena[3]).astype(bfloat)
    kv_load.wait()
    attend_rows_back(
        r.q2,
        r.kv,
        r.c2,
        r.log2,
        r.grad_s,
        r.dq_s,
        r.dkv,
        look_bias(dims, scalars),
        every,
        every,
    )
    self_loads = [
        loads(r.kv1_hbm, r.kv.at[0 : bands * rows]),
        loads(r.q1_hbm, r.q2),
        loads(r.log1_hbm, r.log2),
    ]
    look_back = Scatter(r.dkv, r.arena, tokens, r.parts_l, r.got_l, r.look_send, r.look_recv)
    r.f4[...] += look_back.own()
    pull, gain2, bias2 = norm_backward(dot_nt(r.dq_s[...], r.arena[0]), r.y1[...], r.gain[2:3, :])
    r.vec[row_gain + 2 : row_gain + 3, :] = gain2
    r.vec[row_bias + 2 : row_bias + 3, :] = bias2
    r.gy[...] += pull
    weights1 = layer_loads(r, loads, 1, r.arena)
    wait_all(late)
    red.end(0, 1)
    weight_units(
        dims, r, red, 5, r.c2, r.low_s, r.ha, r.into, r.dq_s, r.dkv, lambda: red.load_second(2, 3)
    )
    red.second(2, 3)
    hidden_load = loads(r.hs_hbm, r.into.at[0 : bands * rows])
    look_back.forward()

    low = r.gy[...].astype(bfloat)
    r.low_s[...] = low
    r.vec[row_out + 1 : row_out + 2, :] = jnp.sum(low.astype(full), axis=0, keepdims=True)
    wait_all(weights1)
    r.grad_s[...] = dot_nt(low, r.arena[3]).astype(bfloat)
    wait_all(self_loads)
    bias = self_bias(me, scalars, rows, bands)
    attend_rows_back(r.q2, r.kv, r.c1, r.log2, r.grad_s, r.dq_s, r.dkv, bias, every, few)
    kv_load = loads(r.kv0_hbm, r.kv.at[0:tokens])
    self_back = Scatter(r.dkv, r.arena, rows, r.parts_m, r.got_s, r.self_send, r.self_recv)
    r.own_m[...] = self_back.own() + dot_nt(r.dq_s[...], r.arena[0])
    red.free_arena()
    red.load_second(4)
    hidden_load.wait()
    red.second(4)
    weight_units(
        dims, r, red, 6, r.c1, r.low_s, r.into.at[0:rows], few_into, r.dq_s, few_dkv
    )

    self_back.forward()
    red.load_third(2, 3)
    dhl = look_back.total(r.f4[...])
    red.third(2, 3)
    pull, gain3, bias3 = norm_backward(
        dhl,
        r.f1[...],
        r.gain[3:4, :],
    )
    r.vec[row_gain + 3 : row_gain + 4, :] = gain3
    r.vec[row_bias + 3 : row_bias + 4, :] = bias3
    gx1 = r.f5[...] + pull
    r.f5[...] = gx1
    low = gx1.astype(bfloat)
    r.low[...] = low
    r.vec[row_out : row_out + 1, :] = jnp.sum(low.astype(full), axis=0, keepdims=True)
    wait_all(weights0)
    r.grad[...] = dot_nt(low, r.att[3]).astype(bfloat)
    kv_load.wait()
    size = WIN * WIN
    for w in range(tokens // size):
        part = slice(w * size, (w + 1) * size)
        bias = window_bias(scalars, r.region, w, page_width)
        attend_rows_back(
            r.q, r.kv, r.context, r.log, r.grad, r.dq, r.dkv, bias, part, part
        )
    red.load_second(5)
    dr = pair_back(r.dkv, r.att, 0, tokens) + dot_nt(r.dq[...], r.att[0])
    pull, gain0, bias0 = norm_backward(dr, r.cot[...].astype(full), r.gain[0:1, :])
    r.vec[row_gain : row_gain + 1, :] = gain0
    r.vec[row_bias : row_bias + 1, :] = bias0
    gx0 = r.f5[...] + pull
    high = gx0.astype(bfloat)
    rest = (gx0 - high.astype(full)).astype(bfloat)
    moved = dot_tn(r.order[...], high) + dot_tn(r.order[...], rest)
    r.vis_grad[tokens - stay :, :] = moved[:stay]
    r.f2[: tokens - stay, :] = moved[stay:]
    halo_back = remote(
        r.f2.at[: tokens - stay], r.vis_grad.at[: tokens - stay], r.halo_send.at[1], r.halo_recv.at[1], to_right
    )
    halo_back.start()
    red.second(5)
    red.load_second(6)
    weight_units(
        dims, r, red, 7, r.context, r.low, r.from_rows, r.from_rows, r.dq, r.dkv.at[0:tokens],
        lambda: red.second(6),
    )

    pull, gain1, bias1 = norm_backward(
        self_back.total(r.own_m[...]),
        r.y0[...].astype(full),
        r.gain[1:2, :],
    )
    r.query_grad[...] = r.gy[...] + pull
    r.vec[row_gain + 1 : row_gain + 2, :] = gain1
    r.vec[row_bias + 1 : row_bias + 2, :] = bias1

    def swap(i, device):
        copy = remote(r.vec, r.vec_in.at[i], r.vec_send.at[i], r.vec_recv.at[i], device)
        copy.start()
        return copy

    def add(i, copy):
        copy.wait()
        r.vec[...] = r.vec[...] + r.vec_in[i]

    copy = swap(0, red.other)
    red.load_third(4)
    red.third(4)
    red.load_own(7)
    add(0, copy)
    copy = swap(1, {"row": red.next})
    red.fourth(2, 3)
    red.load_third(5)
    red.third(5)
    add(1, copy)
    copy = swap(2, {"row": red.far})
    red.load_third(6)
    red.third(6)
    add(2, copy)
    copy = swap(3, red.along_x)
    red.end(2, 3)
    red.fourth(4)
    red.load_second(7)
    red.second(7)
    red.fourth(5)
    add(3, copy)
    copy = swap(4, red.along_y)
    red.end(4)
    red.fourth(6)
    red.load_third(7)
    red.third(7)
    add(4, copy)
    put_vectors(dims, r)
    red.end(5)
    red.fourth(7)
    red.end(6)
    red.end(7)
    halo.wait()
    halo_back.wait()
    red.finish()


def shards(
    vis_stream,
    query_stream,
    w_qkv,
    w_out,
    b_out,
    w_up,
    b_up,
    w_down,
    b_down,
    norm_gain,
    norm_bias,
    page_cols,
    query_len,
    prompt_len,
    region_ids,
    vis_cotangent,
    query_cotangent,
):
    band_rows, page_width, width = vis_stream.shape[1:]
    tokens = band_rows * page_width
    rows = query_stream.shape[1]
    bands, pages = lax.axis_size("row"), lax.axis_size("page")
    me = lax.axis_index("row")
    hidden_units = w_up.shape[2]
    slab = width // pages
    dims = dict(
        page_width=page_width,
        bands=bands,
        tokens=tokens,
        rows=rows,
        pages=pages,
        slab=slab,
    )
    qkv_any, out_any = (w_qkv, ANY), (w_out, ANY)
    log_lanes = full_shape(tokens, PAIR)
    y0, gy3 = query_stream[0], query_cotangent[0]
    lengths = dict(
        page_cols=(page_cols, SMEM), query_len=(query_len, SMEM), prompt_len=(prompt_len, SMEM)
    )
    order = jnp.asarray(source_order(page_width, band_rows), bfloat)

    given = dict(
        **lengths,
        vis=(vis_stream, VMEM),
        cot=(vis_cotangent, VMEM),
        y0=(y0, VMEM),
        order=(order, VMEM),
        region=(region_ids, VMEM),
        gain=(norm_gain, VMEM),
        bias=(norm_bias, VMEM),
        b_out=(b_out, VMEM),
        w_qkv=qkv_any,
        w_out=out_any,
    )
    weight = {}
    for a in range(3):
        weight["wqkv%d" % a] = pltpu.VMEM((width, 3 * width), bfloat)
        weight["wout%d" % a] = pltpu.VMEM((width, width), bfloat)
    pair_sems = pltpu.SemaphoreType.DMA((2,))
    peer_sems = pltpu.SemaphoreType.DMA((bands - 1,))
    front = launch(
        partial(front_kernel, dims),
        given,
        {},
        {},
        dict(
            x0=low_shape(tokens, width),
            hv=low_shape(tokens, width),
            q0=low_shape(tokens, width),
            kv0=low_shape(tokens, 2 * width),
            c0=low_shape(tokens, width),
            log0=log_lanes,
            x1=full_shape(tokens, width),
            gx3=low_shape(tokens, width),
            hs=low_shape(bands, rows, width),
            q1=low_shape(rows, width),
            kv1=low_shape(bands * rows, 2 * width),
            c1=low_shape(rows, width),
            log1=full_shape(rows, PAIR),
            y1=full_shape(rows, width),
            ha=low_shape(rows, width),
            q2=low_shape(rows, width),
            hl=low_shape(bands, tokens, width),
            kv2=low_shape(bands * tokens, 2 * width),
            c2=low_shape(rows, width),
            log2=full_shape(rows, PAIR),
            y2=full_shape(rows, width),
            hm=low_shape(rows, width),
        ),
        dict(
            cells=pltpu.VMEM((tokens, width), full),
            halo=pltpu.VMEM((2, SHIFT, page_width, width), bfloat),
            tops=pltpu.VMEM((2 * rows, PAIR), full),
            totals=pltpu.VMEM((2 * rows, PAIR), full),
            partial=pltpu.VMEM((width // PAIR, 2 * rows, PAIR), full),
            halo_send=pair_sems,
            halo_recv=pair_sems,
            self_send=peer_sems,
            self_recv=peer_sems,
            look_send=peer_sems,
            look_recv=peer_sems,
            weight_sems=pltpu.SemaphoreType.DMA((6,)),
            **weight,
        ),
        0,
        40 * tokens * width * width,
    )
    hbm = {
        "x1_hbm": front["x1"],
        "x0_hbm": front["x0"],
        "gx3_hbm": front["gx3"],
        "hv_hbm": front["hv"],
        "hl_hbm": front["hl"],
        "hl_all_hbm": front["hl"].reshape(bands * tokens, width),
        "hs_hbm": front["hs"].reshape(bands * rows, width),
        "ha_hbm": front["ha"],
        "hm_hbm": front["hm"],
        "y1_hbm": front["y1"],
        "y2_hbm": front["y2"],
        "gy3_hbm": gy3,
        "w_qkv": w_qkv,
        "w_out": w_out,
        "w_up": w_up,
        "w_down": w_down,
    }
    for a in range(3):
        for name in ("q", "kv", "c", "log"):
            hbm["%s%d_hbm" % (name, a)] = front["%s%d" % (name, a)]
    near = dict(
        y0=y0,
        order=order,
        region=region_ids,
        gain=norm_gain,
        bias=norm_bias,
        b_out=b_out,
        b_up=b_up,
        b_down=b_down,
    )
    height = bands * slab
    halo_rows = SHIFT * page_width
    vec_shape = full_shape(vec_rows(dims)[-1] + 11, width)
    wide = lambda count: pltpu.VMEM((count, width), full)
    narrow = lambda count: pltpu.VMEM((count, width), bfloat)
    dma = pltpu.SemaphoreType.DMA
    scratch = dict(
        att=pltpu.VMEM((4, width, width), bfloat),
        arena=pltpu.VMEM((4, width, width), bfloat),
        tile=pltpu.VMEM((RING, 2, pages // 2, slab, width), bfloat),
        landed=pltpu.VMEM((RING, pages // 2, slab, width), bfloat),
        sums=pltpu.VMEM((3, 2, 2, height // 2, width), bfloat),
        came=pltpu.VMEM((2, 2, 2, height // 2, width), bfloat),
        pieces=pltpu.VMEM((4, bands, slab, width), bfloat),
        last=pltpu.VMEM((2, 2, slab, width), bfloat),
        hidden=narrow(tokens),
        recv3=pltpu.VMEM((8, 2, slab, width), bfloat),
        recv4=pltpu.VMEM((8, slab, width), bfloat),
        final_up=wide(slab),
        final_down=pltpu.VMEM((bands, slab, width // bands), full),
        final_out=pltpu.VMEM((slab, width // bands), full),
        final_qkv=pltpu.VMEM((slab, 3 * width // bands), full),
        q=narrow(tokens),
        kv=pltpu.VMEM((bands * tokens, 2 * width), bfloat),
        context=narrow(tokens),
        log=pltpu.VMEM((tokens, PAIR), full),
        grad=narrow(tokens),
        dq=narrow(tokens),
        dkv=pltpu.VMEM((bands * tokens, 2 * width), bfloat),
        low=narrow(tokens),
        cot=narrow(tokens),
        from_rows=narrow(tokens),
        into=narrow(bands * tokens),
        f1=wide(tokens),
        f2=wide(tokens),
        f3=wide(tokens),
        f4=wide(tokens),
        f5=wide(tokens),
        q2=narrow(rows),
        c2=narrow(rows),
        c1=narrow(rows),
        log2=pltpu.VMEM((rows, PAIR), full),
        ha=narrow(rows),
        low_s=narrow(rows),
        grad_s=narrow(rows),
        dq_s=narrow(rows),
        y1=wide(rows),
        y2=wide(rows),
        gy=wide(rows),
        own_m=wide(rows),
        parts_m=pltpu.VMEM((bands - 1, rows, width), bfloat),
        parts_l=pltpu.VMEM((bands - 1, tokens, width), bfloat),
        got_m=pltpu.VMEM((bands - 1, rows, width), bfloat),
        got_l=pltpu.VMEM((bands - 1, tokens, width), bfloat),
        got_s=pltpu.VMEM((bands - 1, rows, width), bfloat),
        halo_low=narrow(halo_rows),
        vec=pltpu.VMEM(vec_shape.shape, full),
        vec_in=pltpu.VMEM((5,) + vec_shape.shape, full),
        load_sems=dma((192,)),
        core_send=dma((RING,)),
        core_recv=dma((RING,)),
        core_out=dma((RING, bands)),
        core_free=pltpu.SemaphoreType.REGULAR,
        arena_free=pltpu.SemaphoreType.REGULAR((2,)),
        stage_send=dma((8, 8)),
        stage_recv=dma((8, 8)),
        halo_send=pair_sems,
        halo_recv=pair_sems,
        hm_send=peer_sems,
        hm_recv=peer_sems,
        memo_send=peer_sems,
        memo_recv=peer_sems,
        look_send=peer_sems,
        look_recv=peer_sems,
        self_send=peer_sems,
        self_recv=peer_sems,
        vec_send=dma((5,)),
        vec_recv=dma((5,)),
    )
    result = launch(
        partial(back_kernel, dims),
        lengths
        | {n: (v, VMEM) for n, v in near.items()}
        | {n: (v, ANY) for n, v in hbm.items()},
        {},
        dict(
            vis_out=(low_shape(tokens, width), VMEM),
            vis_grad=(full_shape(tokens, width), VMEM),
            query_grad=(full_shape(rows, width), VMEM),
            query_out=(low_shape(rows, width), VMEM),
            bout=(full_shape(4, slab), VMEM),
            bup=(full_shape(2, height), VMEM),
            bdown=(full_shape(2, slab), VMEM),
            gain_grad=(full_shape(7, slab), VMEM),
            bias_grad=(full_shape(7, slab), VMEM),
            wqkv=(full_shape(4, slab, 3 * width // bands), ANY),
            wout=(full_shape(4, slab, width // bands), ANY),
            wup=(full_shape(2, slab, width), ANY),
            wdown=(full_shape(2, bands, slab, width // bands), ANY),
            bags=(low_shape(8, 2, 2, height, width), ANY),
            recv1=(low_shape(8, 2, 2, height // 2, width), ANY),
            recv2=(low_shape(8, 2, height // 2, width), ANY),
        ),
        {},
        scratch,
        1,
        100 * tokens * width * width,
    )

    names = (
        ("vis_out", "query_out", "vis_grad", "query_grad", "wqkv", "wout", "bout")
        + ("wup", "bup", "wdown", "bdown", "gain_grad", "bias_grad")
    )
    final = dict(zip(names, hand_over([result[n] for n in names])))
    grid_shape = (1, band_rows, page_width, width)
    final["vis_out"] = final["vis_out"].reshape(grid_shape)
    final["vis_grad"] = final["vis_grad"].reshape(grid_shape)
    final["query_out"] = final["query_out"][None]
    final["query_grad"] = final["query_grad"][None]
    final["wdown"] = jnp.swapaxes(final["wdown"], 1, 2)
    return tuple(final[n] for n in names)


def plain_ring(count, distance):
    return [(i, (i + distance) % count) for i in range(count)]


def plain_flipped(count, bit):
    return [(i, i ^ bit) for i in range(count)]


def plain_mat_dot(left, right):
    return jnp.dot(left, right, preferred_element_type=jnp.float32)


def plain_mat_left(left, right):
    return lax.dot_general(
        left, right, (((0,), (0,)), ((), ())), preferred_element_type=jnp.float32
    )


def plain_mat_right(left, right):
    return lax.dot_general(
        left, right, (((1,), (1,)), ((), ())), preferred_element_type=jnp.float32
    )


def plain_norm_forward(values, gain_row, bias_row):
    average = jnp.mean(values, axis=-1, keepdims=True)
    centred = values - average
    spread = jnp.mean(centred * centred, axis=-1, keepdims=True)
    inverse = lax.rsqrt(spread + norm_eps)
    normal = centred * inverse
    return ((normal * gain_row + bias_row).astype(bfloat), normal, inverse)


def plain_norm_backward(grad_result, normal, inverse, gain_row):
    grad_normal = grad_result * gain_row
    first_mean = jnp.mean(grad_normal, axis=-1, keepdims=True)
    second_mean = jnp.mean(grad_normal * normal, axis=-1, keepdims=True)
    grad_input = inverse * (grad_normal - first_mean - normal * second_mean)
    return (grad_input, jnp.sum(grad_result * normal, axis=0), jnp.sum(grad_result, axis=0))


def plain_to_windows(grid_cells):
    row_count, col_count = (grid_cells.shape[0], grid_cells.shape[1])
    trailing = grid_cells.shape[2:]
    carved = grid_cells.reshape((row_count // WIN, WIN, col_count // WIN, WIN) + trailing)
    return jnp.swapaxes(carved, 1, 2).reshape((-1, WIN * WIN) + trailing)


def plain_from_windows(blocks, row_count, col_count):
    trailing = blocks.shape[2:]
    carved = blocks.reshape((row_count // WIN, col_count // WIN, WIN, WIN) + trailing)
    return jnp.swapaxes(carved, 1, 2).reshape((row_count, col_count) + trailing)


def plain_to_shifted(grid_cells):
    count = lax.axis_size("row")
    arriving = lax.ppermute(grid_cells[:SHIFT], "row", plain_ring(count, -1))
    rolled = jnp.concatenate([grid_cells[SHIFT:], arriving], axis=0)
    return plain_to_windows(jnp.roll(rolled, -SHIFT, axis=1)).reshape(-1, grid_cells.shape[2])


def plain_from_shifted(tokens, row_count, col_count):
    count = lax.axis_size("row")
    cells = plain_from_windows(tokens.reshape(-1, WIN * WIN, tokens.shape[1]), row_count, col_count)
    rolled = jnp.roll(cells, SHIFT, axis=1)
    arriving = lax.ppermute(rolled[row_count - SHIFT :], "row", plain_ring(count, 1))
    return jnp.concatenate([arriving, rolled[: row_count - SHIFT]], axis=0)


def plain_gather_row(values):
    count = lax.axis_size("row")
    parts = [values] + [lax.ppermute(values, "row", plain_ring(count, s)) for s in range(1, count)]
    return jnp.concatenate(parts, axis=0)


def plain_scatter_row(partial_sums):
    count = lax.axis_size("row")
    parts = jnp.split(partial_sums.astype(bfloat), count, axis=0)
    total = jnp.split(partial_sums, count, axis=0)[0]
    for s in range(1, count):
        total = total + lax.ppermute(parts[s], "row", plain_ring(count, -s)).astype(jnp.float32)
    return total


def plain_halve(blocks, bit, slot):
    count = lax.axis_size("page")
    mine = (lax.axis_index("page") // bit) % 2
    kept = lax.dynamic_index_in_dim(blocks, mine, slot, keepdims=False)
    sent = lax.dynamic_index_in_dim(blocks, 1 - mine, slot, keepdims=False)
    return kept + lax.ppermute(sent, "page", plain_flipped(count, bit))


def plain_reduce_matrix(grad):
    pages = lax.axis_size("page")
    rows = lax.axis_size("row")
    bits = []
    while 2 ** len(bits) < pages:
        bits.append(2 ** len(bits))
    height, width = grad.shape
    blocks = grad.astype(bfloat).reshape((2,) * len(bits) + (height // pages, width))
    if bits:
        blocks = plain_halve(blocks, 1, len(bits) - 1)
    left, right = jnp.split(blocks, 2, axis=-1)
    rest = bits[1:]
    for bit in rest:
        left = plain_halve(left, bit, left.ndim - 3)
    for bit in reversed(rest):
        right = plain_halve(right, bit, 0)
    share = jnp.concatenate([left, right], axis=-1)
    me = lax.axis_index("row")
    pieces = share.reshape(share.shape[0], rows, width // rows)
    total = lax.dynamic_index_in_dim(pieces, me, 1, keepdims=False).astype(jnp.float32)
    for s in range(1, rows):
        sent = lax.dynamic_index_in_dim(pieces, (me + s) % rows, 1, keepdims=False)
        total = total + lax.ppermute(sent, "row", plain_ring(rows, s)).astype(jnp.float32)
    return total


def plain_reduce_vectors(stack):
    pages = lax.axis_size("page")
    rows = lax.axis_size("row")
    bit = 1
    while bit < pages:
        stack = stack.reshape(-1, 2, stack.shape[-1])
        stack = plain_halve(stack, bit, 1)
        bit *= 2
    vector = stack.reshape(-1)
    total = vector
    for s in range(1, rows):
        total = total + lax.ppermute(vector, "row", plain_ring(rows, s))
    return total


def plain_split_heads(values):
    return values.reshape(values.shape[0], values.shape[1], -1, HDIM)


def plain_masked_scores(queries, key_rows, allowed):
    scores = jnp.einsum(
        "gqhd,gkhd->ghqk",
        plain_split_heads(queries),
        plain_split_heads(key_rows),
        preferred_element_type=jnp.float32,
    ) * HDIM ** (-0.5)
    return jnp.where(allowed[:, None], scores, masked_score)


def plain_attend_forward(queries, key_rows, value_rows, allowed):
    scores = plain_masked_scores(queries, key_rows, allowed)
    row_max = jnp.max(scores, axis=-1, keepdims=True)
    raised = jnp.exp(scores - row_max)
    row_total = jnp.sum(raised, axis=-1, keepdims=True)
    probs_low = (raised / row_total).astype(bfloat)
    context = jnp.einsum(
        "ghqk,gkhd->gqhd", probs_low, plain_split_heads(value_rows), preferred_element_type=jnp.float32
    )
    return (context.reshape(queries.shape).astype(bfloat), row_max + jnp.log(row_total))


def plain_attend_backward(queries, key_rows, value_rows, allowed, log_total, grad_context):
    probs = jnp.exp(plain_masked_scores(queries, key_rows, allowed) - log_total)
    probs_low = probs.astype(bfloat)
    grad_heads = plain_split_heads(grad_context)
    grad_values = jnp.einsum(
        "ghqk,gqhd->gkhd", probs_low, grad_heads, preferred_element_type=jnp.float32
    )
    grad_probs = jnp.einsum(
        "gqhd,gkhd->ghqk", grad_heads, plain_split_heads(value_rows), preferred_element_type=jnp.float32
    )
    row_delta = jnp.sum(probs * grad_probs, axis=-1, keepdims=True)
    grad_scores = (probs * (grad_probs - row_delta)).astype(bfloat)
    grad_queries = jnp.einsum(
        "ghqk,gkhd->gqhd", grad_scores, plain_split_heads(key_rows), preferred_element_type=jnp.float32
    ) * HDIM ** (-0.5)
    grad_keys = jnp.einsum(
        "ghqk,gqhd->gkhd", grad_scores, plain_split_heads(queries), preferred_element_type=jnp.float32
    ) * HDIM ** (-0.5)
    return (
        grad_queries.reshape(queries.shape).astype(bfloat),
        grad_keys.reshape(key_rows.shape).astype(bfloat),
        grad_values.reshape(value_rows.shape).astype(bfloat),
    )


def plain_project(from_rows, to_rows, weight):
    width = weight.shape[0]
    queries = plain_mat_dot(from_rows, weight[:, :width]).astype(bfloat)
    paired = plain_mat_dot(to_rows, weight[:, width:]).astype(bfloat)
    return (queries, paired[:, :width], paired[:, width:])


def plain_project_back(from_rows, to_rows, weight, dq, dk, dv):
    width = weight.shape[0]
    pair = jnp.concatenate([dk, dv], axis=1)
    weight_grad = jnp.concatenate([plain_mat_left(from_rows, dq), plain_mat_left(to_rows, pair)], axis=1)
    return (weight_grad, plain_mat_right(dq, weight[:, :width]), plain_mat_right(pair, weight[:, width:]))


def plain_output_back(context_low, weight, grad_residual):
    grad_low = grad_residual.astype(bfloat)
    return (
        plain_mat_left(context_low, grad_low),
        jnp.sum(grad_low, axis=0, dtype=jnp.float32),
        plain_mat_right(grad_low, weight).astype(bfloat),
    )


def plain_feed_forward(values, gain_row, bias_row, up_weight, up_bias, down_weight, down_bias):
    hidden, normal, inverse = plain_norm_forward(values, gain_row, bias_row)
    upward = plain_mat_dot(hidden, up_weight) + up_bias
    active = jax.nn.gelu(upward, approximate=True).astype(bfloat)
    return (
        values + (plain_mat_dot(active, down_weight) + down_bias),
        (hidden, normal, inverse, upward, active),
    )


def plain_feed_backward(grad_residual, kept_values, gain_row, up_weight, down_weight):
    hidden, normal, inverse, upward, active = kept_values
    grad_low = grad_residual.astype(bfloat)
    grad_down = plain_mat_left(active, grad_low)
    grad_down_bias = jnp.sum(grad_low, axis=0, dtype=jnp.float32)
    grad_active = plain_mat_right(grad_low, down_weight)
    gelu_pull = jax.vjp(partial(jax.nn.gelu, approximate=True), upward)[1]
    grad_up_low = gelu_pull(grad_active)[0].astype(bfloat)
    grad_up = plain_mat_left(hidden, grad_up_low)
    grad_up_bias = jnp.sum(grad_up_low, axis=0, dtype=jnp.float32)
    grad_input, gain_grad, bias_grad = plain_norm_backward(
        plain_mat_right(grad_up_low, up_weight), normal, inverse, gain_row
    )
    return (
        grad_residual + grad_input,
        (grad_up, grad_up_bias, grad_down, grad_down_bias, gain_grad, bias_grad),
    )


def plain_shards(
    vis_stream,
    query_stream,
    w_qkv,
    w_out,
    b_out,
    w_up,
    b_up,
    w_down,
    b_down,
    norm_gain,
    norm_bias,
    page_cols,
    query_len,
    prompt_len,
    region_ids,
    vis_cotangent,
    query_cotangent,
):
    band_rows, page_width, width = vis_stream.shape[1:]
    tokens = band_rows * page_width
    query_rows = query_stream.shape[1]
    bands = lax.axis_size("row")
    me = lax.axis_index("row")
    pages = lax.axis_size("page")
    x0 = plain_to_shifted(vis_stream[0]).astype(jnp.float32)
    gx3 = plain_to_shifted(vis_cotangent[0]).astype(jnp.float32)
    y0 = query_stream[0].astype(jnp.float32)
    gy3 = query_cotangent[0].astype(jnp.float32)
    col_limit, query_limit, prompt_limit = page_cols[0], query_len[0], prompt_len[0]

    own_positions = me * query_rows + jnp.arange(query_rows)
    all_positions = jnp.concatenate(
        [((me - s) % bands) * query_rows + jnp.arange(query_rows) for s in range(bands)]
    )
    key_live = all_positions < query_limit
    self_allowed = key_live[None, :] & (
        (all_positions[None, :] <= own_positions[:, None]) | (all_positions[None, :] < prompt_limit)
    )
    rolled_live = (jnp.arange(page_width) + SHIFT) % page_width < col_limit
    live_tiles = plain_to_windows(jnp.broadcast_to(rolled_live[None, :], (band_rows, page_width)))
    visual_allowed = jnp.broadcast_to(
        jnp.tile(live_tiles.reshape(-1), bands)[None, :], (query_rows, bands * tokens)
    )
    query_allowed = jnp.broadcast_to(key_live[None, :], (tokens, query_rows * bands))
    region_tiles = plain_to_windows(region_ids[0])
    diagonal = jnp.eye(WIN * WIN, dtype=jnp.bool_)
    window_allowed = (region_tiles[:, :, None] == region_tiles[:, None, :]) & (
        live_tiles[:, None, :] | diagonal[None]
    )
    tile_shape = (tokens // (WIN * WIN), WIN * WIN, width)

    hs, n1, i1 = plain_norm_forward(y0, norm_gain[1], norm_bias[1])
    hs_all = plain_gather_row(hs)
    hv, n0, i0 = plain_norm_forward(x0, norm_gain[0], norm_bias[0])
    qw, kw, vw = (v.reshape(tile_shape) for v in plain_project(hv, hv, w_qkv[0]))
    cw, lw = plain_attend_forward(qw, kw, vw, window_allowed)
    cw = cw.reshape(tokens, width)
    x1 = x0 + (plain_mat_dot(cw, w_out[0]) + b_out[0])
    hl, n3, i3 = plain_norm_forward(x1, norm_gain[3], norm_bias[3])
    hl_all = plain_gather_row(hl)

    qs, ks, vs = plain_project(hs, hs_all, w_qkv[1])
    cs, ls = plain_attend_forward(qs[None], ks[None], vs[None], self_allowed[None])
    cs = cs[0]
    y1 = y0 + (plain_mat_dot(cs, w_out[1]) + b_out[1])
    ha, n2, i2 = plain_norm_forward(y1, norm_gain[2], norm_bias[2])
    qa, kl, vl = plain_project(ha, hl_all, w_qkv[2])
    ca, la = plain_attend_forward(qa[None], kl[None], vl[None], visual_allowed[None])
    ca = ca[0]
    y2 = y1 + (plain_mat_dot(ca, w_out[2]) + b_out[2])
    hm, n4, i4 = plain_norm_forward(y2, norm_gain[4], norm_bias[4])
    hm_all = plain_gather_row(hm)
    y3, kept_query = plain_feed_forward(
        y2, norm_gain[6], norm_bias[6], w_up[1], b_up[1], w_down[1], b_down[1]
    )
    gy2, feed_query = plain_feed_backward(gy3, kept_query, norm_gain[6], w_up[1], w_down[1])
    final_up1 = plain_reduce_matrix(feed_query[0])
    final_down1 = plain_reduce_matrix(feed_query[2])

    qr, km, vm = plain_project(hl, hm_all, w_qkv[3])
    cr, lr = plain_attend_forward(qr[None], km[None], vm[None], query_allowed[None])
    cr = cr[0]
    x2 = x1 + (plain_mat_dot(cr, w_out[3]) + b_out[3])
    x3, kept_vis = plain_feed_forward(
        x2, norm_gain[5], norm_bias[5], w_up[0], b_up[0], w_down[0], b_down[0]
    )
    gx2, feed_vis = plain_feed_backward(gx3, kept_vis, norm_gain[5], w_up[0], w_down[0])
    final_up0 = plain_reduce_matrix(feed_vis[0])
    final_down0 = plain_reduce_matrix(feed_vis[2])

    wout3, bout3, dcr = plain_output_back(cr, w_out[3], gx2)
    dqr, dkm, dvm = plain_attend_backward(
        qr[None], km[None], vm[None], query_allowed[None], lr, dcr[None]
    )
    qkv3, dhl, dhm = plain_project_back(hl, hm_all, w_qkv[3], dqr[0], dkm[0], dvm[0])
    gy_memo, gain4, bias4 = plain_norm_backward(plain_scatter_row(dhm), n4, i4, norm_gain[4])
    gy2 = gy2 + gy_memo
    final_out3 = plain_reduce_matrix(wout3)
    final_qkv3 = plain_reduce_matrix(qkv3)

    wout2, bout2, dca = plain_output_back(ca, w_out[2], gy2)
    dqa, dkl, dvl = plain_attend_backward(
        qa[None], kl[None], vl[None], visual_allowed[None], la, dca[None]
    )
    qkv2, dha, dhl_all = plain_project_back(ha, hl_all, w_qkv[2], dqa[0], dkl[0], dvl[0])
    gy_ask, gain2, bias2 = plain_norm_backward(dha, n2, i2, norm_gain[2])
    gy1 = gy2 + gy_ask
    gx_look, gain3, bias3 = plain_norm_backward(dhl + plain_scatter_row(dhl_all), n3, i3, norm_gain[3])
    gx1 = gx2 + gx_look
    final_out2 = plain_reduce_matrix(wout2)
    final_qkv2 = plain_reduce_matrix(qkv2)

    wout1, bout1, dcs = plain_output_back(cs, w_out[1], gy1)
    dqs, dks, dvs = plain_attend_backward(qs[None], ks[None], vs[None], self_allowed[None], ls, dcs[None])
    qkv1, dhs, dhs_all = plain_project_back(hs, hs_all, w_qkv[1], dqs[0], dks[0], dvs[0])
    gy_self, gain1, bias1 = plain_norm_backward(dhs + plain_scatter_row(dhs_all), n1, i1, norm_gain[1])
    gy0 = gy1 + gy_self
    final_out1 = plain_reduce_matrix(wout1)
    final_qkv1 = plain_reduce_matrix(qkv1)

    wout0, bout0, dcw = plain_output_back(cw, w_out[0], gx1)
    dqw, dkw, dvw = plain_attend_backward(qw, kw, vw, window_allowed, lw, dcw.reshape(tile_shape))
    dqw, dkw, dvw = (v.reshape(tokens, width) for v in (dqw, dkw, dvw))
    qkv0, dr_from, dr_into = plain_project_back(hv, hv, w_qkv[0], dqw, dkw, dvw)
    gx_win, gain0, bias0 = plain_norm_backward(dr_from + dr_into, n0, i0, norm_gain[0])
    gx0 = gx1 + gx_win
    final_out0 = plain_reduce_matrix(wout0)
    final_qkv0 = plain_reduce_matrix(qkv0)

    vectors = [
        jnp.stack([bout0, bout1, bout2, bout3]),
        jnp.stack([feed_vis[1], feed_query[1]]),
        jnp.stack([feed_vis[3], feed_query[3]]),
        jnp.stack([gain0, gain1, gain2, gain3, gain4, feed_vis[4], feed_query[4]]),
        jnp.stack([bias0, bias1, bias2, bias3, bias4, feed_vis[5], feed_query[5]]),
    ]
    blocks = [
        jnp.swapaxes(v.reshape(v.shape[0], pages, -1), 0, 1).reshape(pages, -1) for v in vectors
    ]
    reduced = plain_reduce_vectors(jnp.concatenate(blocks, axis=1))
    finals, start = [], 0
    for v in vectors:
        size = v.size // pages
        finals.append(reduced[start : start + size].reshape(v.shape[0], -1))
        start += size

    return (
        plain_from_shifted(x3.astype(bfloat), band_rows, page_width)[None],
        y3[None].astype(bfloat),
        plain_from_shifted(gx0, band_rows, page_width)[None],
        gy0[None],
        jnp.stack([final_qkv0, final_qkv1, final_qkv2, final_qkv3]),
        jnp.stack([final_out0, final_out1, final_out2, final_out3]),
        finals[0],
        jnp.stack([final_up0, final_up1]),
        finals[1],
        jnp.stack([final_down0, final_down1]),
        finals[2],
        finals[3],
        finals[4],
    )


def solution(mesh):
    planned = mesh.shape["page"] == 8 and mesh.shape["row"] == 4
    return jax.shard_map(
        shards if planned else plain_shards,
        mesh=mesh,
        in_specs=(
            P("page", "row", None, None),
            P("page", "row", None),
            P(),
            P(),
            P(),
            P(),
            P(),
            P(),
            P(),
            P(),
            P(),
            P("page"),
            P("page"),
            P("page"),
            P("page", "row", None),
            P("page", "row", None, None),
            P("page", "row", None),
        ),
        out_specs=(
            P("page", "row", None, None),
            P("page", "row", None),
            P("page", "row", None, None),
            P("page", "row", None),
            P(None, "page", "row"),
            P(None, "page", "row"),
            P(None, "page"),
            P(None, "page", "row"),
            P(None, "page"),
            P(None, "page", "row"),
            P(None, "page"),
            P(None, "page"),
            P(None, "page"),
        ),
        check_vma=False,
    )
```
